128 devices in a mesh: member: 8 (over z, y_lo), row: 16 (over y_hi, x, core).
Axes of the slice: x: 4, y: 4 (y_hi: 2, y_lo: 2; y = y_hi * 2 + y_lo), z: 4, core: 2. Of those that a mesh axis runs over, the one named last changes fastest.
Arguments:
- action: bfloat16 [4096, 1024], P('row'), may hold values from -6 to 6
- state_term: bfloat16 [16, 4096, 4096], P('member', 'row'), may hold values from -6 to 6
- target: float32 [4096], P('row'), may hold values from -6 to 6
- weight_a: bfloat16 [16, 1024, 4096], P('member', 'row'), may hold values from -0.21875 to 0.21875
- value_w: bfloat16 [16, 4096], P('member'), may hold values from -0.0234375 to 0.0234375
Outputs:
- weight_grad: bfloat16 [16, 1024, 4096], P('member', 'row')
- value_grad: float32 [16, 4096], P('member')
- state_grad: bfloat16 [16, 4096, 4096], P('member', 'row')
- diversity: float32 [4096], P('row')
The draws below stay inside these ranges and needn't reach their ends.
All inputs are finite; a program needn't handle non-finite values.
Results may differ from the reference program's by a relative error of at most 0.03.
Values may be sent and summed in bfloat16 or wider, within the bound.
A program may use at most 128 MiB of HBM per device.

```python
import jax
import jax.numpy as jnp
from jax import lax

A = 1024
H = 4096
ROW_DEV = 256
MEMBERS = 16
ROWS = 4096
N_ROW = 16


def draw_weight_a(key, part):
    key = jax.random.fold_in(key, 11)
    common = jnp.clip(jax.random.normal(jax.random.fold_in(key, 1), (A, H), jnp.float32), -5.0, 5.0)
    own = jnp.clip(jax.random.normal(jax.random.fold_in(key, 2), (MEMBERS, A, H), jnp.float32), -5.0, 5.0)
    mixed = 0.8 * common[None] + 0.6 * own
    return (mixed / jnp.sqrt(jnp.float32(A))).astype(jnp.bfloat16)


def steps_of(stream_key, shape, cuts, low, high):
    level, own = 1.0, jax.random.fold_in(stream_key, 6)
    for dim, shards_of in cuts:
        heights = jnp.exp(jax.random.uniform(jax.random.fold_in(own, dim), (shards_of,), jnp.float32, low / len(cuts), high / len(cuts)))
        level = level * jnp.repeat(heights, shape[dim] // shards_of).reshape([-1 if axis == dim else 1 for axis in range(len(shape))])
    return level


def centred(stream_key, dims, scale, limit, split=(), held_as=jnp.bfloat16):
    factor_of = steps_of(stream_key, dims, split, -0.22, 0.18) if split else 1.0
    drawn = jax.random.normal(stream_key, dims, jnp.float32) * scale * factor_of
    return jnp.minimum(jnp.maximum(drawn, -limit), limit).astype(held_as)


def setup_inputs(seed: int = 0) -> dict:
    key_of = jax.random.split(jax.random.key(seed), 6)
    action = centred(key_of[0], (ROWS, A), 1.0, 6.0, ((0, 16),))
    state_term = centred(key_of[1], (MEMBERS, ROWS, H), 1.0, 6.0, ((0, 8), (1, 16)))
    target = centred(key_of[2], (ROWS,), 1.0, 6.0, ((0, 16),), jnp.float32)
    weight_a = draw_weight_a(jax.random.fold_in(key_of[5], 71), 0)
    value_w = centred(key_of[4], (MEMBERS, H), (16 * H) ** -0.5, 0.0234375, ((0, 8),))
    return dict(action=action, state_term=state_term, target=target, weight_a=weight_a, value_w=value_w)


EPS = 1e-06
ETA = 5.0

def forward_member(weights, value_row, state_rows, action):
    pre_act = state_rows.astype(jnp.float32) + jnp.dot(action, weights, preferred_element_type=jnp.float32)
    sigmoid_part = jax.nn.sigmoid(pre_act)
    hidden = pre_act * sigmoid_part
    slope_first = sigmoid_part * (1.0 + pre_act * (1.0 - sigmoid_part))
    slope_second = sigmoid_part * (1.0 - sigmoid_part) * (2.0 + pre_act * (1.0 - 2.0 * sigmoid_part))
    value_float = value_row.astype(jnp.float32)
    q_value = lax.optimization_barrier(jnp.sum(hidden * value_float, axis=-1))
    tangent = (slope_first * value_float).astype(jnp.bfloat16)
    action_grad = lax.dot_general(tangent, weights, (((1,), (1,)), ((), ())), preferred_element_type=jnp.float32)
    grad_norm = jnp.sqrt(lax.optimization_barrier(jnp.sum(action_grad * action_grad, axis=-1, keepdims=True)) + EPS)
    unit_grad = action_grad / grad_norm
    return (hidden, slope_first, slope_second, q_value, tangent, unit_grad, grad_norm)

def reference(action, state_term, target, weight_a, value_w):

    def front(operands):
        weights, value_row, state_rows = operands
        outs_front = forward_member(weights, value_row, state_rows, action)
        return outs_front[5].astype(jnp.bfloat16)
    units = lax.map(front, (weight_a, value_w, state_term))
    unit_float = units.astype(jnp.float32)
    total = lax.optimization_barrier(jnp.sum(unit_float, axis=0))
    cross_sum = lax.optimization_barrier(jnp.sum(lax.optimization_barrier(jnp.sum(unit_float * total[None], axis=2)), axis=0))
    square_sum = lax.optimization_barrier(jnp.sum(lax.optimization_barrier(jnp.sum(unit_float * unit_float, axis=2)), axis=0))
    pairs = MEMBERS * (MEMBERS - 1)
    diversity = (cross_sum - square_sum) / pairs

    def back(operands):
        weights, value_row, state_rows, unit_b = operands
        hidden, slope_first, slope_second, q_value, tangent, unit_grad, grad_norm = forward_member(weights, value_row, state_rows, action)
        dir_grad = 2.0 * ETA / pairs * (total - unit_b.astype(jnp.float32))
        along = lax.optimization_barrier(jnp.sum(unit_grad * dir_grad, axis=-1, keepdims=True))
        cotangent = ((dir_grad - unit_grad * along) / grad_norm).astype(jnp.bfloat16)
        back_term = jnp.dot(cotangent, weights, preferred_element_type=jnp.float32)
        residue = (q_value - target)[:, None]
        value_float = value_row.astype(jnp.float32)
        pre_grad = value_float * (slope_first * residue + slope_second * back_term)
        value_grad = lax.optimization_barrier(jnp.sum(hidden * residue + slope_first * back_term, axis=0))
        pre_b = pre_grad.astype(jnp.bfloat16)
        left = jnp.concatenate([action.reshape(N_ROW, ROW_DEV, A), cotangent.reshape(N_ROW, ROW_DEV, A)], axis=1)
        right = jnp.concatenate([pre_b.reshape(N_ROW, ROW_DEV, H), tangent.reshape(N_ROW, ROW_DEV, H)], axis=1)

        def block_sum(accum, pieces):
            left_blk, right_blk = pieces
            partial_sum = lax.dot_general(left_blk, right_blk, (((0,), (0,)), ((), ())), preferred_element_type=jnp.float32)
            rounded = lax.optimization_barrier(partial_sum.astype(jnp.bfloat16))
            return (accum + rounded.astype(jnp.float32), None)
        grad_sum, unused = lax.scan(block_sum, jnp.zeros((A, H), jnp.float32), (left, right))
        return (grad_sum.astype(jnp.bfloat16), value_grad, pre_b)
    weight_grad, value_grad, state_grad = lax.map(back, (weight_a, value_w, state_term, units))
    return (weight_grad, value_grad, state_grad, diversity)
```

```python
import jax
import jax.numpy as jnp
from jax import lax
from jax.experimental import pallas as pl
from jax.experimental.pallas import tpu as pltpu
from jax.sharding import PartitionSpec as P

EPS = 1e-06
ETA = 5.0
MESH = pl.DeviceIdType.MESH
F32 = jnp.float32
BF16 = jnp.bfloat16

ACT = 1024
HID = 4096
ROWS = 256
LOCAL = 2
MEMBER_DEV = 8
PAIRS = 16 * 15
WIDTH = 256
PER_MEMBER = HID // WIDTH
BLOCKS = LOCAL * PER_MEMBER
PIECE = ROWS // MEMBER_DEV

SEND_AHEAD = 6
FORWARD_AHEAD = 4
SIBLING_AHEAD = 2
CORE_BEHIND = 1
SECOND_BEHIND = 3
LAST_BEHIND = 5


def x_first_in_scatter(block):
    return lax.rem(block * 9, 16) < 9


def wait_for(ref, sem):
    pltpu.make_async_copy(ref, ref, sem).wait()


def fold(value):
    out = value[:, 0:128]
    for pos in range(128, value.shape[1], 128):
        out = out + value[:, pos : pos + 128]
    return out


def wide(value, width):
    return jnp.concatenate([value] * (width // 128), axis=1)


def kernel(
    action_ref, state_hbm, target_ref, weight_hbm, value_ref,
    wgrad_hbm, vgrad_ref, sgrad_hbm, div_ref,
    wbuf, state, pre, grad, unit_b, cot, lhs, rhs, core_in, ring_in,
    piece_out, piece_in, total, square_out, square_in, value_w, q_acc, resid, rnorm, vsum, vin,
    load_sem, state_sem, x_sem, y_sem, second_sem, sib_sem, link_done, sib_done,
    core_sem, core_done, ring_sem, last_sem, ring_done, sgrad_sem, wgrad_sem,
    misc_sem,
):
    member = lax.axis_index("member")
    row = lax.axis_index("row")
    yhi = row // 8
    xpos = lax.rem(row // 2, 4)
    core = lax.rem(row, 2)
    oyhi = 1 - yhi
    ocore = 1 - core

    def at_row(yy, xx, cc):
        return (member, yy * 8 + xx * 2 + cc)

    sibling = at_row(yhi, xpos, ocore)
    across = at_row(oyhi, xpos, core)
    ring_x = [lax.rem(xpos + d, 4) for d in (1, 2, 3)]
    ring = [at_row(yhi, xx, core) for xx in ring_x]
    peers = [lax.rem(member + d, MEMBER_DEV) for d in range(1, MEMBER_DEV)]

    def send(src, dst, done, arrived, dev):
        pltpu.make_async_remote_copy(
            src_ref=src, dst_ref=dst, send_sem=done, recv_sem=arrived, device_id=dev, device_id_type=MESH
        ).start()

    barrier = pltpu.get_barrier_semaphore()
    everyone = [sibling, across] + ring + [(peer, row) for peer in peers]
    for dev in everyone:
        pl.semaphore_signal(barrier, inc=1, device_id=dev, device_id_type=MESH)

    def columns(block):
        return pl.ds(pl.multiple_of(lax.rem(block, PER_MEMBER) * WIDTH, WIDTH), WIDTH)

    def load_block(block, carry):
        m = block // PER_MEMBER
        pltpu.make_async_copy(
            weight_hbm.at[m, :, columns(block)], wbuf.at[block, yhi, xpos, core], load_sem.at[block]
        ).start()
        return carry

    lax.fori_loop(0, BLOCKS, load_block, 0)

    def load_state(block, carry):
        m = block // PER_MEMBER
        pltpu.make_async_copy(
            state_hbm.at[m, :, columns(block)], state.at[block], state_sem.at[block]
        ).start()
        return carry

    lax.fori_loop(0, BLOCKS, load_state, 0)

    for m in range(LOCAL):
        row_w = value_ref[m : m + 1, :].astype(F32)
        for pos in range(PER_MEMBER):
            value_w[m * PER_MEMBER + pos] = row_w[:, pos * WIDTH : (pos + 1) * WIDTH]
    grad[...] = jnp.zeros_like(grad)
    q_acc[...] = jnp.zeros_like(q_acc)
    for half in range(2):
        part = action_ref[half * 128 : (half + 1) * 128, :].astype(F32)
        lhs[:, half * 128 : (half + 1) * 128] = jnp.transpose(part).astype(BF16)

    pl.semaphore_wait(barrier, len(everyone))

    def first_send(b):
        wait_for(wbuf.at[b, yhi, xpos, core], load_sem.at[b])
        own = wbuf.at[b, yhi, xpos, core]
        for dev in ring:
            send(own, own, link_done.at[b], x_sem.at[b], dev)

        @pl.when(x_first_in_scatter(b))
        def _():
            send(own, own, link_done.at[b], y_sem.at[b], across)

    def forward(b):
        wait_for(wbuf.at[b, yhi, pl.ds(0, 3), core], x_sem.at[b])
        mine = wbuf.at[b, yhi, :, core]
        cross = x_first_in_scatter(b)

        @pl.when(jnp.logical_not(cross))
        def _():
            send(mine, mine, link_done.at[b], y_sem.at[b], across)

        send(mine, mine, sib_done.at[b], sib_sem.at[b], sibling)

        @pl.when(cross)
        def _():
            other = wbuf.at[b, oyhi, xpos, core]
            wait_for(other, y_sem.at[b])
            for dev in ring:
                send(other, other, link_done.at[b], second_sem.at[b], dev)

    def to_sibling(b):
        cross = x_first_in_scatter(b)

        @pl.when(cross)
        def _():
            wait_for(wbuf.at[b, oyhi, pl.ds(0, 3), core], second_sem.at[b])

        @pl.when(jnp.logical_not(cross))
        def _():
            wait_for(wbuf.at[b, oyhi, :, core], y_sem.at[b])

        theirs = wbuf.at[b, oyhi, :, core]
        send(theirs, theirs, sib_done.at[b], sib_sem.at[b], sibling)

    def compute_forward(b):
        m = b // PER_MEMBER
        wait_for(state.at[b], state_sem.at[b])
        wait_for(wbuf.at[b, :, :, ocore], sib_sem.at[b])
        weights = wbuf[b].reshape(ACT, WIDTH)
        pre[b] = state[b].astype(F32) + jnp.dot(action_ref[...], weights, preferred_element_type=F32)
        vw = value_w[b]
        step = 64
        for pos in range(0, ROWS, step):
            p = pre[b, pos : pos + step, :]
            sig = 0.5 + 0.5 * jnp.tanh(0.5 * p)
            hidden = p * sig
            slope = sig + hidden * (1.0 - sig)
            rhs[pos : pos + step, :] = (slope * vw).astype(BF16)
            q_acc[m, pos : pos + step, :] += fold(hidden * vw)
        grad[m] += lax.dot_general(
            rhs[0:ROWS, :], weights, (((1,), (1,)), ((), ())), preferred_element_type=F32
        )

    def forward_step(i, carry):
        t = i - SEND_AHEAD

        @pl.when(t + SEND_AHEAD < BLOCKS)
        def _():
            first_send(t + SEND_AHEAD)

        @pl.when(jnp.logical_and(t + FORWARD_AHEAD >= 0, t + FORWARD_AHEAD < BLOCKS))
        def _():
            forward(t + FORWARD_AHEAD)

        @pl.when(jnp.logical_and(t + SIBLING_AHEAD >= 0, t + SIBLING_AHEAD < BLOCKS))
        def _():
            to_sibling(t + SIBLING_AHEAD)

        @pl.when(t >= 0)
        def _():
            compute_forward(t)

        return carry

    lax.fori_loop(0, BLOCKS + SEND_AHEAD, forward_step, 0)

    def make_piece(k):
        rows = pl.ds(pl.multiple_of(k * PIECE, PIECE), PIECE)
        both = []
        squares = None
        for m in range(LOCAL):
            g = grad[m, rows, :]
            inv = 1.0 / jnp.sqrt(jnp.sum(g * g, axis=-1, keepdims=True) + EPS)
            u = g * inv
            ub = u.astype(BF16)
            grad[m, rows, :] = u
            unit_b[m, rows, :] = ub
            rnorm[m, rows, :] = jnp.broadcast_to(inv, (PIECE, 128))
            uf = ub.astype(F32)
            both.append(uf)
            sq = fold(uf * uf)
            squares = sq if squares is None else squares + sq
        square_out[rows, :] = squares
        return (both[0] + both[1]).astype(BF16)

    for peer in peers:
        piece_out[peer] = make_piece(peer)
        send(piece_out.at[peer], piece_in.at[member], misc_sem.at[0], misc_sem.at[1], (peer, row))
    piece_in[member] = make_piece(member)

    target_rows = jnp.transpose(jnp.broadcast_to(target_ref[...], (128, ROWS)))
    for m in range(LOCAL):
        q = jnp.sum(q_acc[m], axis=-1, keepdims=True)
        resid[m] = q - target_rows

    wait_for(piece_in.at[pl.ds(0, MEMBER_DEV - 1)], misc_sem.at[1])
    acc = piece_in[0].astype(F32)
    for k in range(1, MEMBER_DEV):
        acc = acc + piece_in[k].astype(F32)
    my_rows = pl.ds(pl.multiple_of(member * PIECE, PIECE), PIECE)
    total[my_rows, :] = acc.astype(BF16)
    for peer in peers:
        send(total.at[my_rows], total.at[my_rows], misc_sem.at[2], misc_sem.at[3], (peer, row))
    square_lane = jnp.sum(jnp.transpose(square_out[...]), axis=0, keepdims=True)
    square_in[member] = jnp.broadcast_to(square_lane, (8, ROWS))
    for peer in peers:
        send(square_in.at[member], square_in.at[member], misc_sem.at[4], misc_sem.at[5], (peer, row))
    wait_for(total.at[pl.ds(0, PIECE * (MEMBER_DEV - 1))], misc_sem.at[3])

    def make_cot(m):
        step = 64
        for pos in range(0, ROWS, step):
            u = grad[m, pos : pos + step, :]
            d = (2.0 * ETA / PAIRS) * (
                total[pos : pos + step, :].astype(F32) - unit_b[m, pos : pos + step, :].astype(F32)
            )
            along = jnp.sum(u * d, axis=-1, keepdims=True)
            c = (d - u * along) * wide(rnorm[m, pos : pos + step, :], ACT)
            cot[m, pos : pos + step, :] = c.astype(BF16)

    def place_cot(m):
        for half in range(2):
            part = cot[m, half * 128 : (half + 1) * 128, :].astype(F32)
            lhs[:, ROWS + half * 128 : ROWS + (half + 1) * 128] = jnp.transpose(part).astype(BF16)

    make_cot(0)
    place_cot(0)

    def compute_backward(b):
        m = b // PER_MEMBER
        weights = wbuf[b].reshape(ACT, WIDTH)
        back_all = jnp.dot(cot[m], weights, preferred_element_type=F32)
        vw = value_w[b]
        step = 64
        vacc = jnp.zeros((1, WIDTH), F32)
        for pos in range(0, ROWS, step):
            p = pre[b, pos : pos + step, :]
            back = back_all[pos : pos + step, :]
            res = wide(resid[m, pos : pos + step, :], WIDTH)
            sig = 0.5 + 0.5 * jnp.tanh(0.5 * p)
            rest = 1.0 - sig
            hidden = p * sig
            slope = sig + hidden * rest
            curve = sig * rest * (2.0 + p * (rest - sig))
            dpre = (vw * (slope * res + curve * back)).astype(BF16)
            vacc = vacc + jnp.sum(hidden * res + slope * back, axis=0, keepdims=True)
            rhs[pos : pos + step, :] = dpre
            state[b, pos : pos + step, :] = dpre
            rhs[ROWS + pos : ROWS + pos + step, :] = (slope * vw).astype(BF16)
        vsum[b] = vacc
        pltpu.make_async_copy(state.at[b], sgrad_hbm.at[m, :, columns(b)], sgrad_sem.at[b]).start()
        wait_for(wbuf.at[b, :, :, core], sib_done.at[b])
        wait_for(ring_in.at[b], link_done.at[b])
        part = jnp.dot(lhs[...], rhs[...], preferred_element_type=F32)
        wbuf[b] = part.astype(BF16).reshape(2, 4, 2, 64, WIDTH)
        send(wbuf.at[b, :, :, ocore], core_in.at[b], core_done.at[b], core_sem.at[b], sibling)

    def second_send(b):
        wait_for(core_in.at[b], core_sem.at[b])
        for yy in range(2):
            for xx in range(4):
                wbuf[b, yy, xx, core] = (
                    wbuf[b, yy, xx, core].astype(F32) + core_in[b, yy, xx].astype(F32)
                ).astype(BF16)
        x_first = x_first_in_scatter(b)

        @pl.when(x_first)
        def _():
            for d in range(3):
                send(
                    wbuf.at[b, :, ring_x[d], core], ring_in.at[b, pl.ds(2 * d, 2)],
                    ring_done.at[b], ring_sem.at[b], ring[d],
                )

        @pl.when(jnp.logical_not(x_first))
        def _():
            send(
                wbuf.at[b, oyhi, :, core], ring_in.at[b, pl.ds(0, 4)],
                ring_done.at[b], ring_sem.at[b], across,
            )

    def last_send(b):
        x_first = x_first_in_scatter(b)

        @pl.when(x_first)
        def _():
            wait_for(ring_in.at[b, pl.ds(0, 6)], ring_sem.at[b])
            for yy in range(2):
                s = wbuf[b, yy, xpos, core].astype(F32)
                for d in range(3):
                    s = s + ring_in[b, 2 * d + yy].astype(F32)
                wbuf[b, yy, xpos, core] = s.astype(BF16)
            send(
                wbuf.at[b, oyhi, xpos, core], ring_in.at[b, 6],
                ring_done.at[b], last_sem.at[b], across,
            )

        @pl.when(jnp.logical_not(x_first))
        def _():
            wait_for(ring_in.at[b, pl.ds(0, 4)], ring_sem.at[b])
            for xx in range(4):
                wbuf[b, yhi, xx, core] = (
                    wbuf[b, yhi, xx, core].astype(F32) + ring_in[b, xx].astype(F32)
                ).astype(BF16)
            for d in range(3):
                send(
                    wbuf.at[b, yhi, ring_x[d], core], ring_in.at[b, 4 + d],
                    ring_done.at[b], last_sem.at[b], ring[d],
                )

    def finish(b):
        m = b // PER_MEMBER
        x_first = x_first_in_scatter(b)

        @pl.when(x_first)
        def _():
            wait_for(ring_in.at[b, 6], last_sem.at[b])
            wbuf[b, yhi, xpos, core] = (
                wbuf[b, yhi, xpos, core].astype(F32) + ring_in[b, 6].astype(F32)
            ).astype(BF16)

        @pl.when(jnp.logical_not(x_first))
        def _():
            wait_for(ring_in.at[b, pl.ds(4, 3)], last_sem.at[b])
            s = wbuf[b, yhi, xpos, core].astype(F32)
            for d in range(3):
                s = s + ring_in[b, 4 + d].astype(F32)
            wbuf[b, yhi, xpos, core] = s.astype(BF16)

        pltpu.make_async_copy(
            wbuf.at[b, yhi, xpos, core], wgrad_hbm.at[m, :, columns(b)], wgrad_sem.at[b]
        ).start()

    def backward_step(t, carry):
        @pl.when(t == PER_MEMBER - 2)
        def _():
            make_cot(1)

        @pl.when(t == PER_MEMBER)
        def _():
            place_cot(1)

        @pl.when(t < BLOCKS)
        def _():
            compute_backward(t)

        @pl.when(t == BLOCKS)
        def _():
            send(vsum, vin.at[0], misc_sem.at[6], misc_sem.at[7], sibling)

        @pl.when(jnp.logical_and(t >= CORE_BEHIND, t - CORE_BEHIND < BLOCKS))
        def _():
            second_send(t - CORE_BEHIND)

        @pl.when(t == BLOCKS + 1)
        def _():
            wait_for(vsum, misc_sem.at[6])
            wait_for(vin.at[0], misc_sem.at[7])
            vsum[...] = vsum[...] + vin[0]
            send(vsum, vin.at[1], misc_sem.at[8], misc_sem.at[9], across)

        @pl.when(jnp.logical_and(t >= SECOND_BEHIND, t - SECOND_BEHIND < BLOCKS))
        def _():
            last_send(t - SECOND_BEHIND)

        @pl.when(t == BLOCKS + 3)
        def _():
            wait_for(vsum, misc_sem.at[8])
            wait_for(vin.at[1], misc_sem.at[9])
            vin[2 + xpos] = vsum[...] + vin[1]
            for dev in ring:
                send(vin.at[2 + xpos], vin.at[2 + xpos], misc_sem.at[10], misc_sem.at[11], dev)

        @pl.when(jnp.logical_and(t >= LAST_BEHIND, t - LAST_BEHIND < BLOCKS))
        def _():
            finish(t - LAST_BEHIND)

        return carry

    lax.fori_loop(0, BLOCKS + LAST_BEHIND, backward_step, 0)

    wait_for(square_in.at[pl.ds(0, MEMBER_DEV - 1)], misc_sem.at[5])
    tsq = []
    for pos in range(0, ROWS, 64):
        tf = total[pos : pos + 64, :].astype(F32)
        tsq.append(fold(tf * tf))
    cross_sum = jnp.sum(jnp.transpose(jnp.concatenate(tsq, axis=0)), axis=0, keepdims=True)
    squares = square_in[0]
    for k in range(1, MEMBER_DEV):
        squares = squares + square_in[k]
    div_ref[...] = (cross_sum - squares[0:1, :]) * (1.0 / PAIRS)

    wait_for(vin.at[pl.ds(2, 3)], misc_sem.at[11])
    for b in range(BLOCKS):
        m, pos = b // PER_MEMBER, b % PER_MEMBER
        vgrad_ref[m : m + 1, pos * WIDTH : (pos + 1) * WIDTH] = (vin[2, b] + vin[3, b]) + (vin[4, b] + vin[5, b])

    wait_for(piece_out.at[pl.ds(0, MEMBER_DEV - 1)], misc_sem.at[0])
    wait_for(total.at[pl.ds(0, PIECE * (MEMBER_DEV - 1))], misc_sem.at[2])
    wait_for(square_in.at[pl.ds(0, MEMBER_DEV - 1)], misc_sem.at[4])
    wait_for(vin.at[pl.ds(2, 3)], misc_sem.at[10])

    def drain(b, carry):
        m = b // PER_MEMBER
        wait_for(core_in.at[b], core_done.at[b])
        wait_for(ring_in.at[b], ring_done.at[b])
        wait_for(state.at[b], sgrad_sem.at[b])
        wait_for(wbuf.at[b, yhi, xpos, core], wgrad_sem.at[b])
        return carry

    lax.fori_loop(0, BLOCKS, drain, 0)


def body(action, state_term, target, weight_a, value_w):
    any_spec = pl.BlockSpec(memory_space=pl.ANY)
    vmem_spec = pl.BlockSpec(memory_space=pltpu.VMEM)
    dma = pltpu.SemaphoreType.DMA
    wgrad, vgrad, sgrad, div = pl.pallas_call(
        kernel,
        out_shape=(
            jax.ShapeDtypeStruct((LOCAL, 64, HID), BF16),
            jax.ShapeDtypeStruct((LOCAL, HID), F32),
            jax.ShapeDtypeStruct((LOCAL, ROWS, HID), BF16),
            jax.ShapeDtypeStruct((1, ROWS), F32),
        ),
        in_specs=[vmem_spec, any_spec, vmem_spec, any_spec, vmem_spec],
        out_specs=(any_spec, vmem_spec, any_spec, vmem_spec),
        scratch_shapes=[
            pltpu.VMEM((BLOCKS, 2, 4, 2, 64, WIDTH), BF16),
            pltpu.VMEM((BLOCKS, ROWS, WIDTH), BF16),
            pltpu.VMEM((BLOCKS, ROWS, WIDTH), F32),
            pltpu.VMEM((LOCAL, ROWS, ACT), F32),
            pltpu.VMEM((LOCAL, ROWS, ACT), BF16),
            pltpu.VMEM((LOCAL, ROWS, ACT), BF16),
            pltpu.VMEM((ACT, 2 * ROWS), BF16),
            pltpu.VMEM((2 * ROWS, WIDTH), BF16),
            pltpu.VMEM((BLOCKS, 2, 4, 64, WIDTH), BF16),
            pltpu.VMEM((BLOCKS, 7, 64, WIDTH), BF16),
            pltpu.VMEM((MEMBER_DEV, PIECE, ACT), BF16),
            pltpu.VMEM((MEMBER_DEV, PIECE, ACT), BF16),
            pltpu.VMEM((ROWS, ACT), BF16),
            pltpu.VMEM((ROWS, 128), F32),
            pltpu.VMEM((MEMBER_DEV, 8, ROWS), F32),
            pltpu.VMEM((BLOCKS, 1, WIDTH), F32),
            pltpu.VMEM((LOCAL, ROWS, 128), F32),
            pltpu.VMEM((LOCAL, ROWS, 128), F32),
            pltpu.VMEM((LOCAL, ROWS, 128), F32),
            pltpu.VMEM((BLOCKS, 1, WIDTH), F32),
            pltpu.VMEM((6, BLOCKS, 1, WIDTH), F32),
        ]
        + [dma((BLOCKS,)) for _ in range(15)]
        + [dma((12,))],
        compiler_params=pltpu.CompilerParams(
            collective_id=1, has_side_effects=True, vmem_limit_bytes=60 * 1024 * 1024
        ),
    )(action, state_term, target.reshape(1, ROWS), weight_a, value_w)
    return (wgrad, vgrad, sgrad, div.reshape(ROWS))


def solution(mesh):
    in_specs = (
        P("row", None),
        P("member", "row", None),
        P("row"),
        P("member", "row", None),
        P("member", None),
    )
    out_specs = (P("member", "row", None), P("member", None), P("member", "row", None), P("row"))
    return jax.shard_map(body, mesh=mesh, in_specs=in_specs, out_specs=out_specs, check_vma=False)
```

```python
import jax
import jax.numpy as jnp
from jax import lax
from jax.experimental import pallas as pl
from jax.experimental.pallas import tpu as pltpu
from jax.sharding import PartitionSpec as P

EPS = 1e-06
ETA = 5.0
MESH = pl.DeviceIdType.MESH
F32 = jnp.float32
BF16 = jnp.bfloat16

ACT = 1024
HID = 4096
ROWS = 256
LOCAL = 2
MEMBER_DEV = 8
PAIRS = 16 * 15
WIDTH = 256
PER_MEMBER = HID // WIDTH
BLOCKS = LOCAL * PER_MEMBER
PIECE = ROWS // MEMBER_DEV
GROUP = 8
SGRAD_PARTS = 4

SEND_AHEAD = 24
FORWARD_AHEAD = 16
THIRD_AHEAD = 9
SIBLING_AHEAD = 2
CORE_BEHIND = 1
SECOND_BEHIND = 5
THIRD_BEHIND = 8
LAST_BEHIND = 11


def x_first_in_scatter(block):
    return lax.rem(block * 9, 16) < 9


def wait_for(ref, sem):
    pltpu.make_async_copy(ref, ref, sem).wait()


def fold(value):
    out = value[:, 0:128]
    for pos in range(128, value.shape[1], 128):
        out = out + value[:, pos : pos + 128]
    return out


def wide(value, width):
    return jnp.concatenate([value] * (width // 128), axis=1)


def kernel(
    action_ref, state_hbm, target_ref, weight_hbm, value_ref,
    wgrad_hbm, vgrad_ref, sgrad_hbm, div_ref,
    wbuf, state, pre, grad, unit_b, cot, lhs, rhs, core_in, ring_in,
    piece_out, piece_in, total, square_out, square_in, value_w, q_acc, resid, rnorm, vsum, vin,
    load_sem, state_sem, link_done, sib_done, core_done, ring_done, sgrad_sem, wgrad_sem,
    x_sem, y_sem, second_sem, sib_sem, core_sem, ring_sem, mid_sem, last_sem,
    misc_sem,
):
    member = lax.axis_index("member")
    row = lax.axis_index("row")
    yhi = row // 8
    xpos = lax.rem(row // 2, 4)
    core = lax.rem(row, 2)
    oyhi = 1 - yhi
    ocore = 1 - core

    def at_row(yy, xx, cc):
        return (member, yy * 8 + xx * 2 + cc)

    sibling = at_row(yhi, xpos, ocore)
    across = at_row(oyhi, xpos, core)
    xright, xfar, xleft = [lax.rem(xpos + d, 4) for d in (1, 2, 3)]
    right = at_row(yhi, xright, core)
    left = at_row(yhi, xleft, core)
    pair_first = at_row(yhi, xpos + 1 - 2 * lax.rem(xpos, 2), core)
    pair_second = at_row(yhi, 3 - xpos, core)
    low, high = pl.ds(0, 32), pl.ds(32, 32)
    peers = [lax.rem(member + d, MEMBER_DEV) for d in range(1, MEMBER_DEV)]

    def send(src, dst, done, arrived, dev):
        pltpu.make_async_remote_copy(
            src_ref=src, dst_ref=dst, send_sem=done, recv_sem=arrived, device_id=dev, device_id_type=MESH
        ).start()

    barrier = pltpu.get_barrier_semaphore()
    everyone = [sibling, across, right, left] + [(peer, row) for peer in peers]
    for dev in everyone:
        pl.semaphore_signal(barrier, inc=1, device_id=dev, device_id_type=MESH)

    def columns(block):
        return pl.ds(pl.multiple_of(lax.rem(block, PER_MEMBER) * WIDTH, WIDTH), WIDTH)

    def load_block(block, carry):
        m = block // PER_MEMBER
        pltpu.make_async_copy(
            weight_hbm.at[m, :, columns(block)], wbuf.at[block, yhi, xpos, core], load_sem.at[block // GROUP]
        ).start()
        return carry

    lax.fori_loop(0, BLOCKS, load_block, 0)

    def load_state(block, carry):
        m = block // PER_MEMBER
        pltpu.make_async_copy(
            state_hbm.at[m, :, columns(block)], state.at[block], state_sem.at[block // GROUP]
        ).start()
        return carry

    lax.fori_loop(0, BLOCKS, load_state, 0)

    for m in range(LOCAL):
        row_w = value_ref[m : m + 1, :].astype(F32)
        for pos in range(PER_MEMBER):
            value_w[m * PER_MEMBER + pos] = row_w[:, pos * WIDTH : (pos + 1) * WIDTH]
    grad[...] = jnp.zeros_like(grad)
    q_acc[...] = jnp.zeros_like(q_acc)
    for half in range(2):
        part = action_ref[half * 128 : (half + 1) * 128, :].astype(F32)
        lhs[:, half * 128 : (half + 1) * 128] = jnp.transpose(part).astype(BF16)

    pl.semaphore_wait(barrier, len(everyone))

    def first_send(b):
        own = wbuf.at[b, yhi, xpos, core]

        @pl.when(lax.rem(b, GROUP) == 0)
        def _():
            wait_for(wbuf.at[pl.ds(b, GROUP), yhi, xpos, core], load_sem.at[b // GROUP])

        kind_a = x_first_in_scatter(b)

        @pl.when(kind_a)
        def _():
            send(own, own, link_done, y_sem.at[b], across)

        @pl.when(jnp.logical_not(kind_a))
        def _():
            send(own, own, link_done, x_sem.at[b], right)
            send(own, own, link_done, x_sem.at[b], left)

    def second_hop(b):
        kind_a = x_first_in_scatter(b)

        @pl.when(kind_a)
        def _():
            wait_for(wbuf.at[b, oyhi, xpos, core], y_sem.at[b])
            both = wbuf.at[b, :, xpos, core]
            send(both, both, link_done, x_sem.at[b], right)
            send(both, both, link_done, x_sem.at[b], left)

        @pl.when(jnp.logical_not(kind_a))
        def _():
            wait_for(wbuf.at[b, yhi, pl.ds(0, 2), core], x_sem.at[b])
            one = wbuf.at[b, yhi, xleft, core, low]
            send(one, one, link_done, second_sem.at[b], right)
            two = wbuf.at[b, yhi, xright, core, high]
            send(two, two, link_done, second_sem.at[b], left)

    def third_hop(b):
        kind_a = x_first_in_scatter(b)

        @pl.when(kind_a)
        def _():
            wait_for(wbuf.at[b, :, pl.ds(0, 2), core], x_sem.at[b])
            one = wbuf.at[b, :, xleft, core, low]
            send(one, one, link_done, second_sem.at[b], right)
            two = wbuf.at[b, :, xright, core, high]
            send(two, two, link_done, second_sem.at[b], left)

        @pl.when(jnp.logical_not(kind_a))
        def _():
            wait_for(wbuf.at[b, yhi, xfar, core], second_sem.at[b])
            mine = wbuf.at[b, yhi, :, core]
            send(mine, mine, link_done, y_sem.at[b], across)
            send(mine, mine, sib_done, sib_sem.at[b], sibling)

    def to_sibling(b):
        kind_a = x_first_in_scatter(b)

        @pl.when(kind_a)
        def _():
            wait_for(wbuf.at[b, :, xfar, core], second_sem.at[b])
            full = wbuf.at[b, :, :, core]
            send(full, full, sib_done, sib_sem.at[b], sibling)

        @pl.when(jnp.logical_not(kind_a))
        def _():
            theirs = wbuf.at[b, oyhi, :, core]
            wait_for(theirs, y_sem.at[b])
            send(theirs, theirs, sib_done, sib_sem.at[b], sibling)

    def compute_forward(b):
        m = b // PER_MEMBER

        @pl.when(lax.rem(b, GROUP) == 0)
        def _():
            wait_for(state.at[pl.ds(b, GROUP)], state_sem.at[b // GROUP])

        wait_for(wbuf.at[b, :, :, ocore], sib_sem.at[b])
        weights = wbuf[b].reshape(ACT, WIDTH)
        pre[b] = state[b].astype(F32) + jnp.dot(action_ref[...], weights, preferred_element_type=F32)
        vw = value_w[b]
        step = 64
        for pos in range(0, ROWS, step):
            p = pre[b, pos : pos + step, :]
            sig = 0.5 + 0.5 * jnp.tanh(0.5 * p)
            hidden = p * sig
            slope = sig + hidden * (1.0 - sig)
            rhs[pos : pos + step, :] = (slope * vw).astype(BF16)
            q_acc[m, pos : pos + step, :] += fold(hidden * vw)
        grad[m] += lax.dot_general(
            rhs[0:ROWS, :], weights, (((1,), (1,)), ((), ())), preferred_element_type=F32
        )

    def forward_step(i, carry):
        t = i - SEND_AHEAD

        @pl.when(t + SEND_AHEAD < BLOCKS)
        def _():
            first_send(t + SEND_AHEAD)

        @pl.when(jnp.logical_and(t + FORWARD_AHEAD >= 0, t + FORWARD_AHEAD < BLOCKS))
        def _():
            second_hop(t + FORWARD_AHEAD)

        @pl.when(jnp.logical_and(t + THIRD_AHEAD >= 0, t + THIRD_AHEAD < BLOCKS))
        def _():
            third_hop(t + THIRD_AHEAD)

        @pl.when(jnp.logical_and(t + SIBLING_AHEAD >= 0, t + SIBLING_AHEAD < BLOCKS))
        def _():
            to_sibling(t + SIBLING_AHEAD)

        @pl.when(t >= 0)
        def _():
            compute_forward(t)

        return carry

    lax.fori_loop(0, BLOCKS + SEND_AHEAD, forward_step, 0)

    def make_piece(k):
        rows = pl.ds(pl.multiple_of(k * PIECE, PIECE), PIECE)
        both = []
        squares = None
        for m in range(LOCAL):
            g = grad[m, rows, :]
            inv = 1.0 / jnp.sqrt(jnp.sum(g * g, axis=-1, keepdims=True) + EPS)
            u = g * inv
            ub = u.astype(BF16)
            grad[m, rows, :] = u
            unit_b[m, rows, :] = ub
            rnorm[m, rows, :] = jnp.broadcast_to(inv, (PIECE, 128))
            uf = ub.astype(F32)
            both.append(uf)
            sq = fold(uf * uf)
            squares = sq if squares is None else squares + sq
        square_out[rows, :] = squares
        return (both[0] + both[1]).astype(BF16)

    for peer in peers:
        piece_out[peer] = make_piece(peer)
        send(piece_out.at[peer], piece_in.at[member], misc_sem.at[0], misc_sem.at[1], (peer, row))
    piece_in[member] = make_piece(member)

    target_rows = jnp.transpose(jnp.broadcast_to(target_ref[...], (128, ROWS)))
    for m in range(LOCAL):
        q = jnp.sum(q_acc[m], axis=-1, keepdims=True)
        resid[m] = q - target_rows

    wait_for(piece_in.at[pl.ds(0, MEMBER_DEV - 1)], misc_sem.at[1])
    acc = piece_in[0].astype(F32)
    for k in range(1, MEMBER_DEV):
        acc = acc + piece_in[k].astype(F32)
    my_rows = pl.ds(pl.multiple_of(member * PIECE, PIECE), PIECE)
    total[my_rows, :] = acc.astype(BF16)
    for peer in peers:
        send(total.at[my_rows], total.at[my_rows], misc_sem.at[2], misc_sem.at[3], (peer, row))
    square_lane = jnp.sum(jnp.transpose(square_out[...]), axis=0, keepdims=True)
    square_in[member] = jnp.broadcast_to(square_lane, (8, ROWS))
    for peer in peers:
        send(square_in.at[member], square_in.at[member], misc_sem.at[4], misc_sem.at[5], (peer, row))
    wait_for(total.at[pl.ds(0, PIECE * (MEMBER_DEV - 1))], misc_sem.at[3])

    def make_cot(m):
        step = 64
        for pos in range(0, ROWS, step):
            u = grad[m, pos : pos + step, :]
            d = (2.0 * ETA / PAIRS) * (
                total[pos : pos + step, :].astype(F32) - unit_b[m, pos : pos + step, :].astype(F32)
            )
            along = jnp.sum(u * d, axis=-1, keepdims=True)
            c = (d - u * along) * wide(rnorm[m, pos : pos + step, :], ACT)
            cot[m, pos : pos + step, :] = c.astype(BF16)

    def place_cot(m):
        for half in range(2):
            part = cot[m, half * 128 : (half + 1) * 128, :].astype(F32)
            lhs[:, ROWS + half * 128 : ROWS + (half + 1) * 128] = jnp.transpose(part).astype(BF16)

    make_cot(0)
    place_cot(0)
    wait_for(ring_in, link_done)
    wait_for(core_in, sib_done)

    def compute_backward(b):
        m = b // PER_MEMBER
        weights = wbuf[b].reshape(ACT, WIDTH)
        back_all = jnp.dot(cot[m], weights, preferred_element_type=F32)
        vw = value_w[b]
        step = 64
        vacc = jnp.zeros((1, WIDTH), F32)
        for pos in range(0, ROWS, step):
            p = pre[b, pos : pos + step, :]
            back = back_all[pos : pos + step, :]
            res = wide(resid[m, pos : pos + step, :], WIDTH)
            sig = 0.5 + 0.5 * jnp.tanh(0.5 * p)
            rest = 1.0 - sig
            hidden = p * sig
            slope = sig + hidden * rest
            curve = sig * rest * (2.0 + p * (rest - sig))
            dpre = (vw * (slope * res + curve * back)).astype(BF16)
            vacc = vacc + jnp.sum(hidden * res + slope * back, axis=0, keepdims=True)
            rhs[pos : pos + step, :] = dpre
            state[b, pos : pos + step, :] = dpre
            rhs[ROWS + pos : ROWS + pos + step, :] = (slope * vw).astype(BF16)
        vsum[b] = vacc
        pltpu.make_async_copy(state.at[b], sgrad_hbm.at[m, :, columns(b)], sgrad_sem).start()
        part = jnp.dot(lhs[...], rhs[...], preferred_element_type=F32)
        wbuf[b] = part.astype(BF16).reshape(2, 4, 2, 64, WIDTH)
        send(wbuf.at[b, :, :, ocore], core_in.at[b], core_done, core_sem.at[b], sibling)

    def second_send(b):
        wait_for(core_in.at[b], core_sem.at[b])
        for yy in range(2):
            for xx in range(4):
                wbuf[b, yy, xx, core] = (
                    wbuf[b, yy, xx, core].astype(F32) + core_in[b, yy, xx].astype(F32)
                ).astype(BF16)
        kind_a = x_first_in_scatter(b)

        @pl.when(kind_a)
        def _():
            send(wbuf.at[b, :, xfar, core, low], ring_in.at[b, pl.ds(0, 2), low], ring_done, ring_sem.at[b], right)
            send(wbuf.at[b, :, xfar, core, high], ring_in.at[b, pl.ds(0, 2), high], ring_done, ring_sem.at[b], left)

        @pl.when(jnp.logical_not(kind_a))
        def _():
            send(wbuf.at[b, oyhi, :, core], ring_in.at[b, pl.ds(0, 4)], ring_done, ring_sem.at[b], across)

    def add_in(b, yy, xx, parts):
        s = wbuf[b, yy, xx, core].astype(F32)
        for part in parts:
            s = s + ring_in[b, part].astype(F32)
        wbuf[b, yy, xx, core] = s.astype(BF16)

    def add_half(b, yy, xx, part, rows):
        wbuf[b, yy, xx, core, rows] = (
            wbuf[b, yy, xx, core, rows].astype(F32) + ring_in[b, part, rows].astype(F32)
        ).astype(BF16)

    def third_send(b):
        kind_a = x_first_in_scatter(b)

        @pl.when(kind_a)
        def _():
            wait_for(ring_in.at[b, pl.ds(0, 2)], ring_sem.at[b])
            for yy in range(2):
                add_half(b, yy, xright, yy, low)
                add_half(b, yy, xleft, yy, high)
            send(wbuf.at[b, :, xright, core], ring_in.at[b, pl.ds(2, 2)], ring_done, mid_sem.at[b], right)
            send(wbuf.at[b, :, xleft, core], ring_in.at[b, pl.ds(4, 2)], ring_done, mid_sem.at[b], left)

        @pl.when(jnp.logical_not(kind_a))
        def _():
            wait_for(ring_in.at[b, pl.ds(0, 4)], ring_sem.at[b])
            for xx in range(4):
                add_in(b, yhi, xx, [xx])
            send(wbuf.at[b, yhi, xfar, core, low], ring_in.at[b, 4, low], ring_done, mid_sem.at[b], right)
            send(wbuf.at[b, yhi, xfar, core, high], ring_in.at[b, 4, high], ring_done, mid_sem.at[b], left)

    def last_send(b):
        kind_a = x_first_in_scatter(b)

        @pl.when(kind_a)
        def _():
            wait_for(ring_in.at[b, pl.ds(2, 4)], mid_sem.at[b])
            for yy in range(2):
                add_in(b, yy, xpos, [2 + yy, 4 + yy])
            send(wbuf.at[b, oyhi, xpos, core], ring_in.at[b, 6], ring_done, last_sem.at[b], across)

        @pl.when(jnp.logical_not(kind_a))
        def _():
            wait_for(ring_in.at[b, 4], mid_sem.at[b])
            add_half(b, yhi, xright, 4, low)
            add_half(b, yhi, xleft, 4, high)
            send(wbuf.at[b, yhi, xright, core], ring_in.at[b, 5], ring_done, last_sem.at[b], right)
            send(wbuf.at[b, yhi, xleft, core], ring_in.at[b, 6], ring_done, last_sem.at[b], left)

    def finish(b):
        m = b // PER_MEMBER
        kind_a = x_first_in_scatter(b)

        @pl.when(kind_a)
        def _():
            wait_for(ring_in.at[b, 6], last_sem.at[b])
            add_in(b, yhi, xpos, [6])

        @pl.when(jnp.logical_not(kind_a))
        def _():
            wait_for(ring_in.at[b, pl.ds(5, 2)], last_sem.at[b])
            add_in(b, yhi, xpos, [5, 6])

        pltpu.make_async_copy(
            wbuf.at[b, yhi, xpos, core], wgrad_hbm.at[m, :, columns(b)], wgrad_sem
        ).start()

    def backward_step(t, carry):
        @pl.when(t == PER_MEMBER - 2)
        def _():
            make_cot(1)

        @pl.when(t == PER_MEMBER)
        def _():
            place_cot(1)

        @pl.when(t < BLOCKS)
        def _():
            compute_backward(t)

        @pl.when(t == BLOCKS)
        def _():
            send(vsum, vin.at[0], misc_sem.at[6], misc_sem.at[7], sibling)

        @pl.when(jnp.logical_and(t >= CORE_BEHIND, t - CORE_BEHIND < BLOCKS))
        def _():
            second_send(t - CORE_BEHIND)

        @pl.when(t == BLOCKS + 1)
        def _():
            wait_for(vsum, misc_sem.at[6])
            wait_for(vin.at[0], misc_sem.at[7])
            vin[1] = vsum[...] + vin[0]
            send(vin.at[1], vin.at[2], misc_sem.at[8], misc_sem.at[9], across)

        @pl.when(jnp.logical_and(t >= SECOND_BEHIND, t - SECOND_BEHIND < BLOCKS))
        def _():
            third_send(t - SECOND_BEHIND)

        @pl.when(t == BLOCKS + 2)
        def _():
            wait_for(vin.at[2], misc_sem.at[9])
            vin[3] = vin[1] + vin[2]
            send(vin.at[3], vin.at[4], misc_sem.at[10], misc_sem.at[11], pair_first)

        @pl.when(jnp.logical_and(t >= THIRD_BEHIND, t - THIRD_BEHIND < BLOCKS))
        def _():
            last_send(t - THIRD_BEHIND)

        @pl.when(t == BLOCKS + 4)
        def _():
            wait_for(vin.at[4], misc_sem.at[11])
            vin[5] = vin[3] + vin[4]
            send(vin.at[5], vin.at[6], misc_sem.at[12], misc_sem.at[13], pair_second)

        @pl.when(jnp.logical_and(t >= LAST_BEHIND, t - LAST_BEHIND < BLOCKS))
        def _():
            finish(t - LAST_BEHIND)

        return carry

    lax.fori_loop(0, BLOCKS + LAST_BEHIND, backward_step, 0)

    wait_for(square_in.at[pl.ds(0, MEMBER_DEV - 1)], misc_sem.at[5])
    tsq = []
    for pos in range(0, ROWS, 64):
        tf = total[pos : pos + 64, :].astype(F32)
        tsq.append(fold(tf * tf))
    cross_sum = jnp.sum(jnp.transpose(jnp.concatenate(tsq, axis=0)), axis=0, keepdims=True)
    squares = square_in[0]
    for k in range(1, MEMBER_DEV):
        squares = squares + square_in[k]
    div_ref[...] = (cross_sum - squares[0:1, :]) * (1.0 / PAIRS)

    wait_for(vin.at[6], misc_sem.at[13])
    for b in range(BLOCKS):
        m, pos = b // PER_MEMBER, b % PER_MEMBER
        vgrad_ref[m : m + 1, pos * WIDTH : (pos + 1) * WIDTH] = vin[5, b] + vin[6, b]

    wait_for(piece_out.at[pl.ds(0, MEMBER_DEV - 1)], misc_sem.at[0])
    wait_for(total.at[pl.ds(0, PIECE * (MEMBER_DEV - 1))], misc_sem.at[2])
    wait_for(square_in.at[pl.ds(0, MEMBER_DEV - 1)], misc_sem.at[4])
    for pos in (8, 10, 12):
        wait_for(vin.at[0], misc_sem.at[pos])

    wait_for(core_in, core_done)
    wait_for(ring_in, ring_done)
    wait_for(state, sgrad_sem)
    wait_for(wbuf.at[:, yhi, xpos, core], wgrad_sem)


def hand_out(
    wgrad, vgrad, sgrad, div, wgrad_out, vgrad_out, sgrad_out, div_out,
    wgrad_buf, vgrad_buf, sgrad_buf, div_buf, in_sem, out_sem,
):
    steps = []
    for m in range(LOCAL):
        for part in range(SGRAD_PARTS):
            rows = pl.ds(part * (ROWS // SGRAD_PARTS), ROWS // SGRAD_PARTS)
            steps.append((sgrad.at[m, rows], sgrad_buf.at[m, rows], sgrad_out.at[m, rows]))
    for m in range(LOCAL):
        steps.append((wgrad.at[m], wgrad_buf.at[m], wgrad_out.at[m]))
    steps.append((vgrad, vgrad_buf, vgrad_out))
    steps.append((div, div_buf, div_out))
    loads = [pltpu.make_async_copy(src, buf, in_sem.at[i]) for i, (src, buf, dst) in enumerate(steps)]
    stores = [pltpu.make_async_copy(buf, dst, out_sem.at[i]) for i, (src, buf, dst) in enumerate(steps)]
    for load in loads:
        load.start()
    for load, store in zip(loads, stores):
        load.wait()
        store.start()
    for store in stores:
        store.wait()


def body(action, state_term, target, weight_a, value_w):
    any_spec = pl.BlockSpec(memory_space=pl.ANY)
    vmem_spec = pl.BlockSpec(memory_space=pltpu.VMEM)
    dma = pltpu.SemaphoreType.DMA
    wgrad, vgrad, sgrad, div = pl.pallas_call(
        kernel,
        out_shape=(
            jax.ShapeDtypeStruct((LOCAL, 64, HID), BF16),
            jax.ShapeDtypeStruct((LOCAL, HID), F32),
            jax.ShapeDtypeStruct((LOCAL, ROWS, HID), BF16),
            jax.ShapeDtypeStruct((1, ROWS), F32),
        ),
        in_specs=[vmem_spec, any_spec, vmem_spec, any_spec, vmem_spec],
        out_specs=(any_spec, vmem_spec, any_spec, vmem_spec),
        scratch_shapes=[
            pltpu.VMEM((BLOCKS, 2, 4, 2, 64, WIDTH), BF16),
            pltpu.VMEM((BLOCKS, ROWS, WIDTH), BF16),
            pltpu.VMEM((BLOCKS, ROWS, WIDTH), F32),
            pltpu.VMEM((LOCAL, ROWS, ACT), F32),
            pltpu.VMEM((LOCAL, ROWS, ACT), BF16),
            pltpu.VMEM((LOCAL, ROWS, ACT), BF16),
            pltpu.VMEM((ACT, 2 * ROWS), BF16),
            pltpu.VMEM((2 * ROWS, WIDTH), BF16),
            pltpu.VMEM((BLOCKS, 2, 4, 64, WIDTH), BF16),
            pltpu.VMEM((BLOCKS, 7, 64, WIDTH), BF16),
            pltpu.VMEM((MEMBER_DEV, PIECE, ACT), BF16),
            pltpu.VMEM((MEMBER_DEV, PIECE, ACT), BF16),
            pltpu.VMEM((ROWS, ACT), BF16),
            pltpu.VMEM((ROWS, 128), F32),
            pltpu.VMEM((MEMBER_DEV, 8, ROWS), F32),
            pltpu.VMEM((BLOCKS, 1, WIDTH), F32),
            pltpu.VMEM((LOCAL, ROWS, 128), F32),
            pltpu.VMEM((LOCAL, ROWS, 128), F32),
            pltpu.VMEM((LOCAL, ROWS, 128), F32),
            pltpu.VMEM((BLOCKS, 1, WIDTH), F32),
            pltpu.VMEM((7, BLOCKS, 1, WIDTH), F32),
        ]
        + [dma((BLOCKS // GROUP,)) for _ in range(2)]
        + [dma for _ in range(6)]
        + [dma((BLOCKS,)) for _ in range(8)]
        + [dma((14,))],
        compiler_params=pltpu.CompilerParams(
            collective_id=1, has_side_effects=True, vmem_limit_bytes=60 * 1024 * 1024
        ),
    )(action, state_term, target.reshape(1, ROWS), weight_a, value_w)
    wgrad, vgrad, sgrad, div = pl.pallas_call(
        hand_out,
        out_shape=tuple(jax.ShapeDtypeStruct(x.shape, x.dtype) for x in (wgrad, vgrad, sgrad, div)),
        in_specs=[any_spec] * 4,
        out_specs=(any_spec,) * 4,
        scratch_shapes=[pltpu.VMEM(x.shape, x.dtype) for x in (wgrad, vgrad, sgrad, div)]
        + [dma((2 + LOCAL * (SGRAD_PARTS + 1),))] * 2,
        compiler_params=pltpu.CompilerParams(vmem_limit_bytes=60 * 1024 * 1024),
    )(wgrad, vgrad, sgrad, div)
    return (wgrad, vgrad, sgrad, div.reshape(ROWS))


def solution(mesh):
    in_specs = (
        P("row", None),
        P("member", "row", None),
        P("row"),
        P("member", "row", None),
        P("member", None),
    )
    out_specs = (P("member", "row", None), P("member", None), P("member", "row", None), P("row"))
    return jax.shard_map(body, mesh=mesh, in_specs=in_specs, out_specs=out_specs, check_vma=False)
```

```python
import jax
import jax.numpy as jnp
from jax import lax
from jax.experimental import pallas as pl
from jax.experimental.pallas import tpu as pltpu
from jax.sharding import PartitionSpec as P

EPS = 1e-06
ETA = 5.0
MESH = pl.DeviceIdType.MESH
F32 = jnp.float32
BF16 = jnp.bfloat16

ACT = 1024
HID = 4096
ROWS = 256
LOCAL = 2
MEMBER_DEV = 8
PAIRS = 16 * 15
WIDTH = 256
PER_MEMBER = HID // WIDTH
BLOCKS = LOCAL * PER_MEMBER
PIECE = ROWS // MEMBER_DEV
GROUP = 8
HALF_PIECE = PIECE // 2
HALF = ROWS // 2
SGRAD_PARTS = 4

SEND_AHEAD = 24
FORWARD_AHEAD = 16
THIRD_AHEAD = 9
SIBLING_AHEAD = 2
CORE_BEHIND = 2
SECOND_BEHIND = 6
THIRD_BEHIND = 16
LAST_BEHIND = 31


def x_first_in_scatter(block):
    return lax.rem(block * 9, 16) < 9


def wait_for(ref, sem):
    pltpu.make_async_copy(ref, ref, sem).wait()


def fold(value):
    out = value[:, 0:128]
    for pos in range(128, value.shape[1], 128):
        out = out + value[:, pos : pos + 128]
    return out


def wide(value, width):
    return jnp.concatenate([value] * (width // 128), axis=1)


def kernel(
    action_ref, state_hbm, target_ref, weight_hbm, value_ref,
    wgrad_hbm, vgrad_ref, sgrad_hbm, div_ref,
    wbuf, state, hidden, slope, curve, grad, unit_b, cot, lhs, rhs, core_in, ring_in,
    piece_out, piece_in, total, square_out, square_in, value_w, q_acc, resid, rnorm, vsum, vin,
    load_sem, state_sem, link_done, sib_done, core_done, ring_done, sgrad_sem, wgrad_sem,
    x_sem, y_sem, second_sem, sib_sem, core_sem, ring_sem, mid_sem, last_sem,
    misc_sem,
):
    member = lax.axis_index("member")
    row = lax.axis_index("row")
    yhi = row // 8
    xpos = lax.rem(row // 2, 4)
    core = lax.rem(row, 2)
    oyhi = 1 - yhi
    ocore = 1 - core

    def at_row(yy, xx, cc):
        return (member, yy * 8 + xx * 2 + cc)

    sibling = at_row(yhi, xpos, ocore)
    across = at_row(oyhi, xpos, core)
    xright, xfar, xleft = [lax.rem(xpos + d, 4) for d in (1, 2, 3)]
    right = at_row(yhi, xright, core)
    left = at_row(yhi, xleft, core)
    pair_first = at_row(yhi, xpos + 1 - 2 * lax.rem(xpos, 2), core)
    pair_second = at_row(yhi, 3 - xpos, core)
    low, high = pl.ds(0, 32), pl.ds(32, 32)
    peers = [lax.rem(member + d, MEMBER_DEV) for d in range(1, MEMBER_DEV)]

    def send(src, dst, done, arrived, dev):
        pltpu.make_async_remote_copy(
            src_ref=src, dst_ref=dst, send_sem=done, recv_sem=arrived, device_id=dev, device_id_type=MESH
        ).start()

    barrier = pltpu.get_barrier_semaphore()
    everyone = [sibling, across, right, left] + [(peer, row) for peer in peers]
    for dev in everyone:
        pl.semaphore_signal(barrier, inc=1, device_id=dev, device_id_type=MESH)

    def columns(block):
        return pl.ds(pl.multiple_of(lax.rem(block, PER_MEMBER) * WIDTH, WIDTH), WIDTH)

    def load_block(block, carry):
        m = block // PER_MEMBER
        pltpu.make_async_copy(
            weight_hbm.at[m, :, columns(block)], wbuf.at[block, yhi, xpos, core], load_sem.at[block // GROUP]
        ).start()
        return carry

    lax.fori_loop(0, BLOCKS, load_block, 0)

    def load_state(block, carry):
        m = block // PER_MEMBER
        pltpu.make_async_copy(
            state_hbm.at[m, :, columns(block)], state.at[block], state_sem.at[block // GROUP]
        ).start()
        return carry

    lax.fori_loop(0, BLOCKS, load_state, 0)

    for m in range(LOCAL):
        row_w = value_ref[m : m + 1, :].astype(F32)
        for pos in range(PER_MEMBER):
            value_w[m * PER_MEMBER + pos] = row_w[:, pos * WIDTH : (pos + 1) * WIDTH]
    grad[...] = jnp.zeros_like(grad)
    q_acc[...] = jnp.zeros_like(q_acc)
    for half in range(2):
        part = action_ref[half * 128 : (half + 1) * 128, :].astype(F32)
        turned = jnp.transpose(part).astype(BF16)
        for m in range(LOCAL):
            lhs[m, :, half * ROWS : half * ROWS + HALF] = turned

    pl.semaphore_wait(barrier, len(everyone))

    def first_send(b):
        own = wbuf.at[b, yhi, xpos, core]

        @pl.when(lax.rem(b, GROUP) == 0)
        def _():
            wait_for(wbuf.at[pl.ds(b, GROUP), yhi, xpos, core], load_sem.at[b // GROUP])

        kind_a = x_first_in_scatter(b)

        @pl.when(kind_a)
        def _():
            send(own, own, link_done, y_sem.at[b], across)

        @pl.when(jnp.logical_not(kind_a))
        def _():
            send(own, own, link_done, x_sem.at[b], right)
            send(own, own, link_done, x_sem.at[b], left)

    def second_hop(b):
        kind_a = x_first_in_scatter(b)

        @pl.when(kind_a)
        def _():
            wait_for(wbuf.at[b, oyhi, xpos, core], y_sem.at[b])
            both = wbuf.at[b, :, xpos, core]
            send(both, both, link_done, x_sem.at[b], right)
            send(both, both, link_done, x_sem.at[b], left)

        @pl.when(jnp.logical_not(kind_a))
        def _():
            wait_for(wbuf.at[b, yhi, pl.ds(0, 2), core], x_sem.at[b])
            one = wbuf.at[b, yhi, xleft, core, low]
            send(one, one, link_done, second_sem.at[b], right)
            two = wbuf.at[b, yhi, xright, core, high]
            send(two, two, link_done, second_sem.at[b], left)

    def third_hop(b):
        kind_a = x_first_in_scatter(b)

        @pl.when(kind_a)
        def _():
            wait_for(wbuf.at[b, :, pl.ds(0, 2), core], x_sem.at[b])
            one = wbuf.at[b, :, xleft, core, low]
            send(one, one, link_done, second_sem.at[b], right)
            two = wbuf.at[b, :, xright, core, high]
            send(two, two, link_done, second_sem.at[b], left)

        @pl.when(jnp.logical_not(kind_a))
        def _():
            wait_for(wbuf.at[b, yhi, xfar, core], second_sem.at[b])
            mine = wbuf.at[b, yhi, :, core]
            send(mine, mine, link_done, y_sem.at[b], across)
            send(mine, mine, sib_done, sib_sem.at[b], sibling)

    def to_sibling(b):
        kind_a = x_first_in_scatter(b)

        @pl.when(kind_a)
        def _():
            wait_for(wbuf.at[b, :, xfar, core], second_sem.at[b])
            full = wbuf.at[b, :, :, core]
            send(full, full, sib_done, sib_sem.at[b], sibling)

        @pl.when(jnp.logical_not(kind_a))
        def _():
            theirs = wbuf.at[b, oyhi, :, core]
            wait_for(theirs, y_sem.at[b])
            send(theirs, theirs, sib_done, sib_sem.at[b], sibling)

    def arrive(b):
        @pl.when(lax.rem(b, GROUP) == 0)
        def _():
            wait_for(state.at[pl.ds(b, GROUP)], state_sem.at[b // GROUP])

        wait_for(wbuf.at[b, :, :, ocore], sib_sem.at[b])

    def forward_product(b):
        return jnp.dot(action_ref[...], wbuf[b].reshape(ACT, WIDTH), preferred_element_type=F32)

    def forward_elementwise(b, product):
        m = b // PER_MEMBER
        vw = value_w[b]
        step = 64
        for pos in range(0, ROWS, step):
            rows = slice(pos, pos + step)
            p = state[b, rows, :].astype(F32) + product[rows, :]
            sig = 0.5 + 0.5 * jnp.tanh(0.5 * p)
            rest = 1.0 - sig
            hid = p * sig
            first = sig + hid * rest
            state[b, rows, :] = (first * vw).astype(BF16)
            slope[b, rows, :] = first.astype(BF16)
            curve[b, rows, :] = (sig * rest * (2.0 + p * (rest - sig)) * vw).astype(BF16)
            hidden[b, rows, :] = hid.astype(BF16)
            q_acc[m, rows, :] += fold(hid * vw)

    def gradient_product(b):
        grad[b // PER_MEMBER] += lax.dot_general(
            state[b], wbuf[b].reshape(ACT, WIDTH), (((1,), (1,)), ((), ())), preferred_element_type=F32
        )

    def compute_forward(t):
        @pl.when(t == 0)
        def _():
            arrive(t)
            forward_elementwise(t, forward_product(t))

        @pl.when(t > 0)
        def _():
            arrive(t)
            product = forward_product(t)
            gradient_product(t - 1)
            forward_elementwise(t, product)

        @pl.when(t == BLOCKS - 1)
        def _():
            gradient_product(t)

    def forward_step(i, carry):
        t = i - SEND_AHEAD

        @pl.when(t + SEND_AHEAD < BLOCKS)
        def _():
            first_send(t + SEND_AHEAD)

        @pl.when(jnp.logical_and(t + FORWARD_AHEAD >= 0, t + FORWARD_AHEAD < BLOCKS))
        def _():
            second_hop(t + FORWARD_AHEAD)

        @pl.when(jnp.logical_and(t + THIRD_AHEAD >= 0, t + THIRD_AHEAD < BLOCKS))
        def _():
            third_hop(t + THIRD_AHEAD)

        @pl.when(jnp.logical_and(t + SIBLING_AHEAD >= 0, t + SIBLING_AHEAD < BLOCKS))
        def _():
            to_sibling(t + SIBLING_AHEAD)

        @pl.when(t >= 0)
        def _():
            compute_forward(t)

        return carry

    lax.fori_loop(0, BLOCKS + SEND_AHEAD, forward_step, 0)

    def make_piece(k, half):
        rows = pl.ds(pl.multiple_of(k * PIECE + half * HALF_PIECE, HALF_PIECE), HALF_PIECE)
        both = []
        squares = None
        for m in range(LOCAL):
            g = grad[m, rows, :]
            inv = 1.0 / jnp.sqrt(jnp.sum(g * g, axis=-1, keepdims=True) + EPS)
            u = g * inv
            ub = u.astype(BF16)
            grad[m, rows, :] = u
            unit_b[m, rows, :] = ub
            rnorm[m, rows, :] = jnp.broadcast_to(inv, (HALF_PIECE, 128))
            uf = ub.astype(F32)
            both.append(uf)
            sq = fold(uf * uf)
            squares = sq if squares is None else squares + sq
        square_out[rows, :] = squares
        return (both[0] + both[1]).astype(BF16)

    for half in range(2):
        rows = pl.ds(half * HALF_PIECE, HALF_PIECE)
        for peer in peers:
            piece_out[peer, rows] = make_piece(peer, half)
            send(
                piece_out.at[peer, rows], piece_in.at[member, rows],
                misc_sem.at[0], misc_sem.at[14 + half], (peer, row),
            )
        piece_in[member, rows] = make_piece(member, half)

    target_rows = jnp.transpose(jnp.broadcast_to(target_ref[...], (128, ROWS)))
    for m in range(LOCAL):
        q = jnp.sum(q_acc[m], axis=-1, keepdims=True)
        resid[m] = q - target_rows

    for half in range(2):
        rows = pl.ds(half * HALF_PIECE, HALF_PIECE)
        wait_for(piece_in.at[pl.ds(0, MEMBER_DEV - 1), rows], misc_sem.at[14 + half])
        acc = piece_in[0, rows].astype(F32)
        for k in range(1, MEMBER_DEV):
            acc = acc + piece_in[k, rows].astype(F32)
        mine = pl.ds(pl.multiple_of(member * PIECE + half * HALF_PIECE, HALF_PIECE), HALF_PIECE)
        total[mine, :] = acc.astype(BF16)
        for peer in peers:
            send(total.at[mine], total.at[mine], misc_sem.at[2], misc_sem.at[3], (peer, row))
    square_lane = jnp.sum(jnp.transpose(square_out[...]), axis=0, keepdims=True)
    square_in[member] = jnp.broadcast_to(square_lane, (8, ROWS))
    for peer in peers:
        send(square_in.at[member], square_in.at[member], misc_sem.at[4], misc_sem.at[5], (peer, row))
    wait_for(total.at[pl.ds(0, PIECE * (MEMBER_DEV - 1))], misc_sem.at[3])

    def make_cot(m):
        step = 64
        for pos in range(0, ROWS, step):
            u = grad[m, pos : pos + step, :]
            d = (2.0 * ETA / PAIRS) * (
                total[pos : pos + step, :].astype(F32) - unit_b[m, pos : pos + step, :].astype(F32)
            )
            along = jnp.sum(u * d, axis=-1, keepdims=True)
            c = (d - u * along) * wide(rnorm[m, pos : pos + step, :], ACT)
            cot[m, pos : pos + step, :] = c.astype(BF16)

    def place_cot(m):
        for half in range(2):
            part = cot[m, half * 128 : (half + 1) * 128, :].astype(F32)
            lhs[m, :, half * ROWS + HALF : (half + 1) * ROWS] = jnp.transpose(part).astype(BF16)

    make_cot(0)
    place_cot(0)
    wait_for(ring_in, link_done)
    wait_for(core_in, sib_done)

    def back_product(b):
        return jnp.dot(cot[b // PER_MEMBER], wbuf[b].reshape(ACT, WIDTH), preferred_element_type=F32)

    def partial_product(b):
        m = b // PER_MEMBER
        slot = lax.rem(b, 2)
        for q in range(4):
            some = slice(q * 256, (q + 1) * 256)
            part = jnp.dot(lhs[m, some, 0:ROWS], rhs[slot, 0:ROWS, :], preferred_element_type=F32)
            part = part + jnp.dot(
                lhs[m, some, ROWS : 2 * ROWS], rhs[slot, ROWS : 2 * ROWS, :], preferred_element_type=F32
            )
            wbuf[b, q // 2, 2 * (q % 2) : 2 * (q % 2) + 2] = part.astype(BF16).reshape(2, 2, 64, WIDTH)

    def elementwise(b, back_all):
        m = b // PER_MEMBER
        slot = lax.rem(b, 2)
        vacc = jnp.zeros((1, WIDTH), F32)
        step = 64
        for pos in range(0, ROWS, step):
            rows = slice(pos, pos + step)
            at = pos + (pos // HALF) * HALF
            back = back_all[rows, :]
            res = wide(resid[m, rows, :], WIDTH)
            tangent = state[b, rows, :]
            dpre = (tangent.astype(F32) * res + curve[b, rows, :].astype(F32) * back).astype(BF16)
            vacc = vacc + jnp.sum(
                hidden[b, rows, :].astype(F32) * res + slope[b, rows, :].astype(F32) * back, axis=0, keepdims=True
            )
            rhs[slot, at : at + step, :] = dpre
            rhs[slot, at + HALF : at + HALF + step, :] = tangent
            state[b, rows, :] = dpre
        vsum[b] = vacc

    def state_out(b):
        pltpu.make_async_copy(
            state.at[b], sgrad_hbm.at[b // PER_MEMBER, :, columns(b)], sgrad_sem
        ).start()

    def first_send_back(b):
        send(wbuf.at[b, :, :, ocore], core_in.at[b], core_done, core_sem.at[b], sibling)

    def compute_backward(t):
        @pl.when(t == 0)
        def _():
            elementwise(t, back_product(t))
            state_out(t)

        @pl.when(jnp.logical_and(t > 0, t < BLOCKS))
        def _():
            back_all = back_product(t)
            partial_product(t - 1)
            elementwise(t, back_all)
            first_send_back(t - 1)
            state_out(t)

        @pl.when(t == BLOCKS)
        def _():
            partial_product(t - 1)
            first_send_back(t - 1)

    def second_send(b):
        wait_for(core_in.at[b], core_sem.at[b])
        for yy in range(2):
            for xx in range(4):
                wbuf[b, yy, xx, core] = (
                    wbuf[b, yy, xx, core].astype(F32) + core_in[b, yy, xx].astype(F32)
                ).astype(BF16)
        kind_a = x_first_in_scatter(b)

        @pl.when(kind_a)
        def _():
            send(wbuf.at[b, :, xfar, core, low], ring_in.at[b, pl.ds(0, 2), low], ring_done, ring_sem.at[b], right)
            send(wbuf.at[b, :, xfar, core, high], ring_in.at[b, pl.ds(0, 2), high], ring_done, ring_sem.at[b], left)

        @pl.when(jnp.logical_not(kind_a))
        def _():
            send(wbuf.at[b, oyhi, :, core], ring_in.at[b, pl.ds(0, 4)], ring_done, ring_sem.at[b], across)

    def add_in(b, yy, xx, parts):
        s = wbuf[b, yy, xx, core].astype(F32)
        for part in parts:
            s = s + ring_in[b, part].astype(F32)
        wbuf[b, yy, xx, core] = s.astype(BF16)

    def add_half(b, yy, xx, part, rows):
        wbuf[b, yy, xx, core, rows] = (
            wbuf[b, yy, xx, core, rows].astype(F32) + ring_in[b, part, rows].astype(F32)
        ).astype(BF16)

    def third_send(b):
        kind_a = x_first_in_scatter(b)

        @pl.when(kind_a)
        def _():
            wait_for(ring_in.at[b, pl.ds(0, 2)], ring_sem.at[b])
            for yy in range(2):
                add_half(b, yy, xright, yy, low)
                add_half(b, yy, xleft, yy, high)
            send(wbuf.at[b, :, xright, core], ring_in.at[b, pl.ds(2, 2)], ring_done, mid_sem.at[b], right)
            send(wbuf.at[b, :, xleft, core], ring_in.at[b, pl.ds(4, 2)], ring_done, mid_sem.at[b], left)

        @pl.when(jnp.logical_not(kind_a))
        def _():
            wait_for(ring_in.at[b, pl.ds(0, 4)], ring_sem.at[b])
            for xx in range(4):
                add_in(b, yhi, xx, [xx])
            send(wbuf.at[b, yhi, xfar, core, low], ring_in.at[b, 4, low], ring_done, mid_sem.at[b], right)
            send(wbuf.at[b, yhi, xfar, core, high], ring_in.at[b, 4, high], ring_done, mid_sem.at[b], left)

    def last_send(b):
        kind_a = x_first_in_scatter(b)

        @pl.when(kind_a)
        def _():
            wait_for(ring_in.at[b, pl.ds(2, 4)], mid_sem.at[b])
            for yy in range(2):
                add_in(b, yy, xpos, [2 + yy, 4 + yy])
            send(wbuf.at[b, oyhi, xpos, core], ring_in.at[b, 6], ring_done, last_sem.at[b], across)

        @pl.when(jnp.logical_not(kind_a))
        def _():
            wait_for(ring_in.at[b, 4], mid_sem.at[b])
            add_half(b, yhi, xright, 4, low)
            add_half(b, yhi, xleft, 4, high)
            send(wbuf.at[b, yhi, xright, core], ring_in.at[b, 5], ring_done, last_sem.at[b], right)
            send(wbuf.at[b, yhi, xleft, core], ring_in.at[b, 6], ring_done, last_sem.at[b], left)

    def finish(b):
        m = b // PER_MEMBER
        kind_a = x_first_in_scatter(b)

        @pl.when(kind_a)
        def _():
            wait_for(ring_in.at[b, 6], last_sem.at[b])
            add_in(b, yhi, xpos, [6])

        @pl.when(jnp.logical_not(kind_a))
        def _():
            wait_for(ring_in.at[b, pl.ds(5, 2)], last_sem.at[b])
            add_in(b, yhi, xpos, [5, 6])

        pltpu.make_async_copy(
            wbuf.at[b, yhi, xpos, core], wgrad_hbm.at[m, :, columns(b)], wgrad_sem
        ).start()

    def backward_step(t, carry):
        @pl.when(t == PER_MEMBER - 2)
        def _():
            make_cot(1)
            place_cot(1)

        compute_backward(t)

        @pl.when(t == BLOCKS + 1)
        def _():
            send(vsum, vin.at[0], misc_sem.at[6], misc_sem.at[7], sibling)

        @pl.when(jnp.logical_and(t >= CORE_BEHIND, t - CORE_BEHIND < BLOCKS))
        def _():
            second_send(t - CORE_BEHIND)

        @pl.when(t == BLOCKS + 2)
        def _():
            wait_for(vsum, misc_sem.at[6])
            wait_for(vin.at[0], misc_sem.at[7])
            vin[1] = vsum[...] + vin[0]
            send(vin.at[1], vin.at[2], misc_sem.at[8], misc_sem.at[9], across)

        @pl.when(jnp.logical_and(t >= SECOND_BEHIND, t - SECOND_BEHIND < BLOCKS))
        def _():
            third_send(t - SECOND_BEHIND)

        @pl.when(t == BLOCKS + 3)
        def _():
            wait_for(vin.at[2], misc_sem.at[9])
            vin[3] = vin[1] + vin[2]
            send(vin.at[3], vin.at[4], misc_sem.at[10], misc_sem.at[11], pair_first)

        @pl.when(jnp.logical_and(t >= THIRD_BEHIND, t - THIRD_BEHIND < BLOCKS))
        def _():
            last_send(t - THIRD_BEHIND)

        @pl.when(t == BLOCKS + 5)
        def _():
            wait_for(vin.at[4], misc_sem.at[11])
            vin[5] = vin[3] + vin[4]
            send(vin.at[5], vin.at[6], misc_sem.at[12], misc_sem.at[13], pair_second)

        @pl.when(jnp.logical_and(t >= LAST_BEHIND, t - LAST_BEHIND < BLOCKS))
        def _():
            finish(t - LAST_BEHIND)

        return carry

    lax.fori_loop(0, BLOCKS + LAST_BEHIND, backward_step, 0)

    wait_for(square_in.at[pl.ds(0, MEMBER_DEV - 1)], misc_sem.at[5])
    tsq = []
    for pos in range(0, ROWS, 64):
        tf = total[pos : pos + 64, :].astype(F32)
        tsq.append(fold(tf * tf))
    cross_sum = jnp.sum(jnp.transpose(jnp.concatenate(tsq, axis=0)), axis=0, keepdims=True)
    squares = square_in[0]
    for k in range(1, MEMBER_DEV):
        squares = squares + square_in[k]
    div_ref[...] = (cross_sum - squares[0:1, :]) * (1.0 / PAIRS)

    wait_for(vin.at[6], misc_sem.at[13])
    for b in range(BLOCKS):
        m, pos = b // PER_MEMBER, b % PER_MEMBER
        vgrad_ref[m : m + 1, pos * WIDTH : (pos + 1) * WIDTH] = vin[5, b] + vin[6, b]

    wait_for(piece_out.at[pl.ds(0, MEMBER_DEV - 1)], misc_sem.at[0])
    wait_for(total.at[pl.ds(0, PIECE * (MEMBER_DEV - 1))], misc_sem.at[2])
    wait_for(square_in.at[pl.ds(0, MEMBER_DEV - 1)], misc_sem.at[4])
    for pos in (8, 10, 12):
        wait_for(vin.at[0], misc_sem.at[pos])

    wait_for(core_in, core_done)
    wait_for(ring_in, ring_done)
    wait_for(state, sgrad_sem)
    wait_for(wbuf.at[:, yhi, xpos, core], wgrad_sem)


def hand_out(
    wgrad, vgrad, sgrad, div, wgrad_out, vgrad_out, sgrad_out, div_out,
    wgrad_buf, vgrad_buf, sgrad_buf, div_buf, in_sem, out_sem,
):
    steps = []
    for m in range(LOCAL):
        for part in range(SGRAD_PARTS):
            rows = pl.ds(part * (ROWS // SGRAD_PARTS), ROWS // SGRAD_PARTS)
            steps.append((sgrad.at[m, rows], sgrad_buf.at[m, rows], sgrad_out.at[m, rows]))
    for m in range(LOCAL):
        steps.append((wgrad.at[m], wgrad_buf.at[m], wgrad_out.at[m]))
    steps.append((vgrad, vgrad_buf, vgrad_out))
    steps.append((div, div_buf, div_out))
    loads = [pltpu.make_async_copy(src, buf, in_sem.at[i]) for i, (src, buf, dst) in enumerate(steps)]
    stores = [pltpu.make_async_copy(buf, dst, out_sem.at[i]) for i, (src, buf, dst) in enumerate(steps)]
    for load in loads:
        load.start()
    for load, store in zip(loads, stores):
        load.wait()
        store.start()
    for store in stores:
        store.wait()


def body(action, state_term, target, weight_a, value_w):
    any_spec = pl.BlockSpec(memory_space=pl.ANY)
    vmem_spec = pl.BlockSpec(memory_space=pltpu.VMEM)
    dma = pltpu.SemaphoreType.DMA
    wgrad, vgrad, sgrad, div = pl.pallas_call(
        kernel,
        out_shape=(
            jax.ShapeDtypeStruct((LOCAL, 64, HID), BF16),
            jax.ShapeDtypeStruct((LOCAL, HID), F32),
            jax.ShapeDtypeStruct((LOCAL, ROWS, HID), BF16),
            jax.ShapeDtypeStruct((1, ROWS), F32),
        ),
        in_specs=[vmem_spec, any_spec, vmem_spec, any_spec, vmem_spec],
        out_specs=(any_spec, vmem_spec, any_spec, vmem_spec),
        scratch_shapes=[
            pltpu.VMEM((BLOCKS, 2, 4, 2, 64, WIDTH), BF16),
            pltpu.VMEM((BLOCKS, ROWS, WIDTH), BF16),
            pltpu.VMEM((BLOCKS, ROWS, WIDTH), BF16),
            pltpu.VMEM((BLOCKS, ROWS, WIDTH), BF16),
            pltpu.VMEM((BLOCKS, ROWS, WIDTH), BF16),
            pltpu.VMEM((LOCAL, ROWS, ACT), F32),
            pltpu.VMEM((LOCAL, ROWS, ACT), BF16),
            pltpu.VMEM((LOCAL, ROWS, ACT), BF16),
            pltpu.VMEM((LOCAL, ACT, 2 * ROWS), BF16),
            pltpu.VMEM((2, 2 * ROWS, WIDTH), BF16),
            pltpu.VMEM((BLOCKS, 2, 4, 64, WIDTH), BF16),
            pltpu.VMEM((BLOCKS, 7, 64, WIDTH), BF16),
            pltpu.VMEM((MEMBER_DEV, PIECE, ACT), BF16),
            pltpu.VMEM((MEMBER_DEV, PIECE, ACT), BF16),
            pltpu.VMEM((ROWS, ACT), BF16),
            pltpu.VMEM((ROWS, 128), F32),
            pltpu.VMEM((MEMBER_DEV, 8, ROWS), F32),
            pltpu.VMEM((BLOCKS, 1, WIDTH), F32),
            pltpu.VMEM((LOCAL, ROWS, 128), F32),
            pltpu.VMEM((LOCAL, ROWS, 128), F32),
            pltpu.VMEM((LOCAL, ROWS, 128), F32),
            pltpu.VMEM((BLOCKS, 1, WIDTH), F32),
            pltpu.VMEM((7, BLOCKS, 1, WIDTH), F32),
        ]
        + [dma((BLOCKS // GROUP,)) for _ in range(2)]
        + [dma for _ in range(6)]
        + [dma((BLOCKS,)) for _ in range(8)]
        + [dma((16,))],
        compiler_params=pltpu.CompilerParams(
            collective_id=1, has_side_effects=True, vmem_limit_bytes=60 * 1024 * 1024
        ),
    )(action, state_term, target.reshape(1, ROWS), weight_a, value_w)
    wgrad, vgrad, sgrad, div = pl.pallas_call(
        hand_out,
        out_shape=tuple(jax.ShapeDtypeStruct(x.shape, x.dtype) for x in (wgrad, vgrad, sgrad, div)),
        in_specs=[any_spec] * 4,
        out_specs=(any_spec,) * 4,
        scratch_shapes=[pltpu.VMEM(x.shape, x.dtype) for x in (wgrad, vgrad, sgrad, div)]
        + [dma((2 + LOCAL * (SGRAD_PARTS + 1),))] * 2,
        compiler_params=pltpu.CompilerParams(vmem_limit_bytes=60 * 1024 * 1024),
    )(wgrad, vgrad, sgrad, div)
    return (wgrad, vgrad, sgrad, div.reshape(ROWS))


def solution(mesh):
    in_specs = (
        P("row", None),
        P("member", "row", None),
        P("row"),
        P("member", "row", None),
        P("member", None),
    )
    out_specs = (P("member", "row", None), P("member", None), P("member", "row", None), P("row"))
    return jax.shard_map(body, mesh=mesh, in_specs=in_specs, out_specs=out_specs, check_vma=False)
```

```python
import jax
import jax.numpy as jnp
from jax import lax
from jax.experimental import pallas as pl
from jax.experimental.pallas import tpu as pltpu
from jax.sharding import PartitionSpec as P

EPS = 1e-06
ETA = 5.0
MESH = pl.DeviceIdType.MESH
F32 = jnp.float32
BF16 = jnp.bfloat16

ACT = 1024
HID = 4096
ROWS = 256
LOCAL = 2
MEMBER_DEV = 8
PAIRS = 16 * 15
WIDTH = 256
PER_MEMBER = HID // WIDTH
BLOCKS = LOCAL * PER_MEMBER
PIECE = ROWS // MEMBER_DEV
GROUP = 8
HALF_PIECE = PIECE // 2
HALF = ROWS // 2

GATHER_KINDS = "BABAABBBAAABBAAABABBAABAABBAAABA"
SCATTER_KINDS = "AAABABABAAABABBBAAAAAABABBAABBAB"
GATHER_STEPS = (
    "3023233011001000312011220000000100000000000000000000",
    "0000112201300220000102110110210210221000000000000000",
    "0000000120031001310100100021030201031103000100000000",
    "0000000000000212011011000030101002102211011211120000",
)
GATHER_LEAD = 20
SCATTER_STEPS = (
    "00001130111120111003021022100111011100100000",
    "00000011100202021102000023010200001010201100",
    "00000000000201011000112030000000110012212000",
    "00000000000000000000000001010000200002330010",
)
PER_WORD = 13


def is_a(kinds, block):
    low, high = [
        sum((letter == "A") << pos for pos, letter in enumerate(part)) for part in (kinds[:16], kinds[16:])
    ]
    return lax.rem(lax.shift_right_logical(jnp.where(block < 16, low, high), lax.rem(block, 16)), 2) == 1


def count_at(digits, t):
    words = [
        sum(int(digit) << (2 * pos) for pos, digit in enumerate(digits[start : start + PER_WORD]))
        for start in range(0, len(digits), PER_WORD)
    ]
    word = jnp.int32(words[0])
    for pos in range(1, len(words)):
        word = jnp.where(t // PER_WORD == pos, words[pos], word)
    return lax.rem(lax.shift_right_logical(word, 2 * lax.rem(t, PER_WORD)), 4)


def run_steps(steps, counts, done):
    after = []
    for step, count, first in zip(steps, counts, done):
        def one(b, carry, step=step):
            step(b)
            return carry

        lax.fori_loop(first, first + count, one, 0)
        after.append(first + count)
    return tuple(after)


def wait_for(ref, sem):
    pltpu.make_async_copy(ref, ref, sem).wait()


def fold(value):
    out = value[:, 0:128]
    for pos in range(128, value.shape[1], 128):
        out = out + value[:, pos : pos + 128]
    return out


def wide(value, width):
    return jnp.concatenate([value] * (width // 128), axis=1)


def kernel(
    action_ref, state_hbm, target_ref, weight_hbm, value_ref,
    wgrad_ref, vgrad_ref, state, div_ref,
    wbuf, hidden, slope, curve, grad, unit_b, cot, lhs, rhs, core_in, ring_in,
    piece_out, piece_in, total, square_out, square_in, value_w, q_acc, resid, rnorm, vsum, vin,
    load_sem, state_sem, link_done, sib_done, core_done, ring_done,
    x_sem, y_sem, second_sem, sib_sem,
    misc_sem,
):
    member = lax.axis_index("member")
    row = lax.axis_index("row")
    yhi = row // 8
    xpos = lax.rem(row // 2, 4)
    core = lax.rem(row, 2)
    oyhi = 1 - yhi
    ocore = 1 - core

    def at_row(yy, xx, cc):
        return (member, yy * 8 + xx * 2 + cc)

    sibling = at_row(yhi, xpos, ocore)
    across = at_row(oyhi, xpos, core)
    xright, xfar, xleft = [lax.rem(xpos + d, 4) for d in (1, 2, 3)]
    right = at_row(yhi, xright, core)
    left = at_row(yhi, xleft, core)
    pair_first = at_row(yhi, xpos + 1 - 2 * lax.rem(xpos, 2), core)
    pair_second = at_row(yhi, 3 - xpos, core)
    low, high = pl.ds(0, 32), pl.ds(32, 32)
    peers = [lax.rem(member + d, MEMBER_DEV) for d in range(1, MEMBER_DEV)]

    def send(src, dst, done, arrived, dev):
        pltpu.make_async_remote_copy(
            src_ref=src, dst_ref=dst, send_sem=done, recv_sem=arrived, device_id=dev, device_id_type=MESH
        ).start()

    core_sem, ring_sem, mid_sem, last_sem = sib_sem, x_sem, second_sem, y_sem

    barrier = pltpu.get_barrier_semaphore()
    everyone = [sibling, across, right, left] + [(peer, row) for peer in peers]
    for dev in everyone:
        pl.semaphore_signal(barrier, inc=1, device_id=dev, device_id_type=MESH)

    def columns(block):
        return pl.ds(pl.multiple_of(lax.rem(block, PER_MEMBER) * WIDTH, WIDTH), WIDTH)

    def load_block(block, carry):
        m = block // PER_MEMBER
        pltpu.make_async_copy(
            weight_hbm.at[m, :, columns(block)], wbuf.at[block, yhi, xpos, core], load_sem.at[block // GROUP]
        ).start()
        return carry

    lax.fori_loop(0, BLOCKS, load_block, 0)

    def load_state(block, carry):
        m = block // PER_MEMBER
        pltpu.make_async_copy(
            state_hbm.at[m, :, columns(block)], state.at[block], state_sem.at[block // GROUP]
        ).start()
        return carry

    lax.fori_loop(0, BLOCKS, load_state, 0)

    for m in range(LOCAL):
        row_w = value_ref[m : m + 1, :].astype(F32)
        for pos in range(PER_MEMBER):
            value_w[m * PER_MEMBER + pos] = row_w[:, pos * WIDTH : (pos + 1) * WIDTH]
    grad[...] = jnp.zeros_like(grad)
    q_acc[...] = jnp.zeros_like(q_acc)
    for half in range(2):
        part = action_ref[half * 128 : (half + 1) * 128, :].astype(F32)
        turned = jnp.transpose(part).astype(BF16)
        for m in range(LOCAL):
            lhs[m, :, half * ROWS : half * ROWS + HALF] = turned

    pl.semaphore_wait(barrier, len(everyone))

    def first_send(b):
        own = wbuf.at[b, yhi, xpos, core]

        @pl.when(lax.rem(b, GROUP) == 0)
        def _():
            wait_for(wbuf.at[pl.ds(b, GROUP), yhi, xpos, core], load_sem.at[b // GROUP])

        kind_a = is_a(GATHER_KINDS, b)

        @pl.when(kind_a)
        def _():
            send(own, own, link_done, y_sem.at[b], across)

        @pl.when(jnp.logical_not(kind_a))
        def _():
            send(own, own, link_done, x_sem.at[b], right)
            send(own, own, link_done, x_sem.at[b], left)

    def second_hop(b):
        kind_a = is_a(GATHER_KINDS, b)

        @pl.when(kind_a)
        def _():
            wait_for(wbuf.at[b, oyhi, xpos, core], y_sem.at[b])
            both = wbuf.at[b, :, xpos, core]
            send(both, both, link_done, x_sem.at[b], right)
            send(both, both, link_done, x_sem.at[b], left)

        @pl.when(jnp.logical_not(kind_a))
        def _():
            wait_for(wbuf.at[b, yhi, pl.ds(0, 2), core], x_sem.at[b])
            one = wbuf.at[b, yhi, xleft, core, low]
            send(one, one, link_done, second_sem.at[b], right)
            two = wbuf.at[b, yhi, xright, core, high]
            send(two, two, link_done, second_sem.at[b], left)

    def third_hop(b):
        kind_a = is_a(GATHER_KINDS, b)

        @pl.when(kind_a)
        def _():
            wait_for(wbuf.at[b, :, pl.ds(0, 2), core], x_sem.at[b])
            one = wbuf.at[b, :, xleft, core, low]
            send(one, one, link_done, second_sem.at[b], right)
            two = wbuf.at[b, :, xright, core, high]
            send(two, two, link_done, second_sem.at[b], left)

        @pl.when(jnp.logical_not(kind_a))
        def _():
            wait_for(wbuf.at[b, yhi, xfar, core], second_sem.at[b])
            mine = wbuf.at[b, yhi, :, core]
            send(mine, mine, link_done, y_sem.at[b], across)
            send(mine, mine, sib_done, sib_sem.at[b], sibling)

    def to_sibling(b):
        kind_a = is_a(GATHER_KINDS, b)

        @pl.when(kind_a)
        def _():
            wait_for(wbuf.at[b, :, xfar, core], second_sem.at[b])
            full = wbuf.at[b, :, :, core]
            send(full, full, sib_done, sib_sem.at[b], sibling)

        @pl.when(jnp.logical_not(kind_a))
        def _():
            theirs = wbuf.at[b, oyhi, :, core]
            wait_for(theirs, y_sem.at[b])
            send(theirs, theirs, sib_done, sib_sem.at[b], sibling)

    def arrive(b):
        @pl.when(lax.rem(b, GROUP) == 0)
        def _():
            wait_for(state.at[pl.ds(b, GROUP)], state_sem.at[b // GROUP])

        wait_for(wbuf.at[b, :, :, ocore], sib_sem.at[b])

    def forward_product(b):
        return jnp.dot(action_ref[...], wbuf[b].reshape(ACT, WIDTH), preferred_element_type=F32)

    def forward_elementwise(b, product):
        m = b // PER_MEMBER
        vw = value_w[b]
        step = 64
        for pos in range(0, ROWS, step):
            rows = slice(pos, pos + step)
            p = state[b, rows, :].astype(F32) + product[rows, :]
            sig = 0.5 + 0.5 * jnp.tanh(0.5 * p)
            rest = 1.0 - sig
            hid = p * sig
            first = sig + hid * rest
            state[b, rows, :] = (first * vw).astype(BF16)
            slope[b, rows, :] = first.astype(BF16)
            curve[b, rows, :] = (sig * rest * (2.0 + p * (rest - sig)) * vw).astype(BF16)
            hidden[b, rows, :] = hid.astype(BF16)
            q_acc[m, rows, :] += fold(hid * vw)

    def gradient_product(b):
        grad[b // PER_MEMBER] += lax.dot_general(
            state[b], wbuf[b].reshape(ACT, WIDTH), (((1,), (1,)), ((), ())), preferred_element_type=F32
        )

    def compute_forward(t):
        @pl.when(t == 0)
        def _():
            arrive(t)
            forward_elementwise(t, forward_product(t))

        @pl.when(t > 0)
        def _():
            arrive(t)
            product = forward_product(t)
            gradient_product(t - 1)
            forward_elementwise(t, product)

        @pl.when(t == BLOCKS - 1)
        def _():
            gradient_product(t)

    def forward_round(i, done):
        counts = [count_at(digits, i) for digits in GATHER_STEPS]
        done = run_steps((first_send, second_hop, third_hop, to_sibling), counts, done)

        @pl.when(i >= GATHER_LEAD)
        def _():
            compute_forward(i - GATHER_LEAD)

        return done

    zero = jnp.int32(0)
    lax.fori_loop(0, BLOCKS + GATHER_LEAD, forward_round, (zero, zero, zero, zero))

    def make_piece(k, half):
        rows = pl.ds(pl.multiple_of(k * PIECE + half * HALF_PIECE, HALF_PIECE), HALF_PIECE)
        both = []
        squares = None
        for m in range(LOCAL):
            g = grad[m, rows, :]
            inv = 1.0 / jnp.sqrt(jnp.sum(g * g, axis=-1, keepdims=True) + EPS)
            u = g * inv
            ub = u.astype(BF16)
            grad[m, rows, :] = u
            unit_b[m, rows, :] = ub
            rnorm[m, rows, :] = jnp.broadcast_to(inv, (HALF_PIECE, 128))
            uf = ub.astype(F32)
            both.append(uf)
            sq = fold(uf * uf)
            squares = sq if squares is None else squares + sq
        square_out[rows, :] = squares
        return (both[0] + both[1]).astype(BF16)

    for half in range(2):
        rows = pl.ds(half * HALF_PIECE, HALF_PIECE)
        for peer in peers:
            piece_out[peer, rows] = make_piece(peer, half)
            send(
                piece_out.at[peer, rows], piece_in.at[member, rows],
                misc_sem.at[0], misc_sem.at[14 + half], (peer, row),
            )
        piece_in[member, rows] = make_piece(member, half)

    target_rows = jnp.transpose(jnp.broadcast_to(target_ref[...], (128, ROWS)))
    for m in range(LOCAL):
        q = jnp.sum(q_acc[m], axis=-1, keepdims=True)
        resid[m] = q - target_rows

    for half in range(2):
        rows = pl.ds(half * HALF_PIECE, HALF_PIECE)
        wait_for(piece_in.at[pl.ds(0, MEMBER_DEV - 1), rows], misc_sem.at[14 + half])
        acc = piece_in[0, rows].astype(F32)
        for k in range(1, MEMBER_DEV):
            acc = acc + piece_in[k, rows].astype(F32)
        mine = pl.ds(pl.multiple_of(member * PIECE + half * HALF_PIECE, HALF_PIECE), HALF_PIECE)
        total[mine, :] = acc.astype(BF16)
        for peer in peers:
            send(total.at[mine], total.at[mine], misc_sem.at[2], misc_sem.at[3], (peer, row))
    square_lane = jnp.sum(jnp.transpose(square_out[...]), axis=0, keepdims=True)
    square_in[member] = jnp.broadcast_to(square_lane, (8, ROWS))
    for peer in peers:
        send(square_in.at[member], square_in.at[member], misc_sem.at[4], misc_sem.at[5], (peer, row))
    wait_for(total.at[pl.ds(0, PIECE * (MEMBER_DEV - 1))], misc_sem.at[3])

    def make_cot(m):
        step = 64
        for pos in range(0, ROWS, step):
            u = grad[m, pos : pos + step, :]
            d = (2.0 * ETA / PAIRS) * (
                total[pos : pos + step, :].astype(F32) - unit_b[m, pos : pos + step, :].astype(F32)
            )
            along = jnp.sum(u * d, axis=-1, keepdims=True)
            c = (d - u * along) * wide(rnorm[m, pos : pos + step, :], ACT)
            cot[m, pos : pos + step, :] = c.astype(BF16)

    def place_cot(m):
        for half in range(2):
            part = cot[m, half * 128 : (half + 1) * 128, :].astype(F32)
            lhs[m, :, half * ROWS + HALF : (half + 1) * ROWS] = jnp.transpose(part).astype(BF16)

    make_cot(0)
    place_cot(0)
    wait_for(ring_in, link_done)
    wait_for(core_in, sib_done)

    def back_product(b):
        return jnp.dot(cot[b // PER_MEMBER], wbuf[b].reshape(ACT, WIDTH), preferred_element_type=F32)

    def partial_product(b):
        m = b // PER_MEMBER
        slot = lax.rem(b, 2)
        for q in range(4):
            some = slice(q * 256, (q + 1) * 256)
            part = jnp.dot(lhs[m, some, 0:ROWS], rhs[slot, 0:ROWS, :], preferred_element_type=F32)
            part = part + jnp.dot(
                lhs[m, some, ROWS : 2 * ROWS], rhs[slot, ROWS : 2 * ROWS, :], preferred_element_type=F32
            )
            wbuf[b, q // 2, 2 * (q % 2) : 2 * (q % 2) + 2] = part.astype(BF16).reshape(2, 2, 64, WIDTH)

    def elementwise(b, back_all):
        m = b // PER_MEMBER
        slot = lax.rem(b, 2)
        vacc = jnp.zeros((1, WIDTH), F32)
        step = 64
        for pos in range(0, ROWS, step):
            rows = slice(pos, pos + step)
            at = pos + (pos // HALF) * HALF
            back = back_all[rows, :]
            res = wide(resid[m, rows, :], WIDTH)
            tangent = state[b, rows, :]
            dpre = (tangent.astype(F32) * res + curve[b, rows, :].astype(F32) * back).astype(BF16)
            vacc = vacc + jnp.sum(
                hidden[b, rows, :].astype(F32) * res + slope[b, rows, :].astype(F32) * back, axis=0, keepdims=True
            )
            rhs[slot, at : at + step, :] = dpre
            rhs[slot, at + HALF : at + HALF + step, :] = tangent
            state[b, rows, :] = dpre
        vsum[b] = vacc

    def first_send_back(b):
        send(wbuf.at[b, :, :, ocore], core_in.at[b], core_done, core_sem.at[b], sibling)

    def compute_backward(t):
        @pl.when(t == 0)
        def _():
            elementwise(t, back_product(t))

        @pl.when(jnp.logical_and(t > 0, t < BLOCKS))
        def _():
            back_all = back_product(t)
            partial_product(t - 1)
            elementwise(t, back_all)
            first_send_back(t - 1)

        @pl.when(t == BLOCKS)
        def _():
            partial_product(t - 1)
            first_send_back(t - 1)

    def second_send(b):
        wait_for(core_in.at[b], core_sem.at[b])
        for yy in range(2):
            for xx in range(4):
                wbuf[b, yy, xx, core] = (
                    wbuf[b, yy, xx, core].astype(F32) + core_in[b, yy, xx].astype(F32)
                ).astype(BF16)
        kind_a = is_a(SCATTER_KINDS, b)

        @pl.when(kind_a)
        def _():
            send(wbuf.at[b, :, xfar, core, low], ring_in.at[b, pl.ds(0, 2), low], ring_done, ring_sem.at[b], right)
            send(wbuf.at[b, :, xfar, core, high], ring_in.at[b, pl.ds(0, 2), high], ring_done, ring_sem.at[b], left)

        @pl.when(jnp.logical_not(kind_a))
        def _():
            send(wbuf.at[b, oyhi, :, core], ring_in.at[b, pl.ds(0, 4)], ring_done, ring_sem.at[b], across)

    def add_in(b, yy, xx, parts):
        s = wbuf[b, yy, xx, core].astype(F32)
        for part in parts:
            s = s + ring_in[b, part].astype(F32)
        wbuf[b, yy, xx, core] = s.astype(BF16)

    def add_half(b, yy, xx, part, rows):
        wbuf[b, yy, xx, core, rows] = (
            wbuf[b, yy, xx, core, rows].astype(F32) + ring_in[b, part, rows].astype(F32)
        ).astype(BF16)

    def third_send(b):
        kind_a = is_a(SCATTER_KINDS, b)

        @pl.when(kind_a)
        def _():
            wait_for(ring_in.at[b, pl.ds(0, 2)], ring_sem.at[b])
            for yy in range(2):
                add_half(b, yy, xright, yy, low)
                add_half(b, yy, xleft, yy, high)
            send(wbuf.at[b, :, xright, core], ring_in.at[b, pl.ds(2, 2)], ring_done, mid_sem.at[b], right)
            send(wbuf.at[b, :, xleft, core], ring_in.at[b, pl.ds(4, 2)], ring_done, mid_sem.at[b], left)

        @pl.when(jnp.logical_not(kind_a))
        def _():
            wait_for(ring_in.at[b, pl.ds(0, 4)], ring_sem.at[b])
            for xx in range(4):
                add_in(b, yhi, xx, [xx])
            send(wbuf.at[b, yhi, xfar, core, low], ring_in.at[b, 4, low], ring_done, mid_sem.at[b], right)
            send(wbuf.at[b, yhi, xfar, core, high], ring_in.at[b, 4, high], ring_done, mid_sem.at[b], left)

    def last_send(b):
        kind_a = is_a(SCATTER_KINDS, b)

        @pl.when(kind_a)
        def _():
            wait_for(ring_in.at[b, pl.ds(2, 4)], mid_sem.at[b])
            for yy in range(2):
                add_in(b, yy, xpos, [2 + yy, 4 + yy])
            send(wbuf.at[b, oyhi, xpos, core], ring_in.at[b, 6], ring_done, last_sem.at[b], across)

        @pl.when(jnp.logical_not(kind_a))
        def _():
            wait_for(ring_in.at[b, 4], mid_sem.at[b])
            add_half(b, yhi, xright, 4, low)
            add_half(b, yhi, xleft, 4, high)
            send(wbuf.at[b, yhi, xright, core], ring_in.at[b, 5], ring_done, last_sem.at[b], right)
            send(wbuf.at[b, yhi, xleft, core], ring_in.at[b, 6], ring_done, last_sem.at[b], left)

    def finish(b):
        kind_a = is_a(SCATTER_KINDS, b)

        def store(parts):
            out = wbuf[b, yhi, xpos, core].astype(F32)
            for part in parts:
                out = out + ring_in[b, part].astype(F32)
            wgrad_ref[b] = out.astype(BF16)

        @pl.when(kind_a)
        def _():
            wait_for(ring_in.at[b, 6], last_sem.at[b])
            store([6])

        @pl.when(jnp.logical_not(kind_a))
        def _():
            wait_for(ring_in.at[b, pl.ds(5, 2)], last_sem.at[b])
            store([5, 6])

    rounds = len(SCATTER_STEPS[0])

    def backward_round(t, done):
        @pl.when(t == PER_MEMBER - 2)
        def _():
            make_cot(1)
            place_cot(1)

        compute_backward(t)

        @pl.when(t == BLOCKS + 1)
        def _():
            send(vsum, vin.at[0], misc_sem.at[6], misc_sem.at[7], sibling)

        @pl.when(t == BLOCKS + 4)
        def _():
            wait_for(vsum, misc_sem.at[6])
            wait_for(vin.at[0], misc_sem.at[7])
            vin[1] = vsum[...] + vin[0]
            send(vin.at[1], vin.at[2], misc_sem.at[8], misc_sem.at[9], across)

        @pl.when(t == BLOCKS + 7)
        def _():
            wait_for(vin.at[2], misc_sem.at[9])
            vin[3] = vin[1] + vin[2]
            send(vin.at[3], vin.at[4], misc_sem.at[10], misc_sem.at[11], pair_first)

        @pl.when(t == rounds - 1)
        def _():
            wait_for(vin.at[4], misc_sem.at[11])
            vin[5] = vin[3] + vin[4]
            send(vin.at[5], vin.at[6], misc_sem.at[12], misc_sem.at[13], pair_second)

        counts = [
            jnp.where(t == rounds - 1, BLOCKS - first, count_at(digits, t))
            for digits, first in zip(SCATTER_STEPS, done)
        ]
        return run_steps((second_send, third_send, last_send, finish), counts, done)

    lax.fori_loop(0, rounds, backward_round, (zero, zero, zero, zero))

    wait_for(square_in.at[pl.ds(0, MEMBER_DEV - 1)], misc_sem.at[5])
    tsq = []
    for pos in range(0, ROWS, 64):
        tf = total[pos : pos + 64, :].astype(F32)
        tsq.append(fold(tf * tf))
    cross_sum = jnp.sum(jnp.transpose(jnp.concatenate(tsq, axis=0)), axis=0, keepdims=True)
    squares = square_in[0]
    for k in range(1, MEMBER_DEV):
        squares = squares + square_in[k]
    div_ref[...] = (cross_sum - squares[0:1, :]) * (1.0 / PAIRS)

    wait_for(vin.at[6], misc_sem.at[13])
    for b in range(BLOCKS):
        m, pos = b // PER_MEMBER, b % PER_MEMBER
        vgrad_ref[m : m + 1, pos * WIDTH : (pos + 1) * WIDTH] = vin[5, b] + vin[6, b]

    wait_for(piece_out.at[pl.ds(0, MEMBER_DEV - 1)], misc_sem.at[0])
    wait_for(total.at[pl.ds(0, PIECE * (MEMBER_DEV - 1))], misc_sem.at[2])
    wait_for(square_in.at[pl.ds(0, MEMBER_DEV - 1)], misc_sem.at[4])
    for pos in (8, 10, 12):
        wait_for(vin.at[0], misc_sem.at[pos])

    wait_for(core_in, core_done)
    wait_for(ring_in, ring_done)


def hand_out(wgrad, vgrad, sgrad, div, wgrad_out, vgrad_out, sgrad_out, div_out, sem):
    for b in range(BLOCKS):
        m, pos = b // PER_MEMBER, b % PER_MEMBER
        cols = pl.ds(pos * WIDTH, WIDTH)
        pltpu.make_async_copy(sgrad.at[b], sgrad_out.at[m, :, cols], sem.at[0]).start()
        pltpu.make_async_copy(wgrad.at[b], wgrad_out.at[m, :, cols], sem.at[1]).start()
    small = [
        pltpu.make_async_copy(vgrad, vgrad_out, sem.at[2]),
        pltpu.make_async_copy(div, div_out, sem.at[3]),
    ]
    for one in small:
        one.start()
    for one in small:
        one.wait()
    wait_for(wgrad, sem.at[1])
    wait_for(sgrad, sem.at[0])


def body(action, state_term, target, weight_a, value_w):
    any_spec = pl.BlockSpec(memory_space=pl.ANY)
    vmem_spec = pl.BlockSpec(memory_space=pltpu.VMEM)
    dma = pltpu.SemaphoreType.DMA
    wgrad, vgrad, sgrad, div = pl.pallas_call(
        kernel,
        out_shape=(
            pltpu.VMEM((BLOCKS, 64, WIDTH), BF16),
            pltpu.VMEM((LOCAL, HID), F32),
            pltpu.VMEM((BLOCKS, ROWS, WIDTH), BF16),
            pltpu.VMEM((1, ROWS), F32),
        ),
        in_specs=[vmem_spec, any_spec, vmem_spec, any_spec, vmem_spec],
        out_specs=(vmem_spec,) * 4,
        scratch_shapes=[
            pltpu.VMEM((BLOCKS, 2, 4, 2, 64, WIDTH), BF16),
            pltpu.VMEM((BLOCKS, ROWS, WIDTH), BF16),
            pltpu.VMEM((BLOCKS, ROWS, WIDTH), BF16),
            pltpu.VMEM((BLOCKS, ROWS, WIDTH), BF16),
            pltpu.VMEM((LOCAL, ROWS, ACT), F32),
            pltpu.VMEM((LOCAL, ROWS, ACT), BF16),
            pltpu.VMEM((LOCAL, ROWS, ACT), BF16),
            pltpu.VMEM((LOCAL, ACT, 2 * ROWS), BF16),
            pltpu.VMEM((2, 2 * ROWS, WIDTH), BF16),
            pltpu.VMEM((BLOCKS, 2, 4, 64, WIDTH), BF16),
            pltpu.VMEM((BLOCKS, 7, 64, WIDTH), BF16),
            pltpu.VMEM((MEMBER_DEV, PIECE, ACT), BF16),
            pltpu.VMEM((MEMBER_DEV, PIECE, ACT), BF16),
            pltpu.VMEM((ROWS, ACT), BF16),
            pltpu.VMEM((ROWS, 128), F32),
            pltpu.VMEM((MEMBER_DEV, 8, ROWS), F32),
            pltpu.VMEM((BLOCKS, 1, WIDTH), F32),
            pltpu.VMEM((LOCAL, ROWS, 128), F32),
            pltpu.VMEM((LOCAL, ROWS, 128), F32),
            pltpu.VMEM((LOCAL, ROWS, 128), F32),
            pltpu.VMEM((BLOCKS, 1, WIDTH), F32),
            pltpu.VMEM((7, BLOCKS, 1, WIDTH), F32),
        ]
        + [dma((BLOCKS // GROUP,)) for _ in range(2)]
        + [dma for _ in range(4)]
        + [dma((BLOCKS,)) for _ in range(4)]
        + [dma((16,))],
        compiler_params=pltpu.CompilerParams(
            collective_id=1, has_side_effects=True, vmem_limit_bytes=56 * 1024 * 1024
        ),
    )(action, state_term, target.reshape(1, ROWS), weight_a, value_w)
    wgrad, vgrad, sgrad, div = pl.pallas_call(
        hand_out,
        out_shape=(
            jax.ShapeDtypeStruct((LOCAL, 64, HID), BF16),
            jax.ShapeDtypeStruct((LOCAL, HID), F32),
            jax.ShapeDtypeStruct((LOCAL, ROWS, HID), BF16),
            jax.ShapeDtypeStruct((1, ROWS), F32),
        ),
        in_specs=[any_spec] * 4,
        out_specs=(any_spec,) * 4,
        scratch_shapes=[dma((4,))],
        compiler_params=pltpu.CompilerParams(vmem_limit_bytes=1024 * 1024),
    )(wgrad, vgrad, sgrad, div)
    return (wgrad, vgrad, sgrad, div.reshape(ROWS))


def solution(mesh):
    in_specs = (
        P("row", None),
        P("member", "row", None),
        P("row"),
        P("member", "row", None),
        P("member", None),
    )
    out_specs = (P("member", "row", None), P("member", None), P("member", "row", None), P("row"))
    return jax.shard_map(body, mesh=mesh, in_specs=in_specs, out_specs=out_specs, check_vma=False)
```

```python
import jax
import jax.numpy as jnp
from jax import lax
from jax.experimental import pallas as pl
from jax.experimental.pallas import tpu as pltpu
from jax.sharding import PartitionSpec as P

EPS = 1e-06
ETA = 5.0
MESH = pl.DeviceIdType.MESH
F32 = jnp.float32
BF16 = jnp.bfloat16

ACT = 1024
HID = 4096
ROWS = 256
LOCAL = 2
MEMBER_DEV = 8
PAIRS = 16 * 15
WIDTH = 256
PER_MEMBER = HID // WIDTH
BLOCKS = LOCAL * PER_MEMBER
PIECE = ROWS // MEMBER_DEV
GROUP = 8
HALF_PIECE = PIECE // 2
HALF = ROWS // 2

GATHER_KINDS = "BABAABBBAAABBAAABABBAABAABBAAABA"
SCATTER_KINDS = "ABABAABABBAABAABBAAAABBABABAABAB"
GATHER_STEPS = (
    "3023233011001000312011220000000100000000000000000000",
    "0000112201300220000102110110210210221000000000000000",
    "0000000120031001310100100021030201031103000100000000",
    "0000000000000212011011000030101002102211011211120000",
)
GATHER_LEAD = 20
SCATTER_STEPS = (
    "00002021021102201031101201110112010110000000",
    "00000001020300210302002301100020100210020010",
    "00000000000012103011203001000100000003000020",
    "00000000000000010010010100010000101200120210",
)
PER_WORD = 13


def is_a(kinds, block):
    low, high = [
        sum((letter == "A") << pos for pos, letter in enumerate(part)) for part in (kinds[:16], kinds[16:])
    ]
    return lax.rem(lax.shift_right_logical(jnp.where(block < 16, low, high), lax.rem(block, 16)), 2) == 1


def count_at(digits, t):
    words = [
        sum(int(digit) << (2 * pos) for pos, digit in enumerate(digits[start : start + PER_WORD]))
        for start in range(0, len(digits), PER_WORD)
    ]
    word = jnp.int32(words[0])
    for pos in range(1, len(words)):
        word = jnp.where(t // PER_WORD == pos, words[pos], word)
    return lax.rem(lax.shift_right_logical(word, 2 * lax.rem(t, PER_WORD)), 4)


def run_steps(steps, counts, done):
    after = []
    for step, count, first in zip(steps, counts, done):
        def one(b, carry, step=step):
            step(b)
            return carry

        lax.fori_loop(first, first + count, one, 0)
        after.append(first + count)
    return tuple(after)


def wait_for(ref, sem):
    pltpu.make_async_copy(ref, ref, sem).wait()


def fold(value):
    out = value[:, 0:128]
    for pos in range(128, value.shape[1], 128):
        out = out + value[:, pos : pos + 128]
    return out


def wide(value, width):
    return jnp.concatenate([value] * (width // 128), axis=1)


def kernel(
    action_hbm, state_hbm, target_hbm, weight_hbm, value_hbm,
    wgrad_ref, vgrad_ref, state, div_ref,
    wbuf, hidden, slope, curve, grad, unit_b, cot, lhs, rhs, core_in, ring_in,
    piece_out, piece_in, total, square_out, square_in, value_w, q_acc, resid, rnorm, vsum, vin,
    load_sem, state_sem, link_done, sib_done, core_done, ring_done,
    x_sem, y_sem, second_sem, sib_sem,
    misc_sem, action_ref, target_ref, value_ref, small_sem,
):
    member = lax.axis_index("member")
    row = lax.axis_index("row")
    yhi = row // 8
    xpos = lax.rem(row // 2, 4)
    core = lax.rem(row, 2)
    oyhi = 1 - yhi
    ocore = 1 - core

    def at_row(yy, xx, cc):
        return (member, yy * 8 + xx * 2 + cc)

    sibling = at_row(yhi, xpos, ocore)
    across = at_row(oyhi, xpos, core)
    xright, xfar, xleft = [lax.rem(xpos + d, 4) for d in (1, 2, 3)]
    right = at_row(yhi, xright, core)
    left = at_row(yhi, xleft, core)
    pair_first = at_row(yhi, xpos + 1 - 2 * lax.rem(xpos, 2), core)
    pair_second = at_row(yhi, 3 - xpos, core)
    low, high = pl.ds(0, 32), pl.ds(32, 32)
    peers = [lax.rem(member + d, MEMBER_DEV) for d in range(1, MEMBER_DEV)]

    def send(src, dst, done, arrived, dev):
        pltpu.make_async_remote_copy(
            src_ref=src, dst_ref=dst, send_sem=done, recv_sem=arrived, device_id=dev, device_id_type=MESH
        ).start()

    core_sem, ring_sem, mid_sem, last_sem = sib_sem, x_sem, second_sem, y_sem

    barrier = pltpu.get_barrier_semaphore()
    everyone = [sibling, across, right, left] + [(peer, row) for peer in peers]
    for dev in everyone:
        pl.semaphore_signal(barrier, inc=1, device_id=dev, device_id_type=MESH)

    def columns(block):
        return pl.ds(pl.multiple_of(lax.rem(block, PER_MEMBER) * WIDTH, WIDTH), WIDTH)

    def load_block(block, carry):
        m = block // PER_MEMBER
        pltpu.make_async_copy(
            weight_hbm.at[m, :, columns(block)], wbuf.at[block, yhi, xpos, core], load_sem.at[block // GROUP]
        ).start()
        return carry

    lax.fori_loop(0, BLOCKS, load_block, 0)
    small_loads = [
        pltpu.make_async_copy(src, dst, small_sem.at[i])
        for i, (src, dst) in enumerate(((value_hbm, value_ref), (action_hbm, action_ref), (target_hbm, target_ref)))
    ]
    for load in small_loads:
        load.start()

    def load_state(block, carry):
        m = block // PER_MEMBER
        pltpu.make_async_copy(
            state_hbm.at[m, :, columns(block)], state.at[block], state_sem.at[block // GROUP]
        ).start()
        return carry

    lax.fori_loop(0, BLOCKS, load_state, 0)

    for load in small_loads:
        load.wait()
    for m in range(LOCAL):
        row_w = value_ref[m : m + 1, :].astype(F32)
        for pos in range(PER_MEMBER):
            value_w[m * PER_MEMBER + pos] = row_w[:, pos * WIDTH : (pos + 1) * WIDTH]
    grad[...] = jnp.zeros_like(grad)
    q_acc[...] = jnp.zeros_like(q_acc)
    for half in range(2):
        part = action_ref[half * 128 : (half + 1) * 128, :].astype(F32)
        turned = jnp.transpose(part).astype(BF16)
        for m in range(LOCAL):
            lhs[m, :, half * ROWS : half * ROWS + HALF] = turned

    pl.semaphore_wait(barrier, len(everyone))

    def first_send(b):
        own = wbuf.at[b, yhi, xpos, core]

        @pl.when(lax.rem(b, GROUP) == 0)
        def _():
            wait_for(wbuf.at[pl.ds(b, GROUP), yhi, xpos, core], load_sem.at[b // GROUP])

        kind_a = is_a(GATHER_KINDS, b)

        @pl.when(kind_a)
        def _():
            send(own, own, link_done, y_sem.at[b], across)

        @pl.when(jnp.logical_not(kind_a))
        def _():
            send(own, own, link_done, x_sem.at[b], right)
            send(own, own, link_done, x_sem.at[b], left)

    def second_hop(b):
        kind_a = is_a(GATHER_KINDS, b)

        @pl.when(kind_a)
        def _():
            wait_for(wbuf.at[b, oyhi, xpos, core], y_sem.at[b])
            both = wbuf.at[b, :, xpos, core]
            send(both, both, link_done, x_sem.at[b], right)
            send(both, both, link_done, x_sem.at[b], left)

        @pl.when(jnp.logical_not(kind_a))
        def _():
            wait_for(wbuf.at[b, yhi, pl.ds(0, 2), core], x_sem.at[b])
            one = wbuf.at[b, yhi, xleft, core, low]
            send(one, one, link_done, second_sem.at[b], right)
            two = wbuf.at[b, yhi, xright, core, high]
            send(two, two, link_done, second_sem.at[b], left)

    def third_hop(b):
        kind_a = is_a(GATHER_KINDS, b)

        @pl.when(kind_a)
        def _():
            wait_for(wbuf.at[b, :, pl.ds(0, 2), core], x_sem.at[b])

            @pl.when(b == BLOCKS - 1)
            def _():
                for xx in (xpos, xleft, xright):
                    early = wbuf.at[b, :, xx, core]
                    send(early, early, sib_done, sib_sem.at[b], sibling)

            one = wbuf.at[b, :, xleft, core, low]
            send(one, one, link_done, second_sem.at[b], right)
            two = wbuf.at[b, :, xright, core, high]
            send(two, two, link_done, second_sem.at[b], left)

        @pl.when(jnp.logical_not(kind_a))
        def _():
            wait_for(wbuf.at[b, yhi, xfar, core], second_sem.at[b])
            mine = wbuf.at[b, yhi, :, core]
            send(mine, mine, link_done, y_sem.at[b], across)
            send(mine, mine, sib_done, sib_sem.at[b], sibling)

    def to_sibling(b):
        kind_a = is_a(GATHER_KINDS, b)

        @pl.when(kind_a)
        def _():
            wait_for(wbuf.at[b, :, xfar, core], second_sem.at[b])

            @pl.when(b == BLOCKS - 1)
            def _():
                late = wbuf.at[b, :, xfar, core]
                send(late, late, sib_done, sib_sem.at[b], sibling)

            @pl.when(b < BLOCKS - 1)
            def _():
                full = wbuf.at[b, :, :, core]
                send(full, full, sib_done, sib_sem.at[b], sibling)

        @pl.when(jnp.logical_not(kind_a))
        def _():
            theirs = wbuf.at[b, oyhi, :, core]
            wait_for(theirs, y_sem.at[b])
            send(theirs, theirs, sib_done, sib_sem.at[b], sibling)

    def arrive(b):
        @pl.when(lax.rem(b, GROUP) == 0)
        def _():
            wait_for(state.at[pl.ds(b, GROUP)], state_sem.at[b // GROUP])

        wait_for(wbuf.at[b, :, :, ocore], sib_sem.at[b])

    def forward_product(b):
        return jnp.dot(action_ref[...], wbuf[b].reshape(ACT, WIDTH), preferred_element_type=F32)

    def forward_elementwise(b, product):
        m = b // PER_MEMBER
        vw = value_w[b]
        step = 64
        for pos in range(0, ROWS, step):
            rows = slice(pos, pos + step)
            p = state[b, rows, :].astype(F32) + product[rows, :]
            sig = 0.5 + 0.5 * jnp.tanh(0.5 * p)
            rest = 1.0 - sig
            hid = p * sig
            first = sig + hid * rest
            state[b, rows, :] = (first * vw).astype(BF16)
            slope[b, rows, :] = first.astype(BF16)
            curve[b, rows, :] = (sig * rest * (2.0 + p * (rest - sig)) * vw).astype(BF16)
            hidden[b, rows, :] = hid.astype(BF16)
            q_acc[m, rows, :] += fold(hid * vw)

    def gradient_product(b):
        grad[b // PER_MEMBER] += lax.dot_general(
            state[b], wbuf[b].reshape(ACT, WIDTH), (((1,), (1,)), ((), ())), preferred_element_type=F32
        )

    def compute_forward(t):
        @pl.when(t == 0)
        def _():
            arrive(t)
            forward_elementwise(t, forward_product(t))

        @pl.when(t > 0)
        def _():
            arrive(t)
            product = forward_product(t)
            gradient_product(t - 1)
            forward_elementwise(t, product)

        @pl.when(t == BLOCKS - 1)
        def _():
            gradient_product(t)

    def forward_round(i, done):
        counts = [count_at(digits, i) for digits in GATHER_STEPS]
        done = run_steps((first_send, second_hop, third_hop, to_sibling), counts, done)

        @pl.when(i >= GATHER_LEAD)
        def _():
            compute_forward(i - GATHER_LEAD)

        return done

    zero = jnp.int32(0)
    lax.fori_loop(0, BLOCKS + GATHER_LEAD, forward_round, (zero, zero, zero, zero))

    def make_piece(k, half):
        rows = pl.ds(pl.multiple_of(k * PIECE + half * HALF_PIECE, HALF_PIECE), HALF_PIECE)
        both = []
        squares = None
        for m in range(LOCAL):
            g = grad[m, rows, :]
            inv = 1.0 / jnp.sqrt(jnp.sum(g * g, axis=-1, keepdims=True) + EPS)
            u = g * inv
            ub = u.astype(BF16)
            grad[m, rows, :] = u
            unit_b[m, rows, :] = ub
            rnorm[m, rows, :] = jnp.broadcast_to(inv, (HALF_PIECE, 128))
            uf = ub.astype(F32)
            both.append(uf)
            sq = fold(uf * uf)
            squares = sq if squares is None else squares + sq
        square_out[rows, :] = squares
        return (both[0] + both[1]).astype(BF16)

    for half in range(2):
        rows = pl.ds(half * HALF_PIECE, HALF_PIECE)
        for peer in peers:
            piece_out[peer, rows] = make_piece(peer, half)
            send(
                piece_out.at[peer, rows], piece_in.at[member, rows],
                misc_sem.at[0], misc_sem.at[14 + half], (peer, row),
            )
        piece_in[member, rows] = make_piece(member, half)

    target_rows = jnp.transpose(jnp.broadcast_to(target_ref[...], (128, ROWS)))
    for m in range(LOCAL):
        q = jnp.sum(q_acc[m], axis=-1, keepdims=True)
        resid[m] = q - target_rows

    for half in range(2):
        rows = pl.ds(half * HALF_PIECE, HALF_PIECE)
        wait_for(piece_in.at[pl.ds(0, MEMBER_DEV - 1), rows], misc_sem.at[14 + half])
        acc = piece_in[0, rows].astype(F32)
        for k in range(1, MEMBER_DEV):
            acc = acc + piece_in[k, rows].astype(F32)
        mine = pl.ds(pl.multiple_of(member * PIECE + half * HALF_PIECE, HALF_PIECE), HALF_PIECE)
        total[mine, :] = acc.astype(BF16)
        for peer in peers:
            send(total.at[mine], total.at[mine], misc_sem.at[2], misc_sem.at[3], (peer, row))
    square_lane = jnp.sum(jnp.transpose(square_out[...]), axis=0, keepdims=True)
    square_in[member] = jnp.broadcast_to(square_lane, (8, ROWS))
    for peer in peers:
        send(square_in.at[member], square_in.at[member], misc_sem.at[4], misc_sem.at[5], (peer, row))
    wait_for(total.at[pl.ds(0, PIECE * (MEMBER_DEV - 1))], misc_sem.at[3])

    def make_cot(m):
        step = 64
        for pos in range(0, ROWS, step):
            u = grad[m, pos : pos + step, :]
            d = (2.0 * ETA / PAIRS) * (
                total[pos : pos + step, :].astype(F32) - unit_b[m, pos : pos + step, :].astype(F32)
            )
            along = jnp.sum(u * d, axis=-1, keepdims=True)
            c = (d - u * along) * wide(rnorm[m, pos : pos + step, :], ACT)
            cot[m, pos : pos + step, :] = c.astype(BF16)

    def place_cot(m):
        for half in range(2):
            part = cot[m, half * 128 : (half + 1) * 128, :].astype(F32)
            lhs[m, :, half * ROWS + HALF : (half + 1) * ROWS] = jnp.transpose(part).astype(BF16)

    make_cot(0)
    wait_for(ring_in, link_done)
    wait_for(core_in, sib_done)

    def back_product(b):
        return jnp.dot(cot[b // PER_MEMBER], wbuf[b].reshape(ACT, WIDTH), preferred_element_type=F32)

    def partial_product(b):
        m = b // PER_MEMBER
        slot = lax.rem(b, 2)
        for q in range(4):
            some = slice(q * 256, (q + 1) * 256)
            part = jnp.dot(lhs[m, some, 0:ROWS], rhs[slot, 0:ROWS, :], preferred_element_type=F32)
            part = part + jnp.dot(
                lhs[m, some, ROWS : 2 * ROWS], rhs[slot, ROWS : 2 * ROWS, :], preferred_element_type=F32
            )
            wbuf[b, q // 2, 2 * (q % 2) : 2 * (q % 2) + 2] = part.astype(BF16).reshape(2, 2, 64, WIDTH)

    def elementwise(b, back_all):
        m = b // PER_MEMBER
        slot = lax.rem(b, 2)
        vacc = jnp.zeros((1, WIDTH), F32)
        step = 64
        for pos in range(0, ROWS, step):
            rows = slice(pos, pos + step)
            at = pos + (pos // HALF) * HALF
            back = back_all[rows, :]
            res = wide(resid[m, rows, :], WIDTH)
            tangent = state[b, rows, :]
            dpre = (tangent.astype(F32) * res + curve[b, rows, :].astype(F32) * back).astype(BF16)
            vacc = vacc + jnp.sum(
                hidden[b, rows, :].astype(F32) * res + slope[b, rows, :].astype(F32) * back, axis=0, keepdims=True
            )
            rhs[slot, at : at + step, :] = dpre
            rhs[slot, at + HALF : at + HALF + step, :] = tangent
            state[b, rows, :] = dpre
        vsum[b] = vacc

    def first_send_back(b):
        send(wbuf.at[b, :, :, ocore], core_in.at[b], core_done, core_sem.at[b], sibling)

    def compute_backward(t):
        @pl.when(t == 0)
        def _():
            back_all = back_product(t)
            place_cot(0)
            elementwise(t, back_all)

        @pl.when(jnp.logical_and(t > 0, t < BLOCKS))
        def _():
            back_all = back_product(t)
            partial_product(t - 1)
            elementwise(t, back_all)
            first_send_back(t - 1)

        @pl.when(t == BLOCKS)
        def _():
            partial_product(t - 1)
            first_send_back(t - 1)

    def second_send(b):
        wait_for(core_in.at[b], core_sem.at[b])
        for yy in range(2):
            for xx in range(4):
                wbuf[b, yy, xx, core] = (
                    wbuf[b, yy, xx, core].astype(F32) + core_in[b, yy, xx].astype(F32)
                ).astype(BF16)
        kind_a = is_a(SCATTER_KINDS, b)

        @pl.when(kind_a)
        def _():
            send(wbuf.at[b, :, xfar, core, low], ring_in.at[b, pl.ds(0, 2), low], ring_done, ring_sem.at[b], right)
            send(wbuf.at[b, :, xfar, core, high], ring_in.at[b, pl.ds(0, 2), high], ring_done, ring_sem.at[b], left)

        @pl.when(jnp.logical_not(kind_a))
        def _():
            send(wbuf.at[b, oyhi, :, core], ring_in.at[b, pl.ds(0, 4)], ring_done, ring_sem.at[b], across)

    def add_in(b, yy, xx, parts):
        s = wbuf[b, yy, xx, core].astype(F32)
        for part in parts:
            s = s + ring_in[b, part].astype(F32)
        wbuf[b, yy, xx, core] = s.astype(BF16)

    def add_half(b, yy, xx, part, rows):
        wbuf[b, yy, xx, core, rows] = (
            wbuf[b, yy, xx, core, rows].astype(F32) + ring_in[b, part, rows].astype(F32)
        ).astype(BF16)

    def third_send(b):
        kind_a = is_a(SCATTER_KINDS, b)

        @pl.when(kind_a)
        def _():
            wait_for(ring_in.at[b, pl.ds(0, 2)], ring_sem.at[b])
            for yy in range(2):
                add_half(b, yy, xright, yy, low)
                add_half(b, yy, xleft, yy, high)
            send(wbuf.at[b, :, xright, core], ring_in.at[b, pl.ds(2, 2)], ring_done, mid_sem.at[b], right)
            send(wbuf.at[b, :, xleft, core], ring_in.at[b, pl.ds(4, 2)], ring_done, mid_sem.at[b], left)

        @pl.when(jnp.logical_not(kind_a))
        def _():
            wait_for(ring_in.at[b, pl.ds(0, 4)], ring_sem.at[b])
            for xx in range(4):
                add_in(b, yhi, xx, [xx])
            send(wbuf.at[b, yhi, xfar, core, low], ring_in.at[b, 4, low], ring_done, mid_sem.at[b], right)
            send(wbuf.at[b, yhi, xfar, core, high], ring_in.at[b, 4, high], ring_done, mid_sem.at[b], left)

    def last_send(b):
        kind_a = is_a(SCATTER_KINDS, b)

        @pl.when(kind_a)
        def _():
            wait_for(ring_in.at[b, pl.ds(2, 4)], mid_sem.at[b])
            for yy in range(2):
                add_in(b, yy, xpos, [2 + yy, 4 + yy])
            send(wbuf.at[b, oyhi, xpos, core], ring_in.at[b, 6], ring_done, last_sem.at[b], across)

        @pl.when(jnp.logical_not(kind_a))
        def _():
            wait_for(ring_in.at[b, 4], mid_sem.at[b])
            add_half(b, yhi, xright, 4, low)
            add_half(b, yhi, xleft, 4, high)
            send(wbuf.at[b, yhi, xright, core], ring_in.at[b, 5], ring_done, last_sem.at[b], right)
            send(wbuf.at[b, yhi, xleft, core], ring_in.at[b, 6], ring_done, last_sem.at[b], left)

    def finish(b):
        kind_a = is_a(SCATTER_KINDS, b)

        def store(parts):
            out = wbuf[b, yhi, xpos, core].astype(F32)
            for part in parts:
                out = out + ring_in[b, part].astype(F32)
            wgrad_ref[b] = out.astype(BF16)

        @pl.when(kind_a)
        def _():
            wait_for(ring_in.at[b, 6], last_sem.at[b])
            store([6])

        @pl.when(jnp.logical_not(kind_a))
        def _():
            wait_for(ring_in.at[b, pl.ds(5, 2)], last_sem.at[b])
            store([5, 6])

    rounds = len(SCATTER_STEPS[0])

    def diversity():
        wait_for(square_in.at[pl.ds(0, MEMBER_DEV - 1)], misc_sem.at[5])
        tsq = []
        for pos in range(0, ROWS, 64):
            tf = total[pos : pos + 64, :].astype(F32)
            tsq.append(fold(tf * tf))
        cross_sum = jnp.sum(jnp.transpose(jnp.concatenate(tsq, axis=0)), axis=0, keepdims=True)
        squares = square_in[0]
        for k in range(1, MEMBER_DEV):
            squares = squares + square_in[k]
        div_ref[...] = (cross_sum - squares[0:1, :]) * (1.0 / PAIRS)

    def backward_round(t, done):
        @pl.when(t == PER_MEMBER - 2)
        def _():
            make_cot(1)
            place_cot(1)

        compute_backward(t)

        @pl.when(t == BLOCKS - 2)
        def _():
            diversity()

        @pl.when(t == BLOCKS + 1)
        def _():
            send(vsum, vin.at[0], misc_sem.at[6], misc_sem.at[7], sibling)

        @pl.when(t == BLOCKS + 4)
        def _():
            wait_for(vsum, misc_sem.at[6])
            wait_for(vin.at[0], misc_sem.at[7])
            vin[1] = vsum[...] + vin[0]
            send(vin.at[1], vin.at[2], misc_sem.at[8], misc_sem.at[9], across)

        @pl.when(t == BLOCKS + 7)
        def _():
            wait_for(vin.at[2], misc_sem.at[9])
            vin[3] = vin[1] + vin[2]
            send(vin.at[3], vin.at[4], misc_sem.at[10], misc_sem.at[11], pair_first)

        @pl.when(t == rounds - 1)
        def _():
            wait_for(vin.at[4], misc_sem.at[11])
            vin[5] = vin[3] + vin[4]
            send(vin.at[5], vin.at[6], misc_sem.at[12], misc_sem.at[13], pair_second)

        counts = [
            jnp.where(t == rounds - 1, BLOCKS - first, count_at(digits, t))
            for digits, first in zip(SCATTER_STEPS, done)
        ]
        return run_steps((second_send, third_send, last_send, finish), counts, done)

    lax.fori_loop(0, rounds, backward_round, (zero, zero, zero, zero))

    wait_for(vin.at[6], misc_sem.at[13])
    for b in range(BLOCKS):
        m, pos = b // PER_MEMBER, b % PER_MEMBER
        vgrad_ref[m : m + 1, pos * WIDTH : (pos + 1) * WIDTH] = vin[5, b] + vin[6, b]

    wait_for(piece_out.at[pl.ds(0, MEMBER_DEV - 1)], misc_sem.at[0])
    wait_for(total.at[pl.ds(0, PIECE * (MEMBER_DEV - 1))], misc_sem.at[2])
    wait_for(square_in.at[pl.ds(0, MEMBER_DEV - 1)], misc_sem.at[4])
    for pos in (8, 10, 12):
        wait_for(vin.at[0], misc_sem.at[pos])

    wait_for(core_in, core_done)
    wait_for(ring_in, ring_done)


def hand_out(wgrad, vgrad, sgrad, div, wgrad_out, vgrad_out, sgrad_out, div_out, sem):
    for b in range(BLOCKS):
        m, pos = b // PER_MEMBER, b % PER_MEMBER
        cols = pl.ds(pos * WIDTH, WIDTH)
        pltpu.make_async_copy(sgrad.at[b], sgrad_out.at[m, :, cols], sem.at[0]).start()
        pltpu.make_async_copy(wgrad.at[b], wgrad_out.at[m, :, cols], sem.at[1]).start()
    small = [
        pltpu.make_async_copy(vgrad, vgrad_out, sem.at[2]),
        pltpu.make_async_copy(div, div_out, sem.at[3]),
    ]
    for one in small:
        one.start()
    for one in small:
        one.wait()
    wait_for(wgrad, sem.at[1])
    wait_for(sgrad, sem.at[0])


def body(action, state_term, target, weight_a, value_w):
    any_spec = pl.BlockSpec(memory_space=pl.ANY)
    vmem_spec = pl.BlockSpec(memory_space=pltpu.VMEM)
    dma = pltpu.SemaphoreType.DMA
    wgrad, vgrad, sgrad, div = pl.pallas_call(
        kernel,
        out_shape=(
            pltpu.VMEM((BLOCKS, 64, WIDTH), BF16),
            pltpu.VMEM((LOCAL, HID), F32),
            pltpu.VMEM((BLOCKS, ROWS, WIDTH), BF16),
            pltpu.VMEM((1, ROWS), F32),
        ),
        in_specs=[any_spec] * 5,
        out_specs=(vmem_spec,) * 4,
        scratch_shapes=[
            pltpu.VMEM((BLOCKS, 2, 4, 2, 64, WIDTH), BF16),
            pltpu.VMEM((BLOCKS, ROWS, WIDTH), BF16),
            pltpu.VMEM((BLOCKS, ROWS, WIDTH), BF16),
            pltpu.VMEM((BLOCKS, ROWS, WIDTH), BF16),
            pltpu.VMEM((LOCAL, ROWS, ACT), F32),
            pltpu.VMEM((LOCAL, ROWS, ACT), BF16),
            pltpu.VMEM((LOCAL, ROWS, ACT), BF16),
            pltpu.VMEM((LOCAL, ACT, 2 * ROWS), BF16),
            pltpu.VMEM((2, 2 * ROWS, WIDTH), BF16),
            pltpu.VMEM((BLOCKS, 2, 4, 64, WIDTH), BF16),
            pltpu.VMEM((BLOCKS, 7, 64, WIDTH), BF16),
            pltpu.VMEM((MEMBER_DEV, PIECE, ACT), BF16),
            pltpu.VMEM((MEMBER_DEV, PIECE, ACT), BF16),
            pltpu.VMEM((ROWS, ACT), BF16),
            pltpu.VMEM((ROWS, 128), F32),
            pltpu.VMEM((MEMBER_DEV, 8, ROWS), F32),
            pltpu.VMEM((BLOCKS, 1, WIDTH), F32),
            pltpu.VMEM((LOCAL, ROWS, 128), F32),
            pltpu.VMEM((LOCAL, ROWS, 128), F32),
            pltpu.VMEM((LOCAL, ROWS, 128), F32),
            pltpu.VMEM((BLOCKS, 1, WIDTH), F32),
            pltpu.VMEM((7, BLOCKS, 1, WIDTH), F32),
        ]
        + [dma((BLOCKS // GROUP,)) for _ in range(2)]
        + [dma for _ in range(4)]
        + [dma((BLOCKS,)) for _ in range(4)]
        + [dma((16,))]
        + [pltpu.VMEM((ROWS, ACT), BF16), pltpu.VMEM((1, ROWS), F32), pltpu.VMEM((LOCAL, HID), BF16), dma((3,))],
        compiler_params=pltpu.CompilerParams(
            collective_id=1, has_side_effects=True, vmem_limit_bytes=56 * 1024 * 1024
        ),
    )(action, state_term, target.reshape(1, ROWS), weight_a, value_w)
    wgrad, vgrad, sgrad, div = pl.pallas_call(
        hand_out,
        out_shape=(
            jax.ShapeDtypeStruct((LOCAL, 64, HID), BF16),
            jax.ShapeDtypeStruct((LOCAL, HID), F32),
            jax.ShapeDtypeStruct((LOCAL, ROWS, HID), BF16),
            jax.ShapeDtypeStruct((1, ROWS), F32),
        ),
        in_specs=[any_spec] * 4,
        out_specs=(any_spec,) * 4,
        scratch_shapes=[dma((4,))],
        compiler_params=pltpu.CompilerParams(vmem_limit_bytes=1024 * 1024),
    )(wgrad, vgrad, sgrad, div)
    return (wgrad, vgrad, sgrad, div.reshape(ROWS))


def solution(mesh):
    in_specs = (
        P("row", None),
        P("member", "row", None),
        P("row"),
        P("member", "row", None),
        P("member", None),
    )
    out_specs = (P("member", "row", None), P("member", None), P("member", "row", None), P("row"))
    return jax.shard_map(body, mesh=mesh, in_specs=in_specs, out_specs=out_specs, check_vma=False)
```

```python
import jax
import jax.numpy as jnp
from jax import lax
from jax.experimental import pallas as pl
from jax.experimental.pallas import tpu as pltpu
from jax.sharding import PartitionSpec as P

EPS = 1e-06
ETA = 5.0
MESH = pl.DeviceIdType.MESH
F32 = jnp.float32
BF16 = jnp.bfloat16

ACT = 1024
HID = 4096
ROWS = 256
LOCAL = 2
MEMBER_DEV = 8
PAIRS = 16 * 15
WIDTH = 256
PER_MEMBER = HID // WIDTH
BLOCKS = LOCAL * PER_MEMBER
PIECE = ROWS // MEMBER_DEV
GROUP = 8
HALF_PIECE = PIECE // 2
HALF = ROWS // 2

GATHER_KINDS = "BABAABBBAAABBAAABABBAABAABBAAABA"
SCATTER_KINDS = "ABABAABABBAABAABBAAAABBABABAABAB"
GATHER_STEPS = (
    "3023233011001000312011220000000100000000000000000000",
    "0000112201300220000102110110210210221000000000000000",
    "0000000120031001310100100021030201031103000100000000",
    "0000000000000212011011000030101002102211011211120000",
)
GATHER_LEAD = 20
SCATTER_STEPS = (
    "00002021021102201031101201110112010110000000000",
    "00000001020300210302002301100020100210020012000",
    "00000000000012103011203001000100000003000023200",
    "00000000000000010010010100010000101200120210000",
)
PER_WORD = 13


def is_a(kinds, block):
    low, high = [
        sum((letter == "A") << pos for pos, letter in enumerate(part)) for part in (kinds[:16], kinds[16:])
    ]
    return lax.rem(lax.shift_right_logical(jnp.where(block < 16, low, high), lax.rem(block, 16)), 2) == 1


def count_at(digits, t):
    words = [
        sum(int(digit) << (2 * pos) for pos, digit in enumerate(digits[start : start + PER_WORD]))
        for start in range(0, len(digits), PER_WORD)
    ]
    word = jnp.int32(words[0])
    for pos in range(1, len(words)):
        word = jnp.where(t // PER_WORD == pos, words[pos], word)
    return lax.rem(lax.shift_right_logical(word, 2 * lax.rem(t, PER_WORD)), 4)


def run_steps(steps, counts, done):
    after = []
    for step, count, first in zip(steps, counts, done):
        def one(b, carry, step=step):
            step(b)
            return carry

        lax.fori_loop(first, first + count, one, 0)
        after.append(first + count)
    return tuple(after)


def wait_for(ref, sem):
    pltpu.make_async_copy(ref, ref, sem).wait()


def fold(value):
    out = value[:, 0:128]
    for pos in range(128, value.shape[1], 128):
        out = out + value[:, pos : pos + 128]
    return out


def wide(value, width):
    return jnp.concatenate([value] * (width // 128), axis=1)


def kernel(
    action_hbm, state_hbm, target_hbm, weight_hbm, value_hbm,
    wgrad_ref, vgrad_ref, state, div_ref,
    wbuf, hidden, slope, curve, grad, unit_b, cot, lhs, rhs, core_in, ring_in,
    piece_out, piece_in, total, square_out, square_in, value_w, q_acc, resid, rnorm, vsum, vin,
    load_sem, state_sem, link_done, sib_done, core_done, ring_done,
    x_sem, y_sem, second_sem, sib_sem,
    misc_sem, action_ref, target_ref, value_ref, small_sem,
):
    member = lax.axis_index("member")
    row = lax.axis_index("row")
    yhi = row // 8
    xpos = lax.rem(row // 2, 4)
    core = lax.rem(row, 2)
    oyhi = 1 - yhi
    ocore = 1 - core

    def at_row(yy, xx, cc):
        return (member, yy * 8 + xx * 2 + cc)

    sibling = at_row(yhi, xpos, ocore)
    across = at_row(oyhi, xpos, core)
    xright, xfar, xleft = [lax.rem(xpos + d, 4) for d in (1, 2, 3)]
    right = at_row(yhi, xright, core)
    left = at_row(yhi, xleft, core)
    pair_first = at_row(yhi, xpos + 1 - 2 * lax.rem(xpos, 2), core)
    pair_second = at_row(yhi, 3 - xpos, core)
    low, high = pl.ds(0, 32), pl.ds(32, 32)
    peers = [lax.rem(member + d, MEMBER_DEV) for d in range(1, MEMBER_DEV)]

    def send(src, dst, done, arrived, dev):
        pltpu.make_async_remote_copy(
            src_ref=src, dst_ref=dst, send_sem=done, recv_sem=arrived, device_id=dev, device_id_type=MESH
        ).start()

    core_sem, ring_sem, mid_sem, last_sem = sib_sem, x_sem, second_sem, y_sem

    barrier = pltpu.get_barrier_semaphore()
    everyone = [sibling, across, right, left] + [(peer, row) for peer in peers]
    for dev in everyone:
        pl.semaphore_signal(barrier, inc=1, device_id=dev, device_id_type=MESH)

    def columns(block):
        return pl.ds(pl.multiple_of(lax.rem(block, PER_MEMBER) * WIDTH, WIDTH), WIDTH)

    def load_block(block, carry):
        m = block // PER_MEMBER
        pltpu.make_async_copy(
            weight_hbm.at[m, :, columns(block)], wbuf.at[block, yhi, xpos, core], load_sem.at[block // GROUP]
        ).start()
        return carry

    lax.fori_loop(0, BLOCKS, load_block, 0)
    small_loads = [
        pltpu.make_async_copy(src, dst, small_sem.at[i])
        for i, (src, dst) in enumerate(((value_hbm, value_ref), (action_hbm, action_ref), (target_hbm, target_ref)))
    ]
    for load in small_loads:
        load.start()

    def load_state(block, carry):
        m = block // PER_MEMBER
        pltpu.make_async_copy(
            state_hbm.at[m, :, columns(block)], state.at[block], state_sem.at[block // GROUP]
        ).start()
        return carry

    lax.fori_loop(0, BLOCKS, load_state, 0)

    for load in small_loads:
        load.wait()
    for m in range(LOCAL):
        row_w = value_ref[m : m + 1, :].astype(F32)
        for pos in range(PER_MEMBER):
            value_w[m * PER_MEMBER + pos] = row_w[:, pos * WIDTH : (pos + 1) * WIDTH]
    grad[...] = jnp.zeros_like(grad)
    q_acc[...] = jnp.zeros_like(q_acc)
    for half in range(2):
        part = action_ref[half * 128 : (half + 1) * 128, :].astype(F32)
        turned = jnp.transpose(part).astype(BF16)
        for m in range(LOCAL):
            lhs[m, :, half * ROWS : half * ROWS + HALF] = turned

    pl.semaphore_wait(barrier, len(everyone))

    def first_send(b):
        own = wbuf.at[b, yhi, xpos, core]

        @pl.when(lax.rem(b, GROUP) == 0)
        def _():
            wait_for(wbuf.at[pl.ds(b, GROUP), yhi, xpos, core], load_sem.at[b // GROUP])

        kind_a = is_a(GATHER_KINDS, b)

        @pl.when(kind_a)
        def _():
            send(own, own, link_done, y_sem.at[b], across)

        @pl.when(jnp.logical_not(kind_a))
        def _():
            send(own, own, link_done, x_sem.at[b], right)
            send(own, own, link_done, x_sem.at[b], left)

    def second_hop(b):
        kind_a = is_a(GATHER_KINDS, b)

        @pl.when(kind_a)
        def _():
            wait_for(wbuf.at[b, oyhi, xpos, core], y_sem.at[b])
            both = wbuf.at[b, :, xpos, core]
            send(both, both, link_done, x_sem.at[b], right)
            send(both, both, link_done, x_sem.at[b], left)

        @pl.when(jnp.logical_not(kind_a))
        def _():
            wait_for(wbuf.at[b, yhi, pl.ds(0, 2), core], x_sem.at[b])
            one = wbuf.at[b, yhi, xleft, core, low]
            send(one, one, link_done, second_sem.at[b], right)
            two = wbuf.at[b, yhi, xright, core, high]
            send(two, two, link_done, second_sem.at[b], left)

    def third_hop(b):
        kind_a = is_a(GATHER_KINDS, b)

        @pl.when(kind_a)
        def _():
            wait_for(wbuf.at[b, :, pl.ds(0, 2), core], x_sem.at[b])

            @pl.when(b == BLOCKS - 1)
            def _():
                for xx in (xpos, xleft, xright):
                    early = wbuf.at[b, :, xx, core]
                    send(early, early, sib_done, sib_sem.at[b], sibling)

            one = wbuf.at[b, :, xleft, core, low]
            send(one, one, link_done, second_sem.at[b], right)
            two = wbuf.at[b, :, xright, core, high]
            send(two, two, link_done, second_sem.at[b], left)

        @pl.when(jnp.logical_not(kind_a))
        def _():
            wait_for(wbuf.at[b, yhi, xfar, core], second_sem.at[b])
            mine = wbuf.at[b, yhi, :, core]
            send(mine, mine, link_done, y_sem.at[b], across)
            send(mine, mine, sib_done, sib_sem.at[b], sibling)

    def to_sibling(b):
        kind_a = is_a(GATHER_KINDS, b)

        @pl.when(kind_a)
        def _():
            wait_for(wbuf.at[b, :, xfar, core], second_sem.at[b])

            @pl.when(b == BLOCKS - 1)
            def _():
                late = wbuf.at[b, :, xfar, core]
                send(late, late, sib_done, sib_sem.at[b], sibling)

            @pl.when(b < BLOCKS - 1)
            def _():
                full = wbuf.at[b, :, :, core]
                send(full, full, sib_done, sib_sem.at[b], sibling)

        @pl.when(jnp.logical_not(kind_a))
        def _():
            theirs = wbuf.at[b, oyhi, :, core]
            wait_for(theirs, y_sem.at[b])
            send(theirs, theirs, sib_done, sib_sem.at[b], sibling)

    def arrive(b):
        @pl.when(lax.rem(b, GROUP) == 0)
        def _():
            wait_for(state.at[pl.ds(b, GROUP)], state_sem.at[b // GROUP])

        wait_for(wbuf.at[b, :, :, ocore], sib_sem.at[b])

    def forward_product(b):
        return jnp.dot(action_ref[...], wbuf[b].reshape(ACT, WIDTH), preferred_element_type=F32)

    def forward_elementwise(b, product):
        m = b // PER_MEMBER
        vw = value_w[b]
        step = 64
        for pos in range(0, ROWS, step):
            rows = slice(pos, pos + step)
            p = state[b, rows, :].astype(F32) + product[rows, :]
            sig = 0.5 + 0.5 * jnp.tanh(0.5 * p)
            rest = 1.0 - sig
            hid = p * sig
            first = sig + hid * rest
            state[b, rows, :] = (first * vw).astype(BF16)
            slope[b, rows, :] = first.astype(BF16)
            curve[b, rows, :] = (sig * rest * (2.0 + p * (rest - sig)) * vw).astype(BF16)
            hidden[b, rows, :] = hid.astype(BF16)
            q_acc[m, rows, :] += fold(hid * vw)

    def gradient_product(b):
        grad[b // PER_MEMBER] += lax.dot_general(
            state[b], wbuf[b].reshape(ACT, WIDTH), (((1,), (1,)), ((), ())), preferred_element_type=F32
        )

    def compute_forward(t):
        @pl.when(t == 0)
        def _():
            arrive(t)
            forward_elementwise(t, forward_product(t))

        @pl.when(t > 0)
        def _():
            arrive(t)
            product = forward_product(t)
            gradient_product(t - 1)
            forward_elementwise(t, product)

        @pl.when(t == BLOCKS - 1)
        def _():
            gradient_product(t)

    def forward_round(i, done):
        counts = [count_at(digits, i) for digits in GATHER_STEPS]
        done = run_steps((first_send, second_hop, third_hop, to_sibling), counts, done)

        @pl.when(i >= GATHER_LEAD)
        def _():
            compute_forward(i - GATHER_LEAD)

        return done

    zero = jnp.int32(0)
    lax.fori_loop(0, BLOCKS + GATHER_LEAD, forward_round, (zero, zero, zero, zero))

    def make_piece(k, half):
        rows = pl.ds(pl.multiple_of(k * PIECE + half * HALF_PIECE, HALF_PIECE), HALF_PIECE)
        both = []
        squares = None
        for m in range(LOCAL):
            g = grad[m, rows, :]
            inv = 1.0 / jnp.sqrt(jnp.sum(g * g, axis=-1, keepdims=True) + EPS)
            u = g * inv
            ub = u.astype(BF16)
            grad[m, rows, :] = u
            unit_b[m, rows, :] = ub
            rnorm[m, rows, :] = jnp.broadcast_to(inv, (HALF_PIECE, 128))
            uf = ub.astype(F32)
            both.append(uf)
            sq = fold(uf * uf)
            squares = sq if squares is None else squares + sq
        square_out[rows, :] = squares
        return (both[0] + both[1]).astype(BF16)

    for half in range(2):
        rows = pl.ds(half * HALF_PIECE, HALF_PIECE)
        for peer in peers:
            piece_out[peer, rows] = make_piece(peer, half)
            send(
                piece_out.at[peer, rows], piece_in.at[member, rows],
                misc_sem.at[0], misc_sem.at[14 + half], (peer, row),
            )
        piece_in[member, rows] = make_piece(member, half)

    target_rows = jnp.transpose(jnp.broadcast_to(target_ref[...], (128, ROWS)))
    for m in range(LOCAL):
        q = jnp.sum(q_acc[m], axis=-1, keepdims=True)
        resid[m] = q - target_rows

    for half in range(2):
        rows = pl.ds(half * HALF_PIECE, HALF_PIECE)
        wait_for(piece_in.at[pl.ds(0, MEMBER_DEV - 1), rows], misc_sem.at[14 + half])
        acc = piece_in[0, rows].astype(F32)
        for k in range(1, MEMBER_DEV):
            acc = acc + piece_in[k, rows].astype(F32)
        mine = pl.ds(pl.multiple_of(member * PIECE + half * HALF_PIECE, HALF_PIECE), HALF_PIECE)
        total[mine, :] = acc.astype(BF16)
        for peer in peers:
            send(total.at[mine], total.at[mine], misc_sem.at[2], misc_sem.at[3], (peer, row))
    square_lane = jnp.sum(jnp.transpose(square_out[...]), axis=0, keepdims=True)
    square_in[member] = jnp.broadcast_to(square_lane, (8, ROWS))
    for peer in peers:
        send(square_in.at[member], square_in.at[member], misc_sem.at[4], misc_sem.at[5], (peer, row))
    wait_for(total.at[pl.ds(0, PIECE * (MEMBER_DEV - 1))], misc_sem.at[3])

    def make_cot(m):
        step = 64
        for pos in range(0, ROWS, step):
            u = grad[m, pos : pos + step, :]
            d = (2.0 * ETA / PAIRS) * (
                total[pos : pos + step, :].astype(F32) - unit_b[m, pos : pos + step, :].astype(F32)
            )
            along = jnp.sum(u * d, axis=-1, keepdims=True)
            c = (d - u * along) * wide(rnorm[m, pos : pos + step, :], ACT)
            cot[m, pos : pos + step, :] = c.astype(BF16)

    def place_cot(m):
        for half in range(2):
            part = cot[m, half * 128 : (half + 1) * 128, :].astype(F32)
            lhs[m, :, half * ROWS + HALF : (half + 1) * ROWS] = jnp.transpose(part).astype(BF16)

    make_cot(0)
    wait_for(ring_in, link_done)
    wait_for(core_in, sib_done)

    def back_product(b):
        return jnp.dot(cot[b // PER_MEMBER], wbuf[b].reshape(ACT, WIDTH), preferred_element_type=F32)

    def partial_product(b):
        m = b // PER_MEMBER
        slot = lax.rem(b, 2)
        for q in range(4):
            some = slice(q * 256, (q + 1) * 256)
            part = jnp.dot(lhs[m, some, 0:ROWS], rhs[slot, 0:ROWS, :], preferred_element_type=F32)
            part = part + jnp.dot(
                lhs[m, some, ROWS : 2 * ROWS], rhs[slot, ROWS : 2 * ROWS, :], preferred_element_type=F32
            )
            wbuf[b, q // 2, 2 * (q % 2) : 2 * (q % 2) + 2] = part.astype(BF16).reshape(2, 2, 64, WIDTH)

    def elementwise(b, back_all):
        m = b // PER_MEMBER
        slot = lax.rem(b, 2)
        vacc = jnp.zeros((1, WIDTH), F32)
        step = 64
        for pos in range(0, ROWS, step):
            rows = slice(pos, pos + step)
            at = pos + (pos // HALF) * HALF
            back = back_all[rows, :]
            res = wide(resid[m, rows, :], WIDTH)
            tangent = state[b, rows, :]
            dpre = (tangent.astype(F32) * res + curve[b, rows, :].astype(F32) * back).astype(BF16)
            vacc = vacc + jnp.sum(
                hidden[b, rows, :].astype(F32) * res + slope[b, rows, :].astype(F32) * back, axis=0, keepdims=True
            )
            rhs[slot, at : at + step, :] = dpre
            rhs[slot, at + HALF : at + HALF + step, :] = tangent
            state[b, rows, :] = dpre
        vsum[b] = vacc

    def first_send_back(b):
        send(wbuf.at[b, :, :, ocore], core_in.at[b], core_done, core_sem.at[b], sibling)

    def compute_backward(t):
        @pl.when(t == 0)
        def _():
            back_all = back_product(t)
            place_cot(0)
            elementwise(t, back_all)

        @pl.when(jnp.logical_and(t > 0, t < BLOCKS))
        def _():
            back_all = back_product(t)
            partial_product(t - 1)
            elementwise(t, back_all)
            first_send_back(t - 1)

        @pl.when(t == BLOCKS)
        def _():
            partial_product(t - 1)
            first_send_back(t - 1)

    def second_send(b):
        wait_for(core_in.at[b], core_sem.at[b])
        for yy in range(2):
            for xx in range(4):
                wbuf[b, yy, xx, core] = (
                    wbuf[b, yy, xx, core].astype(F32) + core_in[b, yy, xx].astype(F32)
                ).astype(BF16)
        kind_a = is_a(SCATTER_KINDS, b)

        @pl.when(kind_a)
        def _():
            send(wbuf.at[b, :, xfar, core, low], ring_in.at[b, pl.ds(0, 2), low], ring_done, ring_sem.at[b], right)
            send(wbuf.at[b, :, xfar, core, high], ring_in.at[b, pl.ds(0, 2), high], ring_done, ring_sem.at[b], left)

        @pl.when(jnp.logical_not(kind_a))
        def _():
            send(wbuf.at[b, oyhi, :, core], ring_in.at[b, pl.ds(0, 4)], ring_done, ring_sem.at[b], across)

    def add_in(b, yy, xx, parts):
        s = wbuf[b, yy, xx, core].astype(F32)
        for part in parts:
            s = s + ring_in[b, part].astype(F32)
        wbuf[b, yy, xx, core] = s.astype(BF16)

    def add_half(b, yy, xx, part, rows):
        wbuf[b, yy, xx, core, rows] = (
            wbuf[b, yy, xx, core, rows].astype(F32) + ring_in[b, part, rows].astype(F32)
        ).astype(BF16)

    def third_send(b):
        kind_a = is_a(SCATTER_KINDS, b)

        @pl.when(kind_a)
        def _():
            wait_for(ring_in.at[b, pl.ds(0, 2)], ring_sem.at[b])
            for yy in range(2):
                add_half(b, yy, xright, yy, low)
                add_half(b, yy, xleft, yy, high)
            send(wbuf.at[b, :, xright, core], ring_in.at[b, pl.ds(2, 2)], ring_done, mid_sem.at[b], right)
            send(wbuf.at[b, :, xleft, core], ring_in.at[b, pl.ds(4, 2)], ring_done, mid_sem.at[b], left)

        @pl.when(jnp.logical_not(kind_a))
        def _():
            wait_for(ring_in.at[b, pl.ds(0, 4)], ring_sem.at[b])
            for xx in range(4):
                add_in(b, yhi, xx, [xx])
            send(wbuf.at[b, yhi, xfar, core, low], ring_in.at[b, 4, low], ring_done, mid_sem.at[b], right)
            send(wbuf.at[b, yhi, xfar, core, high], ring_in.at[b, 4, high], ring_done, mid_sem.at[b], left)

    def last_send(b):
        kind_a = is_a(SCATTER_KINDS, b)

        @pl.when(kind_a)
        def _():
            wait_for(ring_in.at[b, pl.ds(2, 4)], mid_sem.at[b])
            for yy in range(2):
                add_in(b, yy, xpos, [2 + yy, 4 + yy])
            send(wbuf.at[b, oyhi, xpos, core], ring_in.at[b, 6], ring_done, last_sem.at[b], across)

        @pl.when(jnp.logical_not(kind_a))
        def _():
            wait_for(ring_in.at[b, 4], mid_sem.at[b])
            add_half(b, yhi, xright, 4, low)
            add_half(b, yhi, xleft, 4, high)
            send(wbuf.at[b, yhi, xright, core], ring_in.at[b, 5], ring_done, last_sem.at[b], right)
            send(wbuf.at[b, yhi, xleft, core], ring_in.at[b, 6], ring_done, last_sem.at[b], left)

    def finish(b):
        kind_a = is_a(SCATTER_KINDS, b)

        def store(parts):
            out = wbuf[b, yhi, xpos, core].astype(F32)
            for part in parts:
                out = out + ring_in[b, part].astype(F32)
            wgrad_ref[b] = out.astype(BF16)

        @pl.when(kind_a)
        def _():
            wait_for(ring_in.at[b, 6], last_sem.at[b])
            store([6])

        @pl.when(jnp.logical_not(kind_a))
        def _():
            wait_for(ring_in.at[b, pl.ds(5, 2)], last_sem.at[b])
            store([5, 6])

    rounds = len(SCATTER_STEPS[0])

    def diversity():
        wait_for(square_in.at[pl.ds(0, MEMBER_DEV - 1)], misc_sem.at[5])
        tsq = []
        for pos in range(0, ROWS, 64):
            tf = total[pos : pos + 64, :].astype(F32)
            tsq.append(fold(tf * tf))
        cross_sum = jnp.sum(jnp.transpose(jnp.concatenate(tsq, axis=0)), axis=0, keepdims=True)
        squares = square_in[0]
        for k in range(1, MEMBER_DEV):
            squares = squares + square_in[k]
        div_ref[...] = (cross_sum - squares[0:1, :]) * (1.0 / PAIRS)

    def backward_round(t, done):
        @pl.when(t == PER_MEMBER - 2)
        def _():
            make_cot(1)
            place_cot(1)

        compute_backward(t)

        @pl.when(t == BLOCKS - 2)
        def _():
            diversity()

        @pl.when(t == BLOCKS)
        def _():
            send(vsum, vin.at[0], misc_sem.at[6], misc_sem.at[7], sibling)

        @pl.when(t == BLOCKS + 4)
        def _():
            wait_for(vsum, misc_sem.at[6])
            wait_for(vin.at[0], misc_sem.at[7])
            vin[1] = vsum[...] + vin[0]
            send(vin.at[1], vin.at[2], misc_sem.at[8], misc_sem.at[9], across)

        @pl.when(t == BLOCKS + 11)
        def _():
            wait_for(vin.at[2], misc_sem.at[9])
            vin[3] = vin[1] + vin[2]
            send(vin.at[3], vin.at[4], misc_sem.at[10], misc_sem.at[11], pair_first)

        @pl.when(t == rounds - 1)
        def _():
            wait_for(vin.at[4], misc_sem.at[11])
            vin[5] = vin[3] + vin[4]
            send(vin.at[5], vin.at[6], misc_sem.at[12], misc_sem.at[13], pair_second)

        counts = [
            jnp.where(t == rounds - 1, BLOCKS - first, count_at(digits, t))
            for digits, first in zip(SCATTER_STEPS, done)
        ]
        return run_steps((second_send, third_send, last_send, finish), counts, done)

    lax.fori_loop(0, rounds, backward_round, (zero, zero, zero, zero))

    wait_for(vin.at[6], misc_sem.at[13])
    for b in range(BLOCKS):
        m, pos = b // PER_MEMBER, b % PER_MEMBER
        vgrad_ref[m : m + 1, pos * WIDTH : (pos + 1) * WIDTH] = vin[5, b] + vin[6, b]

    wait_for(piece_out.at[pl.ds(0, MEMBER_DEV - 1)], misc_sem.at[0])
    wait_for(total.at[pl.ds(0, PIECE * (MEMBER_DEV - 1))], misc_sem.at[2])
    wait_for(square_in.at[pl.ds(0, MEMBER_DEV - 1)], misc_sem.at[4])
    for pos in (8, 10, 12):
        wait_for(vin.at[0], misc_sem.at[pos])

    wait_for(core_in, core_done)
    wait_for(ring_in, ring_done)


def hand_out(wgrad, vgrad, sgrad, div, wgrad_out, vgrad_out, sgrad_out, div_out, sem):
    for b in range(BLOCKS):
        m, pos = b // PER_MEMBER, b % PER_MEMBER
        cols = pl.ds(pos * WIDTH, WIDTH)
        pltpu.make_async_copy(sgrad.at[b], sgrad_out.at[m, :, cols], sem.at[0]).start()
        pltpu.make_async_copy(wgrad.at[b], wgrad_out.at[m, :, cols], sem.at[1]).start()
    small = [
        pltpu.make_async_copy(vgrad, vgrad_out, sem.at[2]),
        pltpu.make_async_copy(div, div_out, sem.at[3]),
    ]
    for one in small:
        one.start()
    for one in small:
        one.wait()
    wait_for(wgrad, sem.at[1])
    wait_for(sgrad, sem.at[0])


def body(action, state_term, target, weight_a, value_w):
    any_spec = pl.BlockSpec(memory_space=pl.ANY)
    vmem_spec = pl.BlockSpec(memory_space=pltpu.VMEM)
    dma = pltpu.SemaphoreType.DMA
    wgrad, vgrad, sgrad, div = pl.pallas_call(
        kernel,
        out_shape=(
            pltpu.VMEM((BLOCKS, 64, WIDTH), BF16),
            pltpu.VMEM((LOCAL, HID), F32),
            pltpu.VMEM((BLOCKS, ROWS, WIDTH), BF16),
            pltpu.VMEM((1, ROWS), F32),
        ),
        in_specs=[any_spec] * 5,
        out_specs=(vmem_spec,) * 4,
        scratch_shapes=[
            pltpu.VMEM((BLOCKS, 2, 4, 2, 64, WIDTH), BF16),
            pltpu.VMEM((BLOCKS, ROWS, WIDTH), BF16),
            pltpu.VMEM((BLOCKS, ROWS, WIDTH), BF16),
            pltpu.VMEM((BLOCKS, ROWS, WIDTH), BF16),
            pltpu.VMEM((LOCAL, ROWS, ACT), F32),
            pltpu.VMEM((LOCAL, ROWS, ACT), BF16),
            pltpu.VMEM((LOCAL, ROWS, ACT), BF16),
            pltpu.VMEM((LOCAL, ACT, 2 * ROWS), BF16),
            pltpu.VMEM((2, 2 * ROWS, WIDTH), BF16),
            pltpu.VMEM((BLOCKS, 2, 4, 64, WIDTH), BF16),
            pltpu.VMEM((BLOCKS, 7, 64, WIDTH), BF16),
            pltpu.VMEM((MEMBER_DEV, PIECE, ACT), BF16),
            pltpu.VMEM((MEMBER_DEV, PIECE, ACT), BF16),
            pltpu.VMEM((ROWS, ACT), BF16),
            pltpu.VMEM((ROWS, 128), F32),
            pltpu.VMEM((MEMBER_DEV, 8, ROWS), F32),
            pltpu.VMEM((BLOCKS, 1, WIDTH), F32),
            pltpu.VMEM((LOCAL, ROWS, 128), F32),
            pltpu.VMEM((LOCAL, ROWS, 128), F32),
            pltpu.VMEM((LOCAL, ROWS, 128), F32),
            pltpu.VMEM((BLOCKS, 1, WIDTH), F32),
            pltpu.VMEM((7, BLOCKS, 1, WIDTH), F32),
        ]
        + [dma((BLOCKS // GROUP,)) for _ in range(2)]
        + [dma for _ in range(4)]
        + [dma((BLOCKS,)) for _ in range(4)]
        + [dma((16,))]
        + [pltpu.VMEM((ROWS, ACT), BF16), pltpu.VMEM((1, ROWS), F32), pltpu.VMEM((LOCAL, HID), BF16), dma((3,))],
        compiler_params=pltpu.CompilerParams(
            collective_id=1, has_side_effects=True, vmem_limit_bytes=56 * 1024 * 1024
        ),
    )(action, state_term, target.reshape(1, ROWS), weight_a, value_w)
    wgrad, vgrad, sgrad, div = pl.pallas_call(
        hand_out,
        out_shape=(
            jax.ShapeDtypeStruct((LOCAL, 64, HID), BF16),
            jax.ShapeDtypeStruct((LOCAL, HID), F32),
            jax.ShapeDtypeStruct((LOCAL, ROWS, HID), BF16),
            jax.ShapeDtypeStruct((1, ROWS), F32),
        ),
        in_specs=[any_spec] * 4,
        out_specs=(any_spec,) * 4,
        scratch_shapes=[dma((4,))],
        compiler_params=pltpu.CompilerParams(vmem_limit_bytes=1024 * 1024),
    )(wgrad, vgrad, sgrad, div)
    return (wgrad, vgrad, sgrad, div.reshape(ROWS))


def solution(mesh):
    in_specs = (
        P("row", None),
        P("member", "row", None),
        P("row"),
        P("member", "row", None),
        P("member", None),
    )
    out_specs = (P("member", "row", None), P("member", None), P("member", "row", None), P("row"))
    return jax.shard_map(body, mesh=mesh, in_specs=in_specs, out_specs=out_specs, check_vma=False)
```

```python
import jax
import jax.numpy as jnp
from jax import lax
from jax.experimental import pallas as pl
from jax.experimental.pallas import tpu as pltpu
from jax.sharding import PartitionSpec as P

EPS = 1e-06
ETA = 5.0
MESH = pl.DeviceIdType.MESH
F32 = jnp.float32
BF16 = jnp.bfloat16

ACT = 1024
HID = 4096
ROWS = 256
LOCAL = 2
MEMBER_DEV = 8
PAIRS = 16 * 15
WIDTH = 256
PER_MEMBER = HID // WIDTH
BLOCKS = LOCAL * PER_MEMBER
PIECE = ROWS // MEMBER_DEV
GROUP = 8
HALF_PIECE = PIECE // 2
HALF = ROWS // 2

GATHER_KINDS = "BABABBABABAAABABABBAABAABABAAAAA"
SCATTER_KINDS = "ABABAABABBAABAABBAAAABBABABAABAB"
GATHER_STEPS = (
    "1133121113010121000020321011000000000000000000000000",
    "0000011321001200101130101210123020000110000000000000",
    "0000000000302200031101310011202001001101030101000000",
    "0000000000000000101111011102022012102010121103111000",
)
GATHER_LEAD = 20
SCATTER_STEPS = (
    "00002021021102201031101201110112010110000000000",
    "00000001020300210302002301100020100210020012000",
    "00000000000012103011203001000100000003000023200",
    "00000000000000010010010100010000101200120210000",
)
PER_WORD = 13


def is_a(kinds, block):
    low, high = [
        sum((letter == "A") << pos for pos, letter in enumerate(part)) for part in (kinds[:16], kinds[16:])
    ]
    return lax.rem(lax.shift_right_logical(jnp.where(block < 16, low, high), lax.rem(block, 16)), 2) == 1


def count_at(digits, t):
    words = [
        sum(int(digit) << (2 * pos) for pos, digit in enumerate(digits[start : start + PER_WORD]))
        for start in range(0, len(digits), PER_WORD)
    ]
    word = jnp.int32(words[0])
    for pos in range(1, len(words)):
        word = jnp.where(t // PER_WORD == pos, words[pos], word)
    return lax.rem(lax.shift_right_logical(word, 2 * lax.rem(t, PER_WORD)), 4)


def run_steps(steps, counts, done):
    after = []
    for step, count, first in zip(steps, counts, done):
        def one(b, carry, step=step):
            step(b)
            return carry

        lax.fori_loop(first, first + count, one, 0)
        after.append(first + count)
    return tuple(after)


def wait_for(ref, sem):
    pltpu.make_async_copy(ref, ref, sem).wait()


def fold(value):
    out = value[:, 0:128]
    for pos in range(128, value.shape[1], 128):
        out = out + value[:, pos : pos + 128]
    return out


def wide(value, width):
    return jnp.concatenate([value] * (width // 128), axis=1)


def kernel(
    action_hbm, state_hbm, target_hbm, weight_hbm, value_hbm,
    wgrad_ref, vgrad_ref, state, div_ref,
    wbuf, hidden, slope, curve, grad, unit_b, cot, lhs, rhs, core_in, ring_in,
    piece_out, piece_in, total, square_out, square_in, value_w, q_acc, resid, rnorm, vsum, vin,
    load_sem, state_sem, link_done, sib_done, core_done, ring_done,
    x_sem, y_sem, second_sem, sib_sem,
    misc_sem, action_ref, target_ref, value_ref, small_sem,
):
    member = lax.axis_index("member")
    row = lax.axis_index("row")
    yhi = row // 8
    xpos = lax.rem(row // 2, 4)
    core = lax.rem(row, 2)
    oyhi = 1 - yhi
    ocore = 1 - core

    def at_row(yy, xx, cc):
        return (member, yy * 8 + xx * 2 + cc)

    sibling = at_row(yhi, xpos, ocore)
    across = at_row(oyhi, xpos, core)
    xright, xfar, xleft = [lax.rem(xpos + d, 4) for d in (1, 2, 3)]
    right = at_row(yhi, xright, core)
    left = at_row(yhi, xleft, core)
    pair_first = at_row(yhi, xpos + 1 - 2 * lax.rem(xpos, 2), core)
    pair_second = at_row(yhi, 3 - xpos, core)
    low, high = pl.ds(0, 32), pl.ds(32, 32)
    peers = [lax.rem(member + d, MEMBER_DEV) for d in (1, 7, 2, 6, 3, 5, 4)]

    def send(src, dst, done, arrived, dev):
        pltpu.make_async_remote_copy(
            src_ref=src, dst_ref=dst, send_sem=done, recv_sem=arrived, device_id=dev, device_id_type=MESH
        ).start()

    core_sem, ring_sem, mid_sem, last_sem = sib_sem, x_sem, second_sem, y_sem

    barrier = pltpu.get_barrier_semaphore()
    everyone = [sibling, across, right, left] + [(peer, row) for peer in peers]
    for dev in everyone:
        pl.semaphore_signal(barrier, inc=1, device_id=dev, device_id_type=MESH)

    def columns(block):
        return pl.ds(pl.multiple_of(lax.rem(block, PER_MEMBER) * WIDTH, WIDTH), WIDTH)

    def load_block(block, carry):
        m = block // PER_MEMBER
        pltpu.make_async_copy(
            weight_hbm.at[m, :, columns(block)], wbuf.at[block, yhi, xpos, core], load_sem.at[block // GROUP]
        ).start()
        return carry

    lax.fori_loop(0, BLOCKS, load_block, 0)
    small_loads = [
        pltpu.make_async_copy(src, dst, small_sem.at[i])
        for i, (src, dst) in enumerate(((value_hbm, value_ref), (action_hbm, action_ref), (target_hbm, target_ref)))
    ]
    for load in small_loads:
        load.start()

    def load_state(block, carry):
        m = block // PER_MEMBER
        pltpu.make_async_copy(
            state_hbm.at[m, :, columns(block)], state.at[block], state_sem.at[block // GROUP]
        ).start()
        return carry

    lax.fori_loop(0, BLOCKS, load_state, 0)

    for load in small_loads:
        load.wait()
    for m in range(LOCAL):
        row_w = value_ref[m : m + 1, :].astype(F32)
        for pos in range(PER_MEMBER):
            value_w[m * PER_MEMBER + pos] = row_w[:, pos * WIDTH : (pos + 1) * WIDTH]
    grad[...] = jnp.zeros_like(grad)
    q_acc[...] = jnp.zeros_like(q_acc)
    for half in range(2):
        part = action_ref[half * 128 : (half + 1) * 128, :].astype(F32)
        turned = jnp.transpose(part).astype(BF16)
        for m in range(LOCAL):
            lhs[m, :, half * ROWS : half * ROWS + HALF] = turned

    pl.semaphore_wait(barrier, len(everyone))

    def first_send(b):
        own = wbuf.at[b, yhi, xpos, core]

        @pl.when(lax.rem(b, GROUP) == 0)
        def _():
            wait_for(wbuf.at[pl.ds(b, GROUP), yhi, xpos, core], load_sem.at[b // GROUP])

        kind_a = is_a(GATHER_KINDS, b)

        @pl.when(kind_a)
        def _():
            send(own, own, link_done, y_sem.at[b], across)

        @pl.when(jnp.logical_not(kind_a))
        def _():
            send(own, own, link_done, x_sem.at[b], right)
            send(own, own, link_done, x_sem.at[b], left)

    def second_hop(b):
        kind_a = is_a(GATHER_KINDS, b)

        @pl.when(kind_a)
        def _():
            wait_for(wbuf.at[b, oyhi, xpos, core], y_sem.at[b])
            both = wbuf.at[b, :, xpos, core]
            send(both, both, link_done, x_sem.at[b], right)
            send(both, both, link_done, x_sem.at[b], left)

        @pl.when(jnp.logical_not(kind_a))
        def _():
            wait_for(wbuf.at[b, yhi, pl.ds(0, 2), core], x_sem.at[b])
            one = wbuf.at[b, yhi, xleft, core, low]
            send(one, one, link_done, second_sem.at[b], right)
            two = wbuf.at[b, yhi, xright, core, high]
            send(two, two, link_done, second_sem.at[b], left)

    def third_hop(b):
        kind_a = is_a(GATHER_KINDS, b)

        @pl.when(kind_a)
        def _():
            wait_for(wbuf.at[b, :, pl.ds(0, 2), core], x_sem.at[b])

            @pl.when(b == BLOCKS - 1)
            def _():
                for xx in (xpos, xleft, xright):
                    early = wbuf.at[b, :, xx, core]
                    send(early, early, sib_done, sib_sem.at[b], sibling)

            one = wbuf.at[b, :, xleft, core, low]
            send(one, one, link_done, second_sem.at[b], right)
            two = wbuf.at[b, :, xright, core, high]
            send(two, two, link_done, second_sem.at[b], left)

        @pl.when(jnp.logical_not(kind_a))
        def _():
            wait_for(wbuf.at[b, yhi, xfar, core], second_sem.at[b])
            mine = wbuf.at[b, yhi, :, core]
            send(mine, mine, link_done, y_sem.at[b], across)
            send(mine, mine, sib_done, sib_sem.at[b], sibling)

    def to_sibling(b):
        kind_a = is_a(GATHER_KINDS, b)

        @pl.when(kind_a)
        def _():
            wait_for(wbuf.at[b, :, xfar, core], second_sem.at[b])

            @pl.when(b == BLOCKS - 1)
            def _():
                late = wbuf.at[b, :, xfar, core]
                send(late, late, sib_done, sib_sem.at[b], sibling)

            @pl.when(b < BLOCKS - 1)
            def _():
                full = wbuf.at[b, :, :, core]
                send(full, full, sib_done, sib_sem.at[b], sibling)

        @pl.when(jnp.logical_not(kind_a))
        def _():
            theirs = wbuf.at[b, oyhi, :, core]
            wait_for(theirs, y_sem.at[b])
            send(theirs, theirs, sib_done, sib_sem.at[b], sibling)

    def arrive(b):
        @pl.when(lax.rem(b, GROUP) == 0)
        def _():
            wait_for(state.at[pl.ds(b, GROUP)], state_sem.at[b // GROUP])

        wait_for(wbuf.at[b, :, :, ocore], sib_sem.at[b])

    def forward_product(b):
        return jnp.dot(action_ref[...], wbuf[b].reshape(ACT, WIDTH), preferred_element_type=F32)

    def forward_elementwise(b, product):
        m = b // PER_MEMBER
        vw = value_w[b]
        step = 64
        for pos in range(0, ROWS, step):
            rows = slice(pos, pos + step)
            p = state[b, rows, :].astype(F32) + product[rows, :]
            sig = 0.5 + 0.5 * jnp.tanh(0.5 * p)
            rest = 1.0 - sig
            hid = p * sig
            first = sig + hid * rest
            state[b, rows, :] = (first * vw).astype(BF16)
            slope[b, rows, :] = first.astype(BF16)
            curve[b, rows, :] = (sig * rest * (2.0 + p * (rest - sig)) * vw).astype(BF16)
            hidden[b, rows, :] = hid.astype(BF16)
            q_acc[m, rows, :] += fold(hid * vw)

    def gradient_product(b):
        grad[b // PER_MEMBER] += lax.dot_general(
            state[b], wbuf[b].reshape(ACT, WIDTH), (((1,), (1,)), ((), ())), preferred_element_type=F32
        )

    def compute_forward(t):
        @pl.when(t == 0)
        def _():
            arrive(t)
            forward_elementwise(t, forward_product(t))

        @pl.when(t > 0)
        def _():
            arrive(t)
            product = forward_product(t)
            gradient_product(t - 1)
            forward_elementwise(t, product)

        @pl.when(t == BLOCKS - 1)
        def _():
            gradient_product(t)

    def forward_round(i, done):
        counts = [count_at(digits, i) for digits in GATHER_STEPS]
        done = run_steps((first_send, second_hop, third_hop, to_sibling), counts, done)

        @pl.when(i >= GATHER_LEAD)
        def _():
            compute_forward(i - GATHER_LEAD)

        return done

    zero = jnp.int32(0)
    lax.fori_loop(0, BLOCKS + GATHER_LEAD, forward_round, (zero, zero, zero, zero))

    def make_piece(k, half):
        rows = pl.ds(pl.multiple_of(k * PIECE + half * HALF_PIECE, HALF_PIECE), HALF_PIECE)
        both = []
        squares = None
        for m in range(LOCAL):
            g = grad[m, rows, :]
            inv = 1.0 / jnp.sqrt(jnp.sum(g * g, axis=-1, keepdims=True) + EPS)
            u = g * inv
            ub = u.astype(BF16)
            grad[m, rows, :] = u
            unit_b[m, rows, :] = ub
            rnorm[m, rows, :] = jnp.broadcast_to(inv, (HALF_PIECE, 128))
            uf = ub.astype(F32)
            both.append(uf)
            sq = fold(uf * uf)
            squares = sq if squares is None else squares + sq
        square_out[rows, :] = squares
        return (both[0] + both[1]).astype(BF16)

    for half in range(2):
        rows = pl.ds(half * HALF_PIECE, HALF_PIECE)
        for peer in peers:
            piece_out[peer, rows] = make_piece(peer, half)
            send(
                piece_out.at[peer, rows], piece_in.at[member, rows],
                misc_sem.at[0], misc_sem.at[14 + half], (peer, row),
            )
        piece_in[member, rows] = make_piece(member, half)

    target_rows = jnp.transpose(jnp.broadcast_to(target_ref[...], (128, ROWS)))
    for m in range(LOCAL):
        q = jnp.sum(q_acc[m], axis=-1, keepdims=True)
        resid[m] = q - target_rows

    for half in range(2):
        rows = pl.ds(half * HALF_PIECE, HALF_PIECE)
        wait_for(piece_in.at[pl.ds(0, MEMBER_DEV - 1), rows], misc_sem.at[14 + half])
        acc = piece_in[0, rows].astype(F32)
        for k in range(1, MEMBER_DEV):
            acc = acc + piece_in[k, rows].astype(F32)
        mine = pl.ds(pl.multiple_of(member * PIECE + half * HALF_PIECE, HALF_PIECE), HALF_PIECE)
        total[mine, :] = acc.astype(BF16)
        for peer in peers:
            send(total.at[mine], total.at[mine], misc_sem.at[2], misc_sem.at[3], (peer, row))
    square_lane = jnp.sum(jnp.transpose(square_out[...]), axis=0, keepdims=True)
    square_in[member] = jnp.broadcast_to(square_lane, (8, ROWS))
    for peer in peers:
        send(square_in.at[member], square_in.at[member], misc_sem.at[4], misc_sem.at[5], (peer, row))
    wait_for(total.at[pl.ds(0, PIECE * (MEMBER_DEV - 1))], misc_sem.at[3])

    def make_cot(m):
        step = 64
        for pos in range(0, ROWS, step):
            u = grad[m, pos : pos + step, :]
            d = (2.0 * ETA / PAIRS) * (
                total[pos : pos + step, :].astype(F32) - unit_b[m, pos : pos + step, :].astype(F32)
            )
            along = jnp.sum(u * d, axis=-1, keepdims=True)
            c = (d - u * along) * wide(rnorm[m, pos : pos + step, :], ACT)
            cot[m, pos : pos + step, :] = c.astype(BF16)

    def place_cot(m):
        for half in range(2):
            part = cot[m, half * 128 : (half + 1) * 128, :].astype(F32)
            lhs[m, :, half * ROWS + HALF : (half + 1) * ROWS] = jnp.transpose(part).astype(BF16)

    make_cot(0)
    wait_for(ring_in, link_done)
    wait_for(core_in, sib_done)

    def back_product(b):
        return jnp.dot(cot[b // PER_MEMBER], wbuf[b].reshape(ACT, WIDTH), preferred_element_type=F32)

    def partial_product(b):
        m = b // PER_MEMBER
        slot = lax.rem(b, 2)
        for q in range(4):
            some = slice(q * 256, (q + 1) * 256)
            part = jnp.dot(lhs[m, some, 0:ROWS], rhs[slot, 0:ROWS, :], preferred_element_type=F32)
            part = part + jnp.dot(
                lhs[m, some, ROWS : 2 * ROWS], rhs[slot, ROWS : 2 * ROWS, :], preferred_element_type=F32
            )
            wbuf[b, q // 2, 2 * (q % 2) : 2 * (q % 2) + 2] = part.astype(BF16).reshape(2, 2, 64, WIDTH)

    def elementwise(b, back_all):
        m = b // PER_MEMBER
        slot = lax.rem(b, 2)
        vacc = jnp.zeros((1, WIDTH), F32)
        step = 64
        for pos in range(0, ROWS, step):
            rows = slice(pos, pos + step)
            at = pos + (pos // HALF) * HALF
            back = back_all[rows, :]
            res = wide(resid[m, rows, :], WIDTH)
            tangent = state[b, rows, :]
            dpre = (tangent.astype(F32) * res + curve[b, rows, :].astype(F32) * back).astype(BF16)
            vacc = vacc + jnp.sum(
                hidden[b, rows, :].astype(F32) * res + slope[b, rows, :].astype(F32) * back, axis=0, keepdims=True
            )
            rhs[slot, at : at + step, :] = dpre
            rhs[slot, at + HALF : at + HALF + step, :] = tangent
            state[b, rows, :] = dpre
        vsum[b] = vacc

    def first_send_back(b):
        send(wbuf.at[b, :, :, ocore], core_in.at[b], core_done, core_sem.at[b], sibling)

    def compute_backward(t):
        @pl.when(t == 0)
        def _():
            back_all = back_product(t)
            place_cot(0)
            elementwise(t, back_all)

        @pl.when(jnp.logical_and(t > 0, t < BLOCKS))
        def _():
            back_all = back_product(t)
            partial_product(t - 1)
            elementwise(t, back_all)
            first_send_back(t - 1)

        @pl.when(t == BLOCKS)
        def _():
            partial_product(t - 1)
            first_send_back(t - 1)

    def second_send(b):
        wait_for(core_in.at[b], core_sem.at[b])
        for yy in range(2):
            for xx in range(4):
                wbuf[b, yy, xx, core] = (
                    wbuf[b, yy, xx, core].astype(F32) + core_in[b, yy, xx].astype(F32)
                ).astype(BF16)
        kind_a = is_a(SCATTER_KINDS, b)

        @pl.when(kind_a)
        def _():
            send(wbuf.at[b, :, xfar, core, low], ring_in.at[b, pl.ds(0, 2), low], ring_done, ring_sem.at[b], right)
            send(wbuf.at[b, :, xfar, core, high], ring_in.at[b, pl.ds(0, 2), high], ring_done, ring_sem.at[b], left)

        @pl.when(jnp.logical_not(kind_a))
        def _():
            send(wbuf.at[b, oyhi, :, core], ring_in.at[b, pl.ds(0, 4)], ring_done, ring_sem.at[b], across)

    def add_in(b, yy, xx, parts):
        s = wbuf[b, yy, xx, core].astype(F32)
        for part in parts:
            s = s + ring_in[b, part].astype(F32)
        wbuf[b, yy, xx, core] = s.astype(BF16)

    def add_half(b, yy, xx, part, rows):
        wbuf[b, yy, xx, core, rows] = (
            wbuf[b, yy, xx, core, rows].astype(F32) + ring_in[b, part, rows].astype(F32)
        ).astype(BF16)

    def third_send(b):
        kind_a = is_a(SCATTER_KINDS, b)

        @pl.when(kind_a)
        def _():
            wait_for(ring_in.at[b, pl.ds(0, 2)], ring_sem.at[b])
            for yy in range(2):
                add_half(b, yy, xright, yy, low)
                add_half(b, yy, xleft, yy, high)
            send(wbuf.at[b, :, xright, core], ring_in.at[b, pl.ds(2, 2)], ring_done, mid_sem.at[b], right)
            send(wbuf.at[b, :, xleft, core], ring_in.at[b, pl.ds(4, 2)], ring_done, mid_sem.at[b], left)

        @pl.when(jnp.logical_not(kind_a))
        def _():
            wait_for(ring_in.at[b, pl.ds(0, 4)], ring_sem.at[b])
            for xx in range(4):
                add_in(b, yhi, xx, [xx])
            send(wbuf.at[b, yhi, xfar, core, low], ring_in.at[b, 4, low], ring_done, mid_sem.at[b], right)
            send(wbuf.at[b, yhi, xfar, core, high], ring_in.at[b, 4, high], ring_done, mid_sem.at[b], left)

    def last_send(b):
        kind_a = is_a(SCATTER_KINDS, b)

        @pl.when(kind_a)
        def _():
            wait_for(ring_in.at[b, pl.ds(2, 4)], mid_sem.at[b])
            for yy in range(2):
                add_in(b, yy, xpos, [2 + yy, 4 + yy])
            send(wbuf.at[b, oyhi, xpos, core], ring_in.at[b, 6], ring_done, last_sem.at[b], across)

        @pl.when(jnp.logical_not(kind_a))
        def _():
            wait_for(ring_in.at[b, 4], mid_sem.at[b])
            add_half(b, yhi, xright, 4, low)
            add_half(b, yhi, xleft, 4, high)
            send(wbuf.at[b, yhi, xright, core], ring_in.at[b, 5], ring_done, last_sem.at[b], right)
            send(wbuf.at[b, yhi, xleft, core], ring_in.at[b, 6], ring_done, last_sem.at[b], left)

    def finish(b):
        kind_a = is_a(SCATTER_KINDS, b)

        def store(parts):
            out = wbuf[b, yhi, xpos, core].astype(F32)
            for part in parts:
                out = out + ring_in[b, part].astype(F32)
            wgrad_ref[b] = out.astype(BF16)

        @pl.when(kind_a)
        def _():
            wait_for(ring_in.at[b, 6], last_sem.at[b])
            store([6])

        @pl.when(jnp.logical_not(kind_a))
        def _():
            wait_for(ring_in.at[b, pl.ds(5, 2)], last_sem.at[b])
            store([5, 6])

    rounds = len(SCATTER_STEPS[0])

    def diversity():
        wait_for(square_in.at[pl.ds(0, MEMBER_DEV - 1)], misc_sem.at[5])
        tsq = []
        for pos in range(0, ROWS, 64):
            tf = total[pos : pos + 64, :].astype(F32)
            tsq.append(fold(tf * tf))
        cross_sum = jnp.sum(jnp.transpose(jnp.concatenate(tsq, axis=0)), axis=0, keepdims=True)
        squares = square_in[0]
        for k in range(1, MEMBER_DEV):
            squares = squares + square_in[k]
        div_ref[...] = (cross_sum - squares[0:1, :]) * (1.0 / PAIRS)

    def backward_round(t, done):
        @pl.when(t == PER_MEMBER - 2)
        def _():
            make_cot(1)
            place_cot(1)

        compute_backward(t)

        @pl.when(t == BLOCKS - 2)
        def _():
            diversity()

        @pl.when(t == BLOCKS)
        def _():
            send(vsum, vin.at[0], misc_sem.at[6], misc_sem.at[7], sibling)

        @pl.when(t == BLOCKS + 4)
        def _():
            wait_for(vsum, misc_sem.at[6])
            wait_for(vin.at[0], misc_sem.at[7])
            vin[1] = vsum[...] + vin[0]
            send(vin.at[1], vin.at[2], misc_sem.at[8], misc_sem.at[9], across)

        @pl.when(t == BLOCKS + 11)
        def _():
            wait_for(vin.at[2], misc_sem.at[9])
            vin[3] = vin[1] + vin[2]
            send(vin.at[3], vin.at[4], misc_sem.at[10], misc_sem.at[11], pair_first)

        @pl.when(t == rounds - 1)
        def _():
            wait_for(vin.at[4], misc_sem.at[11])
            vin[5] = vin[3] + vin[4]
            send(vin.at[5], vin.at[6], misc_sem.at[12], misc_sem.at[13], pair_second)

        counts = [
            jnp.where(t == rounds - 1, BLOCKS - first, count_at(digits, t))
            for digits, first in zip(SCATTER_STEPS, done)
        ]
        return run_steps((second_send, third_send, last_send, finish), counts, done)

    lax.fori_loop(0, rounds, backward_round, (zero, zero, zero, zero))

    wait_for(vin.at[6], misc_sem.at[13])
    for b in range(BLOCKS):
        m, pos = b // PER_MEMBER, b % PER_MEMBER
        vgrad_ref[m : m + 1, pos * WIDTH : (pos + 1) * WIDTH] = vin[5, b] + vin[6, b]

    wait_for(piece_out.at[pl.ds(0, MEMBER_DEV - 1)], misc_sem.at[0])
    wait_for(total.at[pl.ds(0, PIECE * (MEMBER_DEV - 1))], misc_sem.at[2])
    wait_for(square_in.at[pl.ds(0, MEMBER_DEV - 1)], misc_sem.at[4])
    for pos in (8, 10, 12):
        wait_for(vin.at[0], misc_sem.at[pos])

    wait_for(core_in, core_done)
    wait_for(ring_in, ring_done)


def hand_out(wgrad, vgrad, sgrad, div, wgrad_out, vgrad_out, sgrad_out, div_out, sem):
    for b in range(BLOCKS):
        m, pos = b // PER_MEMBER, b % PER_MEMBER
        cols = pl.ds(pos * WIDTH, WIDTH)
        pltpu.make_async_copy(sgrad.at[b], sgrad_out.at[m, :, cols], sem.at[0]).start()
        pltpu.make_async_copy(wgrad.at[b], wgrad_out.at[m, :, cols], sem.at[1]).start()
    small = [
        pltpu.make_async_copy(vgrad, vgrad_out, sem.at[2]),
        pltpu.make_async_copy(div, div_out, sem.at[3]),
    ]
    for one in small:
        one.start()
    for one in small:
        one.wait()
    wait_for(wgrad, sem.at[1])
    wait_for(sgrad, sem.at[0])


def body(action, state_term, target, weight_a, value_w):
    any_spec = pl.BlockSpec(memory_space=pl.ANY)
    vmem_spec = pl.BlockSpec(memory_space=pltpu.VMEM)
    dma = pltpu.SemaphoreType.DMA
    wgrad, vgrad, sgrad, div = pl.pallas_call(
        kernel,
        out_shape=(
            pltpu.VMEM((BLOCKS, 64, WIDTH), BF16),
            pltpu.VMEM((LOCAL, HID), F32),
            pltpu.VMEM((BLOCKS, ROWS, WIDTH), BF16),
            pltpu.VMEM((1, ROWS), F32),
        ),
        in_specs=[any_spec] * 5,
        out_specs=(vmem_spec,) * 4,
        scratch_shapes=[
            pltpu.VMEM((BLOCKS, 2, 4, 2, 64, WIDTH), BF16),
            pltpu.VMEM((BLOCKS, ROWS, WIDTH), BF16),
            pltpu.VMEM((BLOCKS, ROWS, WIDTH), BF16),
            pltpu.VMEM((BLOCKS, ROWS, WIDTH), BF16),
            pltpu.VMEM((LOCAL, ROWS, ACT), F32),
            pltpu.VMEM((LOCAL, ROWS, ACT), BF16),
            pltpu.VMEM((LOCAL, ROWS, ACT), BF16),
            pltpu.VMEM((LOCAL, ACT, 2 * ROWS), BF16),
            pltpu.VMEM((2, 2 * ROWS, WIDTH), BF16),
            pltpu.VMEM((BLOCKS, 2, 4, 64, WIDTH), BF16),
            pltpu.VMEM((BLOCKS, 7, 64, WIDTH), BF16),
            pltpu.VMEM((MEMBER_DEV, PIECE, ACT), BF16),
            pltpu.VMEM((MEMBER_DEV, PIECE, ACT), BF16),
            pltpu.VMEM((ROWS, ACT), BF16),
            pltpu.VMEM((ROWS, 128), F32),
            pltpu.VMEM((MEMBER_DEV, 8, ROWS), F32),
            pltpu.VMEM((BLOCKS, 1, WIDTH), F32),
            pltpu.VMEM((LOCAL, ROWS, 128), F32),
            pltpu.VMEM((LOCAL, ROWS, 128), F32),
            pltpu.VMEM((LOCAL, ROWS, 128), F32),
            pltpu.VMEM((BLOCKS, 1, WIDTH), F32),
            pltpu.VMEM((7, BLOCKS, 1, WIDTH), F32),
        ]
        + [dma((BLOCKS // GROUP,)) for _ in range(2)]
        + [dma for _ in range(4)]
        + [dma((BLOCKS,)) for _ in range(4)]
        + [dma((16,))]
        + [pltpu.VMEM((ROWS, ACT), BF16), pltpu.VMEM((1, ROWS), F32), pltpu.VMEM((LOCAL, HID), BF16), dma((3,))],
        compiler_params=pltpu.CompilerParams(
            collective_id=1, has_side_effects=True, vmem_limit_bytes=56 * 1024 * 1024
        ),
    )(action, state_term, target.reshape(1, ROWS), weight_a, value_w)
    wgrad, vgrad, sgrad, div = pl.pallas_call(
        hand_out,
        out_shape=(
            jax.ShapeDtypeStruct((LOCAL, 64, HID), BF16),
            jax.ShapeDtypeStruct((LOCAL, HID), F32),
            jax.ShapeDtypeStruct((LOCAL, ROWS, HID), BF16),
            jax.ShapeDtypeStruct((1, ROWS), F32),
        ),
        in_specs=[any_spec] * 4,
        out_specs=(any_spec,) * 4,
        scratch_shapes=[dma((4,))],
        compiler_params=pltpu.CompilerParams(vmem_limit_bytes=1024 * 1024),
    )(wgrad, vgrad, sgrad, div)
    return (wgrad, vgrad, sgrad, div.reshape(ROWS))


def solution(mesh):
    in_specs = (
        P("row", None),
        P("member", "row", None),
        P("row"),
        P("member", "row", None),
        P("member", None),
    )
    out_specs = (P("member", "row", None), P("member", None), P("member", "row", None), P("row"))
    return jax.shard_map(body, mesh=mesh, in_specs=in_specs, out_specs=out_specs, check_vma=False)
```

```python
import jax
import jax.numpy as jnp
from jax import lax
from jax.experimental import pallas as pl
from jax.experimental.pallas import tpu as pltpu
from jax.sharding import PartitionSpec as P

EPS = 1e-06
ETA = 5.0
MESH = pl.DeviceIdType.MESH
F32 = jnp.float32
BF16 = jnp.bfloat16

ACT = 1024
HID = 4096
ROWS = 256
LOCAL = 2
MEMBER_DEV = 8
PAIRS = 16 * 15
WIDTH = 256
PER_MEMBER = HID // WIDTH
BLOCKS = LOCAL * PER_MEMBER
PIECE = ROWS // MEMBER_DEV
GROUP = 8
HALF_PIECE = PIECE // 2
HALF = ROWS // 2

GATHER_KINDS = "BABAABBBAAABBAAABABBAABAABBAAABA"
SCATTER_KINDS = "ABABAABABBAABAABBAAAABBABABAABAB"
GATHER_STEPS = (
    "3023233011001000312011220000000100000000000000000000",
    "0000112201300220000102110110210210221000000000000000",
    "0000000120031001310100100021030201031103000100000000",
    "0000000000000212011011000030101002102211011211120000",
)
GATHER_LEAD = 20
SCATTER_STEPS = (
    "00002021021102201031101201110112010110000000000",
    "00000001020300210302002301100020100210020012000",
    "00000000000012103011203001000100000003000023200",
    "00000000000000010010010100010000101200120210000",
)
PER_WORD = 13


def is_a(kinds, block):
    low, high = [
        sum((letter == "A") << pos for pos, letter in enumerate(part)) for part in (kinds[:16], kinds[16:])
    ]
    return lax.rem(lax.shift_right_logical(jnp.where(block < 16, low, high), lax.rem(block, 16)), 2) == 1


def count_at(digits, t):
    words = [
        sum(int(digit) << (2 * pos) for pos, digit in enumerate(digits[start : start + PER_WORD]))
        for start in range(0, len(digits), PER_WORD)
    ]
    word = jnp.int32(words[0])
    for pos in range(1, len(words)):
        word = jnp.where(t // PER_WORD == pos, words[pos], word)
    return lax.rem(lax.shift_right_logical(word, 2 * lax.rem(t, PER_WORD)), 4)


def run_steps(steps, counts, done):
    after = []
    for step, count, first in zip(steps, counts, done):
        def one(b, carry, step=step):
            step(b)
            return carry

        lax.fori_loop(first, first + count, one, 0)
        after.append(first + count)
    return tuple(after)


def wait_for(ref, sem):
    pltpu.make_async_copy(ref, ref, sem).wait()


def fold(value):
    out = value[:, 0:128]
    for pos in range(128, value.shape[1], 128):
        out = out + value[:, pos : pos + 128]
    return out


def wide(value, width):
    return jnp.concatenate([value] * (width // 128), axis=1)


def kernel(
    action_hbm, state_hbm, target_hbm, weight_hbm, value_hbm,
    wgrad_ref, vgrad_ref, state, div_ref,
    wbuf, hidden, slope, curve, grad, unit_b, cot, lhs, rhs, core_in, ring_in,
    piece_out, piece_in, total, square_out, square_in, value_w, q_acc, resid, rnorm, vsum, vin,
    load_sem, state_sem, link_done, sib_done, core_done, ring_done,
    x_sem, y_sem, second_sem, sib_sem,
    misc_sem, action_ref, target_ref, value_ref, small_sem,
):
    member = lax.axis_index("member")
    row = lax.axis_index("row")
    yhi = row // 8
    xpos = lax.rem(row // 2, 4)
    core = lax.rem(row, 2)
    oyhi = 1 - yhi
    ocore = 1 - core

    def at_row(yy, xx, cc):
        return (member, yy * 8 + xx * 2 + cc)

    sibling = at_row(yhi, xpos, ocore)
    across = at_row(oyhi, xpos, core)
    xright, xfar, xleft = [lax.rem(xpos + d, 4) for d in (1, 2, 3)]
    right = at_row(yhi, xright, core)
    left = at_row(yhi, xleft, core)
    pair_first = at_row(yhi, xpos + 1 - 2 * lax.rem(xpos, 2), core)
    pair_second = at_row(yhi, 3 - xpos, core)
    low, high = pl.ds(0, 32), pl.ds(32, 32)
    peers = [lax.rem(member + d, MEMBER_DEV) for d in range(1, MEMBER_DEV)]

    def send(src, dst, done, arrived, dev):
        pltpu.make_async_remote_copy(
            src_ref=src, dst_ref=dst, send_sem=done, recv_sem=arrived, device_id=dev, device_id_type=MESH
        ).start()

    core_sem, ring_sem, mid_sem, last_sem = sib_sem, x_sem, second_sem, y_sem

    barrier = pltpu.get_barrier_semaphore()
    everyone = [sibling, across, right, left] + [(peer, row) for peer in peers]
    for dev in everyone:
        pl.semaphore_signal(barrier, inc=1, device_id=dev, device_id_type=MESH)

    def columns(block):
        return pl.ds(pl.multiple_of(lax.rem(block, PER_MEMBER) * WIDTH, WIDTH), WIDTH)

    def load_block(block, carry):
        m = block // PER_MEMBER
        pltpu.make_async_copy(
            weight_hbm.at[m, :, columns(block)], wbuf.at[block, yhi, xpos, core], load_sem.at[block // GROUP]
        ).start()
        return carry

    lax.fori_loop(0, BLOCKS, load_block, 0)
    small_loads = [
        pltpu.make_async_copy(src, dst, small_sem.at[i])
        for i, (src, dst) in enumerate(((value_hbm, value_ref), (action_hbm, action_ref), (target_hbm, target_ref)))
    ]
    for load in small_loads:
        load.start()

    def load_state(block, carry):
        m = block // PER_MEMBER
        pltpu.make_async_copy(
            state_hbm.at[m, :, columns(block)], state.at[block], state_sem.at[block // GROUP]
        ).start()
        return carry

    lax.fori_loop(0, BLOCKS, load_state, 0)

    for load in small_loads:
        load.wait()
    for m in range(LOCAL):
        row_w = value_ref[m : m + 1, :].astype(F32)
        for pos in range(PER_MEMBER):
            value_w[m * PER_MEMBER + pos] = row_w[:, pos * WIDTH : (pos + 1) * WIDTH]
    grad[...] = jnp.zeros_like(grad)
    q_acc[...] = jnp.zeros_like(q_acc)
    for half in range(2):
        part = action_ref[half * 128 : (half + 1) * 128, :].astype(F32)
        turned = jnp.transpose(part).astype(BF16)
        for m in range(LOCAL):
            lhs[m, :, half * ROWS : half * ROWS + HALF] = turned

    pl.semaphore_wait(barrier, len(everyone))

    def first_send(b):
        own = wbuf.at[b, yhi, xpos, core]

        @pl.when(lax.rem(b, GROUP) == 0)
        def _():
            wait_for(wbuf.at[pl.ds(b, GROUP), yhi, xpos, core], load_sem.at[b // GROUP])

        kind_a = is_a(GATHER_KINDS, b)

        @pl.when(kind_a)
        def _():
            send(own, own, link_done, y_sem.at[b], across)

        @pl.when(jnp.logical_not(kind_a))
        def _():
            send(own, own, link_done, x_sem.at[b], right)
            send(own, own, link_done, x_sem.at[b], left)

    def second_hop(b):
        kind_a = is_a(GATHER_KINDS, b)

        @pl.when(kind_a)
        def _():
            wait_for(wbuf.at[b, oyhi, xpos, core], y_sem.at[b])
            both = wbuf.at[b, :, xpos, core]
            send(both, both, link_done, x_sem.at[b], right)
            send(both, both, link_done, x_sem.at[b], left)

        @pl.when(jnp.logical_not(kind_a))
        def _():
            wait_for(wbuf.at[b, yhi, pl.ds(0, 2), core], x_sem.at[b])
            one = wbuf.at[b, yhi, xleft, core, low]
            send(one, one, link_done, second_sem.at[b], right)
            two = wbuf.at[b, yhi, xright, core, high]
            send(two, two, link_done, second_sem.at[b], left)

    def third_hop(b):
        kind_a = is_a(GATHER_KINDS, b)

        @pl.when(kind_a)
        def _():
            wait_for(wbuf.at[b, :, pl.ds(0, 2), core], x_sem.at[b])

            @pl.when(b == BLOCKS - 1)
            def _():
                for xx in (xpos, xleft, xright):
                    early = wbuf.at[b, :, xx, core]
                    send(early, early, sib_done, sib_sem.at[b], sibling)

            one = wbuf.at[b, :, xleft, core, low]
            send(one, one, link_done, second_sem.at[b], right)
            two = wbuf.at[b, :, xright, core, high]
            send(two, two, link_done, second_sem.at[b], left)

        @pl.when(jnp.logical_not(kind_a))
        def _():
            wait_for(wbuf.at[b, yhi, xfar, core], second_sem.at[b])
            mine = wbuf.at[b, yhi, :, core]
            send(mine, mine, link_done, y_sem.at[b], across)
            send(mine, mine, sib_done, sib_sem.at[b], sibling)

    def to_sibling(b):
        kind_a = is_a(GATHER_KINDS, b)

        @pl.when(kind_a)
        def _():
            wait_for(wbuf.at[b, :, xfar, core], second_sem.at[b])

            @pl.when(b == BLOCKS - 1)
            def _():
                late = wbuf.at[b, :, xfar, core]
                send(late, late, sib_done, sib_sem.at[b], sibling)

            @pl.when(b < BLOCKS - 1)
            def _():
                full = wbuf.at[b, :, :, core]
                send(full, full, sib_done, sib_sem.at[b], sibling)

        @pl.when(jnp.logical_not(kind_a))
        def _():
            theirs = wbuf.at[b, oyhi, :, core]
            wait_for(theirs, y_sem.at[b])
            send(theirs, theirs, sib_done, sib_sem.at[b], sibling)

    def arrive(b):
        @pl.when(lax.rem(b, GROUP) == 0)
        def _():
            wait_for(state.at[pl.ds(b, GROUP)], state_sem.at[b // GROUP])

        wait_for(wbuf.at[b, :, :, ocore], sib_sem.at[b])

    def forward_product(b):
        return jnp.dot(action_ref[...], wbuf[b].reshape(ACT, WIDTH), preferred_element_type=F32)

    def forward_elementwise(b, product):
        m = b // PER_MEMBER
        vw = value_w[b]
        step = 64
        for pos in range(0, ROWS, step):
            rows = slice(pos, pos + step)
            p = state[b, rows, :].astype(F32) + product[rows, :]
            sig = 0.5 + 0.5 * jnp.tanh(0.5 * p)
            rest = 1.0 - sig
            hid = p * sig
            first = sig + hid * rest
            state[b, rows, :] = (first * vw).astype(BF16)
            slope[b, rows, :] = first.astype(BF16)
            curve[b, rows, :] = (sig * rest * (2.0 + p * (rest - sig)) * vw).astype(BF16)
            hidden[b, rows, :] = hid.astype(BF16)
            q_acc[m, rows, :] += fold(hid * vw)

    def gradient_product(b):
        grad[b // PER_MEMBER] += lax.dot_general(
            state[b], wbuf[b].reshape(ACT, WIDTH), (((1,), (1,)), ((), ())), preferred_element_type=F32
        )

    def compute_forward(t):
        @pl.when(t == 0)
        def _():
            arrive(t)
            forward_elementwise(t, forward_product(t))

        @pl.when(t > 0)
        def _():
            arrive(t)
            product = forward_product(t)
            gradient_product(t - 1)
            forward_elementwise(t, product)

        @pl.when(t == BLOCKS - 1)
        def _():
            gradient_product(t)

    def forward_round(i, done):
        counts = [count_at(digits, i) for digits in GATHER_STEPS]
        done = run_steps((first_send, second_hop, third_hop, to_sibling), counts, done)

        @pl.when(i >= GATHER_LEAD)
        def _():
            compute_forward(i - GATHER_LEAD)

        return done

    zero = jnp.int32(0)
    lax.fori_loop(0, BLOCKS + GATHER_LEAD, forward_round, (zero, zero, zero, zero))

    def make_piece(k, half):
        rows = pl.ds(pl.multiple_of(k * PIECE + half * HALF_PIECE, HALF_PIECE), HALF_PIECE)
        both = []
        squares = None
        for m in range(LOCAL):
            g = grad[m, rows, :]
            inv = 1.0 / jnp.sqrt(jnp.sum(g * g, axis=-1, keepdims=True) + EPS)
            u = g * inv
            ub = u.astype(BF16)
            grad[m, rows, :] = u
            unit_b[m, rows, :] = ub
            rnorm[m, rows, :] = jnp.broadcast_to(inv, (HALF_PIECE, 128))
            uf = ub.astype(F32)
            both.append(uf)
            sq = fold(uf * uf)
            squares = sq if squares is None else squares + sq
        square_out[rows, :] = squares
        return (both[0] + both[1]).astype(BF16)

    for half in range(2):
        rows = pl.ds(half * HALF_PIECE, HALF_PIECE)
        for peer in peers:
            piece_out[peer, rows] = make_piece(peer, half)
            send(
                piece_out.at[peer, rows], piece_in.at[member, rows],
                misc_sem.at[0], misc_sem.at[14 + half], (peer, row),
            )
        piece_in[member, rows] = make_piece(member, half)

    target_rows = jnp.transpose(jnp.broadcast_to(target_ref[...], (128, ROWS)))
    for m in range(LOCAL):
        q = jnp.sum(q_acc[m], axis=-1, keepdims=True)
        resid[m] = q - target_rows

    for half in range(2):
        rows = pl.ds(half * HALF_PIECE, HALF_PIECE)
        wait_for(piece_in.at[pl.ds(0, MEMBER_DEV - 1), rows], misc_sem.at[14 + half])
        acc = piece_in[0, rows].astype(F32)
        for k in range(1, MEMBER_DEV):
            acc = acc + piece_in[k, rows].astype(F32)
        mine = pl.ds(pl.multiple_of(member * PIECE + half * HALF_PIECE, HALF_PIECE), HALF_PIECE)
        total[mine, :] = acc.astype(BF16)
        for peer in peers:
            send(total.at[mine], total.at[mine], misc_sem.at[2], misc_sem.at[3], (peer, row))
    square_lane = jnp.sum(jnp.transpose(square_out[...]), axis=0, keepdims=True)
    square_in[member] = jnp.broadcast_to(square_lane, (8, ROWS))
    for peer in peers:
        send(square_in.at[member], square_in.at[member], misc_sem.at[4], misc_sem.at[5], (peer, row))
    wait_for(total.at[pl.ds(0, PIECE * (MEMBER_DEV - 1))], misc_sem.at[3])

    def make_cot(m):
        step = 64
        for pos in range(0, ROWS, step):
            u = grad[m, pos : pos + step, :]
            d = (2.0 * ETA / PAIRS) * (
                total[pos : pos + step, :].astype(F32) - unit_b[m, pos : pos + step, :].astype(F32)
            )
            along = jnp.sum(u * d, axis=-1, keepdims=True)
            c = (d - u * along) * wide(rnorm[m, pos : pos + step, :], ACT)
            cot[m, pos : pos + step, :] = c.astype(BF16)

    def place_cot(m):
        for half in range(2):
            part = cot[m, half * 128 : (half + 1) * 128, :].astype(F32)
            lhs[m, :, half * ROWS + HALF : (half + 1) * ROWS] = jnp.transpose(part).astype(BF16)

    make_cot(0)
    wait_for(ring_in, link_done)
    wait_for(core_in, sib_done)

    def back_product(b):
        return jnp.dot(cot[b // PER_MEMBER], wbuf[b].reshape(ACT, WIDTH), preferred_element_type=F32)

    def partial_product(b):
        m = b // PER_MEMBER
        slot = lax.rem(b, 2)
        for q in range(4):
            some = slice(q * 256, (q + 1) * 256)
            part = jnp.dot(lhs[m, some, 0:ROWS], rhs[slot, 0:ROWS, :], preferred_element_type=F32)
            part = part + jnp.dot(
                lhs[m, some, ROWS : 2 * ROWS], rhs[slot, ROWS : 2 * ROWS, :], preferred_element_type=F32
            )
            wbuf[b, q // 2, 2 * (q % 2) : 2 * (q % 2) + 2] = part.astype(BF16).reshape(2, 2, 64, WIDTH)

    def elementwise(b, back_all):
        m = b // PER_MEMBER
        slot = lax.rem(b, 2)
        vacc = jnp.zeros((1, WIDTH), F32)
        step = 64
        for pos in range(0, ROWS, step):
            rows = slice(pos, pos + step)
            at = pos + (pos // HALF) * HALF
            back = back_all[rows, :]
            res = wide(resid[m, rows, :], WIDTH)
            tangent = state[b, rows, :]
            dpre = (tangent.astype(F32) * res + curve[b, rows, :].astype(F32) * back).astype(BF16)
            vacc = vacc + jnp.sum(
                hidden[b, rows, :].astype(F32) * res + slope[b, rows, :].astype(F32) * back, axis=0, keepdims=True
            )
            rhs[slot, at : at + step, :] = dpre
            rhs[slot, at + HALF : at + HALF + step, :] = tangent
            state[b, rows, :] = dpre
        vsum[b] = vacc

    def first_send_back(b):
        send(wbuf.at[b, :, :, ocore], core_in.at[b], core_done, core_sem.at[b], sibling)

    def compute_backward(t):
        @pl.when(t == 0)
        def _():
            back_all = back_product(t)
            place_cot(0)
            elementwise(t, back_all)

        @pl.when(jnp.logical_and(t > 0, t < BLOCKS))
        def _():
            back_all = back_product(t)
            partial_product(t - 1)
            first_send_back(t - 1)
            elementwise(t, back_all)

        @pl.when(t == BLOCKS)
        def _():
            partial_product(t - 1)
            first_send_back(t - 1)

    def second_send(b):
        wait_for(core_in.at[b], core_sem.at[b])
        for yy in range(2):
            for xx in range(4):
                wbuf[b, yy, xx, core] = (
                    wbuf[b, yy, xx, core].astype(F32) + core_in[b, yy, xx].astype(F32)
                ).astype(BF16)
        kind_a = is_a(SCATTER_KINDS, b)

        @pl.when(kind_a)
        def _():
            send(wbuf.at[b, :, xfar, core, low], ring_in.at[b, pl.ds(0, 2), low], ring_done, ring_sem.at[b], right)
            send(wbuf.at[b, :, xfar, core, high], ring_in.at[b, pl.ds(0, 2), high], ring_done, ring_sem.at[b], left)

        @pl.when(jnp.logical_not(kind_a))
        def _():
            send(wbuf.at[b, oyhi, :, core], ring_in.at[b, pl.ds(0, 4)], ring_done, ring_sem.at[b], across)

    def add_in(b, yy, xx, parts):
        s = wbuf[b, yy, xx, core].astype(F32)
        for part in parts:
            s = s + ring_in[b, part].astype(F32)
        wbuf[b, yy, xx, core] = s.astype(BF16)

    def add_half(b, yy, xx, part, rows):
        wbuf[b, yy, xx, core, rows] = (
            wbuf[b, yy, xx, core, rows].astype(F32) + ring_in[b, part, rows].astype(F32)
        ).astype(BF16)

    def third_send(b):
        kind_a = is_a(SCATTER_KINDS, b)

        @pl.when(kind_a)
        def _():
            wait_for(ring_in.at[b, pl.ds(0, 2)], ring_sem.at[b])
            for yy in range(2):
                add_half(b, yy, xright, yy, low)
                add_half(b, yy, xleft, yy, high)
            send(wbuf.at[b, :, xright, core], ring_in.at[b, pl.ds(2, 2)], ring_done, mid_sem.at[b], right)
            send(wbuf.at[b, :, xleft, core], ring_in.at[b, pl.ds(4, 2)], ring_done, mid_sem.at[b], left)

        @pl.when(jnp.logical_not(kind_a))
        def _():
            wait_for(ring_in.at[b, pl.ds(0, 4)], ring_sem.at[b])
            for xx in range(4):
                add_in(b, yhi, xx, [xx])
            send(wbuf.at[b, yhi, xfar, core, low], ring_in.at[b, 4, low], ring_done, mid_sem.at[b], right)
            send(wbuf.at[b, yhi, xfar, core, high], ring_in.at[b, 4, high], ring_done, mid_sem.at[b], left)

    def last_send(b):
        kind_a = is_a(SCATTER_KINDS, b)

        @pl.when(kind_a)
        def _():
            wait_for(ring_in.at[b, pl.ds(2, 4)], mid_sem.at[b])
            for yy in range(2):
                add_in(b, yy, xpos, [2 + yy, 4 + yy])
            send(wbuf.at[b, oyhi, xpos, core], ring_in.at[b, 6], ring_done, last_sem.at[b], across)

        @pl.when(jnp.logical_not(kind_a))
        def _():
            wait_for(ring_in.at[b, 4], mid_sem.at[b])
            add_half(b, yhi, xright, 4, low)
            add_half(b, yhi, xleft, 4, high)
            send(wbuf.at[b, yhi, xright, core], ring_in.at[b, 5], ring_done, last_sem.at[b], right)
            send(wbuf.at[b, yhi, xleft, core], ring_in.at[b, 6], ring_done, last_sem.at[b], left)

    def finish(b):
        kind_a = is_a(SCATTER_KINDS, b)

        def store(parts):
            out = wbuf[b, yhi, xpos, core].astype(F32)
            for part in parts:
                out = out + ring_in[b, part].astype(F32)
            wgrad_ref[b] = out.astype(BF16)

        @pl.when(kind_a)
        def _():
            wait_for(ring_in.at[b, 6], last_sem.at[b])
            store([6])

        @pl.when(jnp.logical_not(kind_a))
        def _():
            wait_for(ring_in.at[b, pl.ds(5, 2)], last_sem.at[b])
            store([5, 6])

    rounds = len(SCATTER_STEPS[0])

    def diversity():
        wait_for(square_in.at[pl.ds(0, MEMBER_DEV - 1)], misc_sem.at[5])
        tsq = []
        for pos in range(0, ROWS, 64):
            tf = total[pos : pos + 64, :].astype(F32)
            tsq.append(fold(tf * tf))
        cross_sum = jnp.sum(jnp.transpose(jnp.concatenate(tsq, axis=0)), axis=0, keepdims=True)
        squares = square_in[0]
        for k in range(1, MEMBER_DEV):
            squares = squares + square_in[k]
        div_ref[...] = (cross_sum - squares[0:1, :]) * (1.0 / PAIRS)

    def backward_round(t, done):
        @pl.when(t == PER_MEMBER - 2)
        def _():
            make_cot(1)
            place_cot(1)

        compute_backward(t)

        @pl.when(t == BLOCKS - 2)
        def _():
            diversity()

        @pl.when(t == BLOCKS)
        def _():
            send(vsum, vin.at[0], misc_sem.at[6], misc_sem.at[7], sibling)

        @pl.when(t == BLOCKS + 4)
        def _():
            wait_for(vsum, misc_sem.at[6])
            wait_for(vin.at[0], misc_sem.at[7])
            vin[1] = vsum[...] + vin[0]
            send(vin.at[1], vin.at[2], misc_sem.at[8], misc_sem.at[9], across)

        @pl.when(t == BLOCKS + 11)
        def _():
            wait_for(vin.at[2], misc_sem.at[9])
            vin[3] = vin[1] + vin[2]
            send(vin.at[3], vin.at[4], misc_sem.at[10], misc_sem.at[11], pair_first)

        @pl.when(t == rounds - 1)
        def _():
            wait_for(vin.at[4], misc_sem.at[11])
            vin[5] = vin[3] + vin[4]
            send(vin.at[5], vin.at[6], misc_sem.at[12], misc_sem.at[13], pair_second)

        counts = [
            jnp.where(t == rounds - 1, BLOCKS - first, count_at(digits, t))
            for digits, first in zip(SCATTER_STEPS, done)
        ]
        return run_steps((second_send, third_send, last_send, finish), counts, done)

    lax.fori_loop(0, rounds, backward_round, (zero, zero, zero, zero))

    wait_for(vin.at[6], misc_sem.at[13])
    for b in range(BLOCKS):
        m, pos = b // PER_MEMBER, b % PER_MEMBER
        vgrad_ref[m : m + 1, pos * WIDTH : (pos + 1) * WIDTH] = vin[5, b] + vin[6, b]

    wait_for(piece_out.at[pl.ds(0, MEMBER_DEV - 1)], misc_sem.at[0])
    wait_for(total.at[pl.ds(0, PIECE * (MEMBER_DEV - 1))], misc_sem.at[2])
    wait_for(square_in.at[pl.ds(0, MEMBER_DEV - 1)], misc_sem.at[4])
    for pos in (8, 10, 12):
        wait_for(vin.at[0], misc_sem.at[pos])

    wait_for(core_in, core_done)
    wait_for(ring_in, ring_done)


def hand_out(wgrad, vgrad, sgrad, div, wgrad_out, vgrad_out, sgrad_out, div_out, sem):
    for b in range(BLOCKS):
        m, pos = b // PER_MEMBER, b % PER_MEMBER
        cols = pl.ds(pos * WIDTH, WIDTH)
        pltpu.make_async_copy(sgrad.at[b], sgrad_out.at[m, :, cols], sem.at[0]).start()
        pltpu.make_async_copy(wgrad.at[b], wgrad_out.at[m, :, cols], sem.at[1]).start()
    small = [
        pltpu.make_async_copy(vgrad, vgrad_out, sem.at[2]),
        pltpu.make_async_copy(div, div_out, sem.at[3]),
    ]
    for one in small:
        one.start()
    for one in small:
        one.wait()
    wait_for(wgrad, sem.at[1])
    wait_for(sgrad, sem.at[0])


def body(action, state_term, target, weight_a, value_w):
    any_spec = pl.BlockSpec(memory_space=pl.ANY)
    vmem_spec = pl.BlockSpec(memory_space=pltpu.VMEM)
    dma = pltpu.SemaphoreType.DMA
    wgrad, vgrad, sgrad, div = pl.pallas_call(
        kernel,
        out_shape=(
            pltpu.VMEM((BLOCKS, 64, WIDTH), BF16),
            pltpu.VMEM((LOCAL, HID), F32),
            pltpu.VMEM((BLOCKS, ROWS, WIDTH), BF16),
            pltpu.VMEM((1, ROWS), F32),
        ),
        in_specs=[any_spec] * 5,
        out_specs=(vmem_spec,) * 4,
        scratch_shapes=[
            pltpu.VMEM((BLOCKS, 2, 4, 2, 64, WIDTH), BF16),
            pltpu.VMEM((BLOCKS, ROWS, WIDTH), BF16),
            pltpu.VMEM((BLOCKS, ROWS, WIDTH), BF16),
            pltpu.VMEM((BLOCKS, ROWS, WIDTH), BF16),
            pltpu.VMEM((LOCAL, ROWS, ACT), F32),
            pltpu.VMEM((LOCAL, ROWS, ACT), BF16),
            pltpu.VMEM((LOCAL, ROWS, ACT), BF16),
            pltpu.VMEM((LOCAL, ACT, 2 * ROWS), BF16),
            pltpu.VMEM((2, 2 * ROWS, WIDTH), BF16),
            pltpu.VMEM((BLOCKS, 2, 4, 64, WIDTH), BF16),
            pltpu.VMEM((BLOCKS, 7, 64, WIDTH), BF16),
            pltpu.VMEM((MEMBER_DEV, PIECE, ACT), BF16),
            pltpu.VMEM((MEMBER_DEV, PIECE, ACT), BF16),
            pltpu.VMEM((ROWS, ACT), BF16),
            pltpu.VMEM((ROWS, 128), F32),
            pltpu.VMEM((MEMBER_DEV, 8, ROWS), F32),
            pltpu.VMEM((BLOCKS, 1, WIDTH), F32),
            pltpu.VMEM((LOCAL, ROWS, 128), F32),
            pltpu.VMEM((LOCAL, ROWS, 128), F32),
            pltpu.VMEM((LOCAL, ROWS, 128), F32),
            pltpu.VMEM((BLOCKS, 1, WIDTH), F32),
            pltpu.VMEM((7, BLOCKS, 1, WIDTH), F32),
        ]
        + [dma((BLOCKS // GROUP,)) for _ in range(2)]
        + [dma for _ in range(4)]
        + [dma((BLOCKS,)) for _ in range(4)]
        + [dma((16,))]
        + [pltpu.VMEM((ROWS, ACT), BF16), pltpu.VMEM((1, ROWS), F32), pltpu.VMEM((LOCAL, HID), BF16), dma((3,))],
        compiler_params=pltpu.CompilerParams(
            collective_id=1, has_side_effects=True, vmem_limit_bytes=56 * 1024 * 1024
        ),
    )(action, state_term, target.reshape(1, ROWS), weight_a, value_w)
    wgrad, vgrad, sgrad, div = pl.pallas_call(
        hand_out,
        out_shape=(
            jax.ShapeDtypeStruct((LOCAL, 64, HID), BF16),
            jax.ShapeDtypeStruct((LOCAL, HID), F32),
            jax.ShapeDtypeStruct((LOCAL, ROWS, HID), BF16),
            jax.ShapeDtypeStruct((1, ROWS), F32),
        ),
        in_specs=[any_spec] * 4,
        out_specs=(any_spec,) * 4,
        scratch_shapes=[dma((4,))],
        compiler_params=pltpu.CompilerParams(vmem_limit_bytes=1024 * 1024),
    )(wgrad, vgrad, sgrad, div)
    return (wgrad, vgrad, sgrad, div.reshape(ROWS))


def solution(mesh):
    in_specs = (
        P("row", None),
        P("member", "row", None),
        P("row"),
        P("member", "row", None),
        P("member", None),
    )
    out_specs = (P("member", "row", None), P("member", None), P("member", "row", None), P("row"))
    return jax.shard_map(body, mesh=mesh, in_specs=in_specs, out_specs=out_specs, check_vma=False)
```
